32 devices in a mesh: dp: 8 (over z, x), seq: 4 (over y, core).
Axes of the slice: x: 2, y: 2, z: 4, core: 2. Of those that a mesh axis runs over, the one named last changes fastest.
Arguments:
- tokens: bfloat16 [2, 8, 1536, 512], P(None, 'dp', 'seq'), may hold values from -6 to 6
- memory: bfloat16 [2, 8, 1024, 512], P(None, 'dp', 'seq'), may hold values from -6 to 6
- cotangent: bfloat16 [2, 8, 1536, 512], P(None, 'dp', 'seq'), may hold values from -6 to 6
- tgt_segments: int32 [2, 8, 1536], P(None, 'dp', 'seq'), may hold values from 0 to 7, never falling along the last dimension, each value on 1 to 768 neighbouring positions
- src_segments: int32 [2, 8, 1024], P(None, 'dp', 'seq'), may hold values from 0 to 7, never falling along the last dimension, each value on 1 to 512 neighbouring positions
- self_qkv: bfloat16 [512, 1536], P('dp'), may hold values from -0.375 to 0.375
- self_out: bfloat16 [512, 512], P('dp'), may hold values from -0.75 to 0.75
- cross_q: bfloat16 [512, 512], P('dp'), may hold values from -0.375 to 0.375
- cross_kv: bfloat16 [512, 1024], P('dp'), may hold values from -0.375 to 0.375
- cross_out: bfloat16 [512, 512], P('dp'), may hold values from -0.75 to 0.75
- ffn_up: bfloat16 [512, 2048], P('dp'), may hold values from -0.25 to 0.25
- ffn_down: bfloat16 [2048, 512], P('dp'), may hold values from -0.1875 to 0.1875
- proj_bias: bfloat16 [7, 512], P(None, 'dp'), may hold values from -1.796875 to 1.796875
- up_bias: bfloat16 [2048], P('dp'), may hold values from -1.796875 to 1.796875
- norm_gain: bfloat16 [3, 512], P(None, 'dp'), may hold values from 0.5 to 1.5
- norm_bias: bfloat16 [3, 512], P(None, 'dp'), may hold values from -1.796875 to 1.796875
Outputs:
- layer_out: bfloat16 [2, 8, 1536, 512], P(None, 'dp', 'seq')
- d_tokens: bfloat16 [2, 8, 1536, 512], P(None, 'dp', 'seq')
- d_memory: bfloat16 [2, 8, 1024, 512], P(None, 'dp', 'seq')
- grad_self_qkv: float32 [512, 1536], P('dp')
- grad_self_out: float32 [512, 512], P('dp')
- grad_cross_q: float32 [512, 512], P('dp')
- grad_cross_kv: float32 [512, 1024], P('dp')
- grad_cross_out: float32 [512, 512], P('dp')
- grad_ffn_up: float32 [512, 2048], P('dp')
- grad_ffn_down: float32 [2048, 512], P('dp')
- grad_proj_bias: float32 [7, 512], P(None, 'dp')
- grad_up_bias: float32 [2048], P('dp')
- grad_norm_gain: float32 [3, 512], P(None, 'dp')
- grad_norm_bias: float32 [3, 512], P(None, 'dp')
The draws below stay inside these ranges and needn't reach their ends.
Inputs may be any that keep to these rules, and one draw needn't show every extreme that they name: `tgt_segments`: along a sequence the ids never fall; each of the 8 documents holds 1 to 768 target positions; target document k attends source document k. `src_segments`: along a sequence the ids never fall; each of the 8 documents holds 1 to 512 source positions.
All inputs are finite; a program needn't handle non-finite values.
Results may differ from the reference program's by a relative error of at most 0.024.
The reference program's roundings to bfloat16 on the way count: a program that leaves them out, or rounds other values in their place, can miss the bound.
Values may be sent and summed in bfloat16 or wider, within the bound.
A program may use at most 192 MiB of HBM per device.

```python
import math
import jax
import jax.numpy as jnp
import numpy as np
from jax import lax

D = 512
H = 8
HD = 64
FF = 2048
MB = 2
DOCS = 8
TGT_LEN = 1536
SRC_LEN = 1024
N_DP = 8


def block_levels(stream_key, dims, cuts, least, top_value):
    loudness, own = 1.0, jax.random.fold_in(stream_key, 6)
    for position, parts in cuts:
        heights = jnp.exp(jax.random.uniform(jax.random.fold_in(own, position), (parts,), jnp.float32, least / len(cuts), top_value / len(cuts)))
        loudness = loudness * jnp.repeat(heights, dims[position] // parts).reshape([-1 if axis == position else 1 for axis in range(len(dims))])
    return loudness


def split_up(count, total, bound, slope):
    weights = [(1 << 20) // math.isqrt(grade ** slope) + 1 for grade in range(2, count + 1)]
    surplus, given = total - bound - (count - 1), [1] * (count - 1)
    while surplus > 0:
        candidates = [i for i in range(count - 1) if given[i] < bound]
        pool, left = sum([weights[i] for i in candidates]), surplus
        for i in candidates:
            addition = min(bound - given[i], max(1, left * weights[i] // pool), surplus)
            given[i] = given[i] + addition
            surplus = surplus - addition
    return np.array([bound] + given)


def uneven(rng, number_of, total, most, lean):
    if number_of == 2:
        one = jax.random.randint(rng, (), max(1, total - most), min(most, total - 1) + 1)
        return jnp.stack([one, total - one])
    sizes = jnp.asarray(split_up(number_of, total, most, lean), jnp.int32)
    couples = (number_of - 1) // 2
    source_of, taker = sizes[1:1 + 2 * couples:2], sizes[2:2 + 2 * couples:2]
    room = jnp.minimum(source_of - 1, most - taker)
    passed = jax.random.randint(jax.random.fold_in(rng, 1), (couples,), 0, 1 << 20) % (room + 1)
    sizes = sizes.at[1:1 + 2 * couples:2].set(source_of - passed).at[2:2 + 2 * couples:2].set(taker + passed)
    return sizes[jax.random.permutation(jax.random.fold_in(rng, 2), number_of)]


def scatter_about(own_key, dims, spread, bound, cuts=(), dtype=jnp.bfloat16):
    factor_of = block_levels(own_key, dims, cuts, -0.22, 0.18) if cuts else 1.0
    array = jax.random.normal(own_key, dims, jnp.float32) * spread * factor_of
    return jnp.minimum(jnp.maximum(array, -bound), bound).astype(dtype)


def setup_inputs(seed: int = 0) -> dict:
    splits = jax.random.split(jax.random.key(seed), 17)
    return {
        "tokens": scatter_about(splits[0], (MB, N_DP, TGT_LEN, D), 1.0, 6.0, ((1, 8), (2, 4))),
        "memory": scatter_about(splits[1], (MB, N_DP, SRC_LEN, D), 1.0, 6.0, ((1, 8), (2, 4))),
        "cotangent": scatter_about(splits[2], (MB, N_DP, TGT_LEN, D), 1.0, 6.0, ((1, 8), (2, 4))),
        "tgt_segments": jax.vmap(lambda own: jnp.searchsorted(jnp.cumsum(uneven(own, DOCS, TGT_LEN, TGT_LEN // 2, 2)), jnp.arange(TGT_LEN), side="right"))(jax.random.split(splits[3], MB * N_DP)).reshape((MB, N_DP, TGT_LEN)).astype(jnp.int32),
        "src_segments": jax.vmap(lambda own: jnp.searchsorted(jnp.cumsum(uneven(own, DOCS, SRC_LEN, SRC_LEN // 2, 2)), jnp.arange(SRC_LEN), side="right"))(jax.random.split(splits[4], MB * N_DP)).reshape((MB, N_DP, SRC_LEN)).astype(jnp.int32),
        "self_qkv": scatter_about(splits[5], (D, 3 * D), (D // 2) ** -0.5, 0.375, ((0, 8),)),
        "self_out": scatter_about(splits[6], (D, D), (D // 8) ** -0.5, 0.75, ((0, 8),)),
        "cross_q": scatter_about(splits[7], (D, D), (D // 2) ** -0.5, 0.375, ((0, 8),)),
        "cross_kv": scatter_about(splits[8], (D, 2 * D), (D // 2) ** -0.5, 0.375, ((0, 8),)),
        "cross_out": scatter_about(splits[9], (D, D), (D // 8) ** -0.5, 0.75, ((0, 8),)),
        "ffn_up": scatter_about(splits[10], (D, FF), D ** -0.5, 0.25, ((0, 8),)),
        "ffn_down": scatter_about(splits[11], (FF, D), (FF // 2) ** -0.5, 0.1875, ((0, 8),)),
        "proj_bias": scatter_about(splits[12], (7, D), 0.3, 1.796875, ((1, 8),)),
        "up_bias": scatter_about(splits[13], (FF,), 0.3, 1.796875, ((0, 8),)),
        "norm_gain": jnp.clip(1.0 + 0.1 * jax.random.normal(splits[14], (3, D), jnp.float32), 0.5, 1.5).astype(jnp.bfloat16),
        "norm_bias": scatter_about(splits[15], (3, D), 0.3, 1.796875, ((1, 8),)),
    }


@jax.custom_vjp
def low(v):
    return lax.optimization_barrier(v.astype(jnp.bfloat16)).astype(jnp.float32)

@jax.custom_vjp
def low_back(v):
    return v

def low_keep(v):
    return (low(v), None)

def low_pass(kept, grad):
    return (grad,)

def back_keep(v):
    return (v, None)

def back_low(kept, grad):
    return (low(grad),)
low.defvjp(low_keep, low_pass)
low_back.defvjp(back_keep, back_low)

def both_ways(tensor):
    return low(low_back(tensor))

def matmul(left, right):
    return jnp.dot(left, right, precision=lax.Precision.HIGHEST, preferred_element_type=jnp.float32)

def gelu_exact(values):
    return values * 0.5 * (1.0 + lax.erf(values * 0.7071067811865476))

def layer_norm(summed, gain, shift):
    center = summed - lax.optimization_barrier(jnp.mean(summed, axis=-1, keepdims=True))
    variance = lax.optimization_barrier(jnp.mean(center * center, axis=-1, keepdims=True))
    return center * lax.rsqrt(variance + 1e-05) * gain + shift

def attend(query_rows, key_rows, value_rows, query_ids, key_ids):
    row_count = query_rows.shape[0]
    block_rows = min(512, row_count)
    key_heads = key_rows.reshape(key_rows.shape[0], H, HD)
    value_heads = value_rows.reshape(value_rows.shape[0], H, HD)

    def one_block(pieces):
        query_block, block_ids = pieces
        scores = jnp.einsum('qhd,khd->hqk', query_block.reshape(block_rows, H, HD), key_heads, precision=lax.Precision.HIGHEST)
        scores = low_back(scores)
        visible = (block_ids[:, None] == key_ids[None, :])[None]
        scores = jnp.where(visible, scores, -1e+30)
        highest = lax.optimization_barrier(jnp.max(scores, axis=-1, keepdims=True))
        weights = jnp.exp(scores - highest)
        probs = weights / lax.optimization_barrier(jnp.sum(weights, axis=-1, keepdims=True))
        mixed_block = jnp.einsum('hqk,khd->qhd', low(probs), value_heads, precision=lax.Precision.HIGHEST)
        return mixed_block.reshape(block_rows, H * HD)
    block_count = row_count // block_rows
    blocks = lax.map(jax.checkpoint(one_block), (query_rows.reshape(block_count, block_rows, H * HD), query_ids.reshape(block_count, block_rows)))
    return blocks.reshape(row_count, H * HD)

def layer(input_rows, source_rows, weights, tgt_ids, src_ids):
    self_qkv, self_out, cross_q, cross_kv, cross_out, ffn_up, ffn_down, proj_bias, up_bias, norm_gain, norm_bias = weights
    packed = matmul(input_rows, self_qkv)
    query_rows = both_ways((packed[:, :D] + proj_bias[0]) * 0.125)
    key_rows = both_ways(packed[:, D:2 * D])
    value_rows = both_ways(packed[:, 2 * D:] + proj_bias[1])
    self_mixed = both_ways(attend(query_rows, key_rows, value_rows, tgt_ids, tgt_ids))
    self_branch = low_back(matmul(self_mixed, self_out) + proj_bias[2])
    first_norm = layer_norm(input_rows + self_branch, norm_gain[0], norm_bias[0])
    cross_query = both_ways((matmul(low(first_norm), cross_q) + proj_bias[3]) * 0.125)
    pair_rows = matmul(source_rows, cross_kv)
    cross_key = both_ways(pair_rows[:, :D])
    cross_value = both_ways(pair_rows[:, D:] + proj_bias[4])
    cross_mixed = both_ways(attend(cross_query, cross_key, cross_value, tgt_ids, src_ids))
    cross_branch = low_back(matmul(cross_mixed, cross_out) + proj_bias[5])
    second = layer_norm(first_norm + cross_branch, norm_gain[1], norm_bias[1])
    hidden = low_back(matmul(low(second), ffn_up) + up_bias)
    active = low(gelu_exact(hidden))
    ffn_branch = low_back(matmul(active, ffn_down) + proj_bias[6])
    return layer_norm(second + ffn_branch, norm_gain[2], norm_bias[2])

def reference(tokens, memory, cotangent, tgt_segments, src_segments, self_qkv, self_out, cross_q, cross_kv, cross_out, ffn_up, ffn_down, proj_bias, up_bias, norm_gain, norm_bias):
    params = tuple((weight.astype(jnp.float32) for weight in (self_qkv, self_out, cross_q, cross_kv, cross_out, ffn_up, ffn_down, proj_bias, up_bias, norm_gain, norm_bias)))
    seq_count = MB * N_DP
    stacked = (tokens.reshape(seq_count, TGT_LEN, D), memory.reshape(seq_count, SRC_LEN, D), cotangent.reshape(seq_count, TGT_LEN, D), tgt_segments.reshape(seq_count, TGT_LEN), src_segments.reshape(seq_count, SRC_LEN))
    zero_grads = tuple((jnp.zeros(weight.shape, jnp.float32) for weight in params))

    def one_sequence(totals, pieces):
        inputs, memory_rows, grad_rows, tgt_ids, src_ids = pieces

        def forward(input_rows, source_rows, weights):
            return layer(input_rows, source_rows, weights, tgt_ids, src_ids)
        output, pullback = jax.vjp(forward, inputs.astype(jnp.float32), memory_rows.astype(jnp.float32), params)
        input_grad, memory_grad, weight_grads = pullback(grad_rows.astype(jnp.float32))
        totals = tuple((total_sum + grad_part for total_sum, grad_part in zip(totals, weight_grads)))
        return (totals, (output.astype(jnp.bfloat16), input_grad.astype(jnp.bfloat16), memory_grad.astype(jnp.bfloat16)))
    totals, (outputs, input_grads, memory_grads) = lax.scan(one_sequence, zero_grads, stacked)
    factor = 1.0 / math.sqrt(MB * N_DP * TGT_LEN)
    totals = tuple((total_sum * factor for total_sum in totals))
    return (outputs.reshape(MB, N_DP, TGT_LEN, D), input_grads.reshape(MB, N_DP, TGT_LEN, D), memory_grads.reshape(MB, N_DP, SRC_LEN, D), totals[0], totals[1], totals[2], totals[3], totals[4], totals[5], totals[6], totals[7], totals[8], totals[9], totals[10])
```

```python
import functools
import math

import jax
import jax.numpy as jnp
from jax import lax
from jax.experimental import pallas as pl
from jax.experimental.pallas import tpu as pltpu
from jax.sharding import PartitionSpec as P

H = 8
MB = 2
RB = 256
KB = 256
F32 = jnp.float32
BF16 = jnp.bfloat16


def mm(left, right):
    return jnp.dot(left, right, preferred_element_type=F32)


def mm_nt(left, right):
    return lax.dot_general(left, right, (((1,), (1,)), ((), ())), preferred_element_type=F32)


def mm_tn(left, right):
    return lax.dot_general(left, right, (((0,), (0,)), ((), ())), preferred_element_type=F32)


def gelu_parts(values):
    cumulative = 0.5 * (1.0 + lax.erf(values * 0.7071067811865476))
    density = jnp.exp(-0.5 * values * values) * 0.3989422804014327
    return values * cumulative, cumulative + values * density


def normalize(summed, gain, shift):
    center = summed - jnp.mean(summed, axis=-1, keepdims=True)
    scale_inv = lax.rsqrt(jnp.mean(center * center, axis=-1, keepdims=True) + 1e-05)
    unit_rows = center * scale_inv
    return unit_rows * gain + shift, unit_rows, scale_inv


def normalize_back(unit_rows, scale_inv, gain, grad_rows):
    scaled = grad_rows * gain
    return scale_inv * (
        scaled
        - jnp.mean(scaled, axis=-1, keepdims=True)
        - unit_rows * jnp.mean(scaled * unit_rows, axis=-1, keepdims=True)
    )


def fold(values, op):
    rows, cols = values.shape
    return op(values.reshape(rows // 8, 8, cols), axis=0)


def layer_kernel(
    bounds,
    x_hbm, m_hbm, ct_ref, vec_ref,
    wqkv_hbm, wout_hbm, wcq_hbm, wckv_hbm, wcout_hbm, wup_hbm, wdown_hbm,
    layer_out, mixed_out, self_low_out, first_low_out, cdq_out, cmixed_out, cross_low_out,
    second_low_out, up_low_out, active_out, down_low_out, dq_out, part_out,
    dkv_hbm, dckv_hbm, vecg_out,
    wqkv, wout, wcq, wckv, wcout, wup, wdown,
    xs, ms, k_s, kt_s, v_s, vt_s, k_c, kt_c, v_c, vt_c,
    p_s, p_c, dk_s, dv_s, dk_c, dv_c,
    qm_s, qm_c, gtm, gm, ot_s, ot_c, dqt, slope_s, sems,
):
    step = pl.program_id(0)
    steps = pl.num_programs(0)
    d_model = xs.shape[1]
    t_len = xs.shape[0]
    s_len = ms.shape[0]
    ff = wup.shape[1]
    hd = d_model // H
    core = bounds[0]
    block = 2 * step + core

    loads = [
        pltpu.make_async_copy(src, dst, sems.at[n])
        for n, (src, dst) in enumerate((
            (x_hbm, xs), (wqkv_hbm, wqkv), (m_hbm, ms), (wckv_hbm, wckv), (wout_hbm, wout), (wcq_hbm, wcq),
            (wcout_hbm, wcout), (wup_hbm, wup), (wdown_hbm, wdown),
        ))
    ]
    vec = vec_ref[...]

    @pl.when(step == 0)
    def _():
        for load in loads:
            load.start()
        dk_s[...] = jnp.zeros_like(dk_s)
        dv_s[...] = jnp.zeros_like(dv_s)
        dk_c[...] = jnp.zeros_like(dk_c)
        dv_c[...] = jnp.zeros_like(dv_c)
        vecg_out[...] = jnp.zeros_like(vecg_out)
        vec_t = vec.T

        def project(rows_ref, w_ref, k_at, kt, k, vt, v, bias_row, bias_row_t, count):
            wk = w_ref[:, k_at:k_at + d_model]
            wv = w_ref[:, k_at + d_model:k_at + 2 * d_model]
            wk_t = wk.T
            wv_t = wv.T

            def one(r, carry):
                at = pl.ds(pl.multiple_of(r * RB, RB), RB)
                rows = rows_ref[at, :]
                k[at, :] = mm(rows, wk).astype(BF16)
                v[at, :] = (mm(rows, wv) + bias_row).astype(BF16)
                kt[:, at] = mm_nt(wk_t, rows).astype(BF16)
                vt[:, at] = (mm_nt(wv_t, rows) + bias_row_t).astype(BF16)
                return carry

            lax.fori_loop(0, count // RB, one, 0)

        loads[0].wait()
        loads[1].wait()
        project(xs, wqkv, d_model, kt_s, k_s, vt_s, v_s, vec[1:2], vec_t[:, 1:2], t_len)
        loads[2].wait()
        loads[3].wait()
        project(ms, wckv, 0, kt_c, k_c, vt_c, v_c, vec[4:5], vec_t[:, 4:5], s_len)
        for load in loads[4:]:
            load.wait()

    qpos = block * RB + lax.broadcasted_iota(jnp.int32, (1, RB), 1)
    lo_s = jnp.zeros((1, RB), jnp.int32)
    hi_s = jnp.full((1, RB), bounds[2], jnp.int32)
    lo_c = jnp.zeros((1, RB), jnp.int32)
    hi_c = jnp.full((1, RB), bounds[2 + 8], jnp.int32)
    for doc in range(1, 8):
        inside = qpos >= bounds[1 + doc]
        lo_s = jnp.where(inside, bounds[1 + doc], lo_s)
        hi_s = jnp.where(inside, bounds[2 + doc], hi_s)
        lo_c = jnp.where(inside, bounds[9 + doc], lo_c)
        hi_c = jnp.where(inside, bounds[10 + doc], hi_c)
    first = block * RB
    last = first + RB - 1
    s_from, s_to, c_from, c_to = 0, bounds[2], 0, bounds[10]
    for doc in range(1, 8):
        in_first = first >= bounds[1 + doc]
        in_last = last >= bounds[1 + doc]
        s_from = jnp.where(in_first, bounds[1 + doc], s_from)
        c_from = jnp.where(in_first, bounds[9 + doc], c_from)
        s_to = jnp.where(in_last, bounds[2 + doc], s_to)
        c_to = jnp.where(in_last, bounds[10 + doc], c_to)

    def block_range(start, stop):
        return lax.div(start, KB), lax.div(stop + (KB - 1), KB)

    def halves(values, axis, h):
        place = lax.broadcasted_iota(jnp.int32, values.shape, axis)
        return jnp.where(place >= hd if h % 2 else place < hd, values, jnp.zeros_like(values))

    def put_masked(rows, rows_t, natural, transposed):
        for h in range(H):
            pair = slice((h // 2) * 2 * hd, (h // 2) * 2 * hd + 2 * hd)
            natural[h] = halves(rows[:, pair], 1, h)
            transposed[h] = halves(rows_t[pair, :], 0, h)

    def attend(qtm, k, vt, p, ot, lo, hi, start, stop):
        j_from, j_to = block_range(start, stop)

        def bias_of(j):
            kpos = j * KB + lax.broadcasted_iota(jnp.int32, (KB, RB), 0)
            return jnp.where((kpos >= lo) & (kpos < hi), 0.0, -1e30).astype(F32)

        def scores(h, at, bias):
            pair = slice((h // 2) * 2 * hd, (h // 2) * 2 * hd + 2 * hd)
            return mm(k[at, pair], qtm[h]) + bias

        def top(j, highest):
            at = pl.ds(pl.multiple_of(j * KB, KB), KB)
            bias = bias_of(j)
            return tuple(jnp.maximum(highest[h], fold(scores(h, at, bias), jnp.max)) for h in range(H))

        highest = lax.fori_loop(j_from, j_to, top, tuple(jnp.full((8, RB), -1e30, F32) for _ in range(H)))
        highest = [jnp.max(part, axis=0, keepdims=True) for part in highest]
        ot[...] = jnp.zeros_like(ot)

        def gather(j, totals):
            at = pl.ds(pl.multiple_of(j * KB, KB), KB)
            bias = bias_of(j)
            out = []
            for h in range(H):
                weights = jnp.exp(scores(h, at, bias) - highest[h])
                low = weights.astype(BF16)
                p[h, at, :] = low
                out.append(totals[h] + fold(weights, jnp.sum))
                head = slice(h * hd, (h + 1) * hd)
                ot[head, :] += mm(vt[head, at], low)
            return tuple(out)

        totals = lax.fori_loop(j_from, j_to, gather, tuple(jnp.zeros((8, RB), F32) for _ in range(H)))
        inverse = []
        for h in range(H):
            inv = 1.0 / jnp.sum(totals[h], axis=0, keepdims=True)
            head = slice(h * hd, (h + 1) * hd)
            ot[head, :] = ot[head, :] * inv
            inverse.append(inv)
        return inverse

    def attend_back(grad_rows, inverse, qm, k, kt, v, p, ot, dk, dv, start, stop):
        j_from, j_to = block_range(start, stop)
        grad_t = grad_rows.T.astype(F32)
        scaled_t = []
        spread = []
        for h in range(H):
            head = slice(h * hd, (h + 1) * hd)
            low_t = (grad_t[head] * inverse[h]).astype(BF16)
            scaled_t.append(low_t)
            spread.append(jnp.sum(ot[head, :] * low_t.astype(F32), axis=0, keepdims=True))
        scaled_t = jnp.concatenate(scaled_t, axis=0)
        put_masked(scaled_t.T, scaled_t, gm, gtm)
        dqt[...] = jnp.zeros_like(dqt)

        def body(j, carry):
            at = pl.ds(pl.multiple_of(j * KB, KB), KB)
            for pair_index in range(H // 2):
                pair = slice(pair_index * 2 * hd, (pair_index + 1) * 2 * hd)
                dk_part = None
                dv_part = None
                for h in (2 * pair_index, 2 * pair_index + 1):
                    low = p[h, at, :]
                    prob_grad = mm(v[at, pair], gtm[h])
                    score_low = (low.astype(F32) * (prob_grad - spread[h])).astype(BF16)
                    dv_h = mm(low, gm[h])
                    dk_h = mm(score_low, qm[h])
                    dv_part = dv_h if dv_part is None else dv_part + dv_h
                    dk_part = dk_h if dk_part is None else dk_part + dk_h
                    head = slice(h * hd, (h + 1) * hd)
                    dqt[head, :] += mm(kt[head, at], score_low)
                dk[at, pair] += dk_part
                dv[at, pair] += dv_part
            return carry

        lax.fori_loop(j_from, j_to, body, 0)
        return dqt[...].astype(BF16).T

    def add_vec(row, values):
        vecg_out[row:row + 1, :] += jnp.sum(values, axis=0, keepdims=True)

    x_rows = xs[pl.ds(pl.multiple_of(first, RB), RB), :]
    q = ((mm(x_rows, wqkv[:, :d_model]) + vec[0:1]) * 0.125).astype(BF16)
    put_masked(q, q.T, qm_s, gtm)
    inv_s = attend(gtm, k_s, vt_s, p_s, ot_s, lo_s, hi_s, s_from, s_to)
    mixed = ot_s[...].astype(BF16).T
    mixed_out[...] = mixed
    first_norm, unit1, scale1 = normalize(
        x_rows.astype(F32) + (mm(mixed, wout[...]) + vec[2:3]), vec[11:12], vec[14:15])
    first_low = first_norm.astype(BF16)
    first_low_out[...] = first_low
    cq = ((mm(first_low, wcq[...]) + vec[3:4]) * 0.125).astype(BF16)
    put_masked(cq, cq.T, qm_c, gtm)
    inv_c = attend(gtm, k_c, vt_c, p_c, ot_c, lo_c, hi_c, c_from, c_to)
    cmixed = ot_c[...].astype(BF16).T
    cmixed_out[...] = cmixed
    second, unit2, scale2 = normalize(
        first_norm + (mm(cmixed, wcout[...]) + vec[5:6]), vec[12:13], vec[15:16])
    second_low = second.astype(BF16)
    second_low_out[...] = second_low
    tile = d_model
    ffn = None
    for t in range(ff // tile):
        cols = slice(t * tile, (t + 1) * tile)
        hidden = mm(second_low, wup[:, cols]) + vec[7 + t:8 + t]
        smooth, slope = gelu_parts(hidden)
        active = smooth.astype(BF16)
        active_out[:, cols] = active
        slope_s[:, cols] = slope
        part = mm(active, wdown[cols, :])
        ffn = part if ffn is None else ffn + part
    third, unit3, scale3 = normalize(second + (ffn + vec[6:7]), vec[13:14], vec[16:17])
    layer_out[...] = third.astype(BF16)

    grad = ct_ref[...].astype(F32)
    add_vec(13, grad * unit3)
    add_vec(16, grad)
    grad_third = normalize_back(unit3, scale3, vec[13:14], grad)
    down_low = grad_third.astype(BF16)
    down_low_out[...] = down_low
    add_vec(6, down_low.astype(F32))
    back = grad_third
    for t in range(ff // tile):
        cols = slice(t * tile, (t + 1) * tile)
        up_low = (mm_nt(down_low, wdown[cols, :]) * slope_s[:, cols]).astype(BF16)
        up_low_out[:, cols] = up_low
        add_vec(7 + t, up_low.astype(F32))
        back = back + mm_nt(up_low, wup[:, cols])
    add_vec(12, back * unit2)
    add_vec(15, back)
    grad_mid = normalize_back(unit2, scale2, vec[12:13], back)
    cross_low = grad_mid.astype(BF16)
    cross_low_out[...] = cross_low
    add_vec(5, cross_low.astype(F32))
    cross_grad = mm_nt(cross_low, wcout[...]).astype(BF16)
    cdq = attend_back(cross_grad, inv_c, qm_c, k_c, kt_c, v_c, p_c, ot_c, dk_c, dv_c, c_from, c_to) * 0.125
    cdq_out[...] = cdq
    add_vec(3, cdq.astype(F32))
    grad_first = grad_mid + mm_nt(cdq, wcq[...])
    add_vec(11, grad_first * unit1)
    add_vec(14, grad_first)
    grad_in = normalize_back(unit1, scale1, vec[11:12], grad_first)
    self_low = grad_in.astype(BF16)
    self_low_out[...] = self_low
    add_vec(2, self_low.astype(F32))
    self_grad = mm_nt(self_low, wout[...]).astype(BF16)
    dq = attend_back(self_grad, inv_s, qm_s, k_s, kt_s, v_s, p_s, ot_s, dk_s, dv_s, s_from, s_to) * 0.125
    dq_out[...] = dq
    add_vec(0, dq.astype(F32))
    part_out[...] = grad_in + mm_nt(dq, wqkv[:, :d_model])

    @pl.when(step == steps - 1)
    def _():
        add_vec(1, dv_s[...])
        add_vec(4, dv_c[...])
        for n in range(2):
            cols = slice(n * 256, (n + 1) * 256)
            p_s[n] = dk_s[:, cols].astype(BF16)
            p_s[2 + n] = dv_s[:, cols].astype(BF16)
            p_c[n] = dk_c[:, cols].astype(BF16)
            p_c[2 + n] = dv_c[:, cols].astype(BF16)
        stores = [
            pltpu.make_async_copy(p_s.at[0:4], dkv_hbm, sems.at[0]),
            pltpu.make_async_copy(p_c.at[0:4], dckv_hbm, sems.at[1]),
        ]
        for store in stores:
            store.start()
        for store in stores:
            store.wait()


def run_layer(bounds, x_full, m_full, ct_full, vec, weights):
    t_len, d_model = x_full.shape
    s_len = m_full.shape[0]
    ff = weights[5].shape[1]
    steps = t_len // (2 * RB)
    own = t_len // 2
    any_spec = pl.BlockSpec(memory_space=pl.ANY)

    def rows(cols):
        return pl.BlockSpec((RB, cols), lambda i, b: (i, 0))

    def arr(cols, dtype=BF16):
        return jax.ShapeDtypeStruct((own, cols), dtype)

    out_shape = [arr(d_model) for _ in range(8)] + [arr(ff), arr(ff), arr(d_model), arr(d_model), arr(d_model, F32)]
    out_specs = [rows(s.shape[1]) for s in out_shape]
    out_shape += [
        jax.ShapeDtypeStruct((4, t_len, 256), BF16),
        jax.ShapeDtypeStruct((4, s_len, 256), BF16),
        jax.ShapeDtypeStruct((32, d_model), F32),
    ]
    out_specs += [any_spec, any_spec, pl.BlockSpec((32, d_model), lambda i, b: (0, 0))]
    bf = lambda *shape: pltpu.VMEM(shape, BF16)
    fl = lambda *shape: pltpu.VMEM(shape, F32)
    scratch = [bf(*w.shape) for w in weights] + [
        bf(t_len, d_model), bf(s_len, d_model),
        bf(t_len, d_model), bf(d_model, t_len), bf(t_len, d_model), bf(d_model, t_len),
        bf(s_len, d_model), bf(d_model, s_len), bf(s_len, d_model), bf(d_model, s_len),
        bf(H, t_len, RB), bf(H, s_len, RB),
        fl(t_len, d_model), fl(t_len, d_model), fl(s_len, d_model), fl(s_len, d_model),
        bf(H, RB, 128), bf(H, RB, 128), bf(H, 128, RB), bf(H, RB, 128),
        fl(d_model, RB), fl(d_model, RB), fl(d_model, RB), fl(RB, ff),
        pltpu.SemaphoreType.DMA((9,)),
    ]
    return pl.pallas_call(
        layer_kernel,
        out_shape=out_shape,
        grid_spec=pltpu.PrefetchScalarGridSpec(
            num_scalar_prefetch=1,
            grid=(steps,),
            in_specs=[any_spec, any_spec, pl.BlockSpec((RB, d_model), lambda i, b: (2 * i + b[0], 0)),
                      pl.BlockSpec((32, d_model), lambda i, b: (0, 0))] + [any_spec] * 7,
            out_specs=out_specs,
            scratch_shapes=scratch,
        ),
        compiler_params=pltpu.CompilerParams(vmem_limit_bytes=64 * 1024 * 1024 - 512 * 1024),
        name="layer",
    )(bounds, x_full, m_full, ct_full, vec, *weights)


def pack_vectors(proj_bias, up_bias, norm_gain, norm_bias, d_model):
    size, at = lax.axis_size("dp"), lax.axis_index("dp")
    width = d_model // size
    rows = jnp.concatenate([proj_bias, jnp.zeros((4, width), BF16), norm_gain, norm_bias], axis=0)
    packed = lax.dynamic_update_slice(jnp.zeros((32, d_model), BF16), rows, (0, at * width))
    flat = lax.dynamic_update_slice(jnp.zeros((4 * d_model,), BF16), up_bias, (at * up_bias.shape[0],))
    return lax.dynamic_update_slice(packed, flat.reshape(4, d_model), (7, 0))


def unpack_vectors(sums, d_model):
    size, at = lax.axis_size("dp"), lax.axis_index("dp")
    width = d_model // size
    own = lax.dynamic_slice(sums, (0, at * width), (32, width))
    up = lax.dynamic_slice(sums[7:11].reshape(-1), (at * 4 * width,), (4 * width,))
    return own[:7], up, own[11:14], own[14:17]


def gather_plain(tokens, memory, cotangent, counts, packed, shards):
    micro = lax.axis_index("seq") // MB

    def whole(rows):
        return lax.all_gather(lax.squeeze(rows, (1,)), "seq", axis=1, tiled=True)[micro]

    weights = [lax.all_gather(shard, "dp", axis=0, tiled=True) for shard in shards]
    vec = lax.psum(packed, "dp").astype(F32)
    bounds = lax.psum(counts, "seq")[micro]
    return whole(tokens), whole(memory), whole(cotangent), bounds, vec, weights


def own_rows(rows, core):
    blocks = rows.reshape(rows.shape[0] // (2 * RB), 2, RB, rows.shape[1])
    return blocks[:, core].reshape(rows.shape[0] // 2, rows.shape[1])


def spread_rows(rows, core):
    blocks = rows.reshape(rows.shape[0] // RB, 1, RB, rows.shape[1])
    blocks = jnp.concatenate([blocks, jnp.zeros_like(blocks)], axis=1)
    blocks = jnp.where(core == 0, blocks, blocks[:, ::-1])
    return blocks.reshape(rows.shape[0] * 2, rows.shape[1])


def settle_plain(x_full, m_full, weights, results, factor):
    (layer_rows, mixed, self_low, first_low, cdq, cmixed, cross_low, second_low, up_low, active, down_low, dq,
     part, dkv, dckv, vec_sums) = results
    place = lax.axis_index("seq")
    micro, core = place // MB, place % MB
    d_model = x_full.shape[1]
    dkv = jnp.moveaxis(dkv, 0, 1).reshape(x_full.shape[0], 2 * d_model)
    dckv = jnp.moveaxis(dckv, 0, 1).reshape(m_full.shape[0], 2 * d_model)
    input_rows = spread_rows(part, core) + mm_nt(dkv, weights[0][:, d_model:])
    memory_rows = mm_nt(dckv, weights[3])

    def home(rows):
        both = jnp.stack([rows, jnp.zeros_like(rows)])
        both = jnp.where(micro == 0, both, both[::-1])
        return lax.psum_scatter(both, "seq", scatter_dimension=1, tiled=True).astype(BF16)[:, None]

    grads = [
        jnp.concatenate([mm_tn(own_rows(x_full, core), dq), mm_tn(x_full, dkv)], axis=1),
        mm_tn(mixed, self_low), mm_tn(first_low, cdq), mm_tn(m_full, dckv), mm_tn(cmixed, cross_low),
        mm_tn(second_low, up_low), mm_tn(active, down_low),
    ]
    grads = [
        lax.psum(lax.psum_scatter(grad, "dp", scatter_dimension=0, tiled=True), "seq") * factor for grad in grads
    ]
    vec_sums = lax.psum(vec_sums, ("dp", "seq")) * factor
    return (home(spread_rows(layer_rows.astype(F32), core)), home(input_rows), home(memory_rows), *grads,
            *unpack_vectors(vec_sums, d_model))


def per_device(
    tokens, memory, cotangent, tgt_segments, src_segments,
    self_qkv, self_out, cross_q, cross_kv, cross_out, ffn_up, ffn_down, proj_bias, up_bias, norm_gain, norm_bias,
):
    d_model = tokens.shape[3]
    place = lax.axis_index("seq")
    core = place % MB
    shards = (self_qkv, self_out, cross_q, cross_kv, cross_out, ffn_up, ffn_down)
    docs = jnp.arange(9)
    tgt_counts = jnp.sum(tgt_segments[:, 0, :, None] < docs, axis=1, dtype=jnp.int32)
    src_counts = jnp.sum(src_segments[:, 0, :, None] < docs[1:], axis=1, dtype=jnp.int32)
    counts = jnp.concatenate([tgt_counts, src_counts], axis=1)
    packed = pack_vectors(proj_bias, up_bias, norm_gain, norm_bias, d_model)
    x_full, m_full, ct_full, bounds, vec, weights = gather_plain(
        tokens, memory, cotangent, counts, packed, shards)
    bounds = jnp.concatenate([core.astype(jnp.int32)[None], bounds, jnp.zeros((2,), jnp.int32)])
    results = run_layer(bounds, x_full, m_full, ct_full, vec, weights)
    row_total = MB * lax.axis_size("dp") * tokens.shape[2] * lax.axis_size("seq")
    return settle_plain(x_full, m_full, weights, results, 1.0 / math.sqrt(row_total))


def solution(mesh):
    rows = P(None, "dp", "seq", None)
    ids = P(None, "dp", "seq")
    sharded = P("dp", None)
    columns = P(None, "dp")
    return jax.shard_map(
        per_device,
        mesh=mesh,
        in_specs=(rows, rows, rows, ids, ids) + (sharded,) * 7 + (columns, P("dp"), columns, columns),
        out_specs=(rows, rows, rows) + (sharded,) * 7 + (columns, P("dp"), columns, columns),
        check_vma=False,
    )
```

```python
import functools
import math

import jax
import jax.numpy as jnp
from jax import lax
from jax.experimental import pallas as pl
from jax.experimental.pallas import tpu as pltpu
from jax.sharding import PartitionSpec as P

H = 8
MB = 2
RB = 256
KB = 256
F32 = jnp.float32
BF16 = jnp.bfloat16


def mm(left, right):
    return jnp.dot(left, right, preferred_element_type=F32)


def mm_nt(left, right):
    return lax.dot_general(left, right, (((1,), (1,)), ((), ())), preferred_element_type=F32)


def mm_tn(left, right):
    return lax.dot_general(left, right, (((0,), (0,)), ((), ())), preferred_element_type=F32)


def gelu_parts(values):
    cumulative = 0.5 * (1.0 + lax.erf(values * 0.7071067811865476))
    density = jnp.exp(-0.5 * values * values) * 0.3989422804014327
    return values * cumulative, cumulative + values * density


def normalize(summed, gain, shift):
    center = summed - jnp.mean(summed, axis=-1, keepdims=True)
    scale_inv = lax.rsqrt(jnp.mean(center * center, axis=-1, keepdims=True) + 1e-05)
    unit_rows = center * scale_inv
    return unit_rows * gain + shift, unit_rows, scale_inv


def normalize_back(unit_rows, scale_inv, gain, grad_rows):
    scaled = grad_rows * gain
    return scale_inv * (
        scaled
        - jnp.mean(scaled, axis=-1, keepdims=True)
        - unit_rows * jnp.mean(scaled * unit_rows, axis=-1, keepdims=True)
    )


def fold(values, op):
    rows, cols = values.shape
    return op(values.reshape(rows // 8, 8, cols), axis=0)


def layer_kernel(
    bounds,
    x_hbm, m_hbm, x_ref, ct_ref, vec_all, w_hbm, wdown_hbm,
    layer_out, mixed_out, self_low_out, first_low_out, cdq_out, cmixed_out, cross_low_out,
    second_low_out, up_low_out, active_out, down_low_out, dq_out, part_out,
    dkv_hbm, dckv_hbm, vecg_out,
    wqkv, wout, wcq, wckv, wcout, wup, wdown,
    k_s, kt_s, v_s, vt_s, k_c, kt_c, v_c, vt_c,
    p_s, p_c, dk_s, dv_s, dk_c, dv_c,
    qm_s, qm_c, gtm, gm, ot_s, ot_c, dqt, slope_s, vec_ref, sems,
):
    step = pl.program_id(0)
    steps = pl.num_programs(0)
    t_len, d_model = k_s.shape
    s_len = k_c.shape[0]
    ff = wup.shape[1]
    hd = d_model // H
    core = bounds[0]
    block = 2 * step + core

    def columns(start, count):
        return w_hbm.at[:, pl.ds(start * d_model, count * d_model)]

    loads = [
        pltpu.make_async_copy(src, dst, sems.at[n])
        for n, (src, dst) in enumerate((
            (columns(0, 3), wqkv), (x_hbm.at[:, pl.ds(0, 256)], p_s.at[0]), (x_hbm.at[:, pl.ds(256, 256)], p_s.at[1]),
            (columns(5, 2), wckv), (m_hbm.at[:, pl.ds(0, 256)], p_c.at[0]), (m_hbm.at[:, pl.ds(256, 256)], p_c.at[1]),
            (columns(3, 1), wout), (columns(4, 1), wcq), (columns(7, 1), wcout), (columns(8, ff // d_model), wup),
            (wdown_hbm, wdown),
        ))
    ]

    @pl.when(step == 0)
    def _():
        for load in loads:
            load.start()
        dk_s[...] = jnp.zeros_like(dk_s)
        dv_s[...] = jnp.zeros_like(dv_s)
        dk_c[...] = jnp.zeros_like(dk_c)
        dv_c[...] = jnp.zeros_like(dv_c)
        vecg_out[...] = jnp.zeros_like(vecg_out)
        vec_ref[...] = jnp.sum(vec_all[...].astype(F32), axis=0)
        vec = vec_ref[...]
        vec_t = vec.T

        def project(rows_ref, w_ref, k_at, kt, k, vt, v, bias_row, bias_row_t, count):
            wk = w_ref[:, k_at:k_at + d_model]
            wv = w_ref[:, k_at + d_model:k_at + 2 * d_model]
            wk_t = wk.T
            wv_t = wv.T

            def one(r, carry):
                at = pl.ds(pl.multiple_of(r * RB, RB), RB)
                rows = jnp.concatenate([rows_ref[0, at, :], rows_ref[1, at, :]], axis=1)
                k[at, :] = mm(rows, wk).astype(BF16)
                v[at, :] = (mm(rows, wv) + bias_row).astype(BF16)
                kt[:, at] = mm_nt(wk_t, rows).astype(BF16)
                vt[:, at] = (mm_nt(wv_t, rows) + bias_row_t).astype(BF16)
                return carry

            lax.fori_loop(0, count // RB, one, 0)

        for load in loads[:3]:
            load.wait()
        project(p_s, wqkv, d_model, kt_s, k_s, vt_s, v_s, vec[1:2], vec_t[:, 1:2], t_len)
        for load in loads[3:6]:
            load.wait()
        project(p_c, wckv, 0, kt_c, k_c, vt_c, v_c, vec[4:5], vec_t[:, 4:5], s_len)
        for load in loads[6:]:
            load.wait()

    vec = vec_ref[...]

    qpos = block * RB + lax.broadcasted_iota(jnp.int32, (1, RB), 1)
    lo_s = jnp.zeros((1, RB), jnp.int32)
    hi_s = jnp.full((1, RB), bounds[2], jnp.int32)
    lo_c = jnp.zeros((1, RB), jnp.int32)
    hi_c = jnp.full((1, RB), bounds[2 + 8], jnp.int32)
    for doc in range(1, 8):
        inside = qpos >= bounds[1 + doc]
        lo_s = jnp.where(inside, bounds[1 + doc], lo_s)
        hi_s = jnp.where(inside, bounds[2 + doc], hi_s)
        lo_c = jnp.where(inside, bounds[9 + doc], lo_c)
        hi_c = jnp.where(inside, bounds[10 + doc], hi_c)
    first = block * RB
    last = first + RB - 1
    s_from, s_to, c_from, c_to = 0, bounds[2], 0, bounds[10]
    for doc in range(1, 8):
        in_first = first >= bounds[1 + doc]
        in_last = last >= bounds[1 + doc]
        s_from = jnp.where(in_first, bounds[1 + doc], s_from)
        c_from = jnp.where(in_first, bounds[9 + doc], c_from)
        s_to = jnp.where(in_last, bounds[2 + doc], s_to)
        c_to = jnp.where(in_last, bounds[10 + doc], c_to)

    def block_range(start, stop):
        return lax.div(start, KB), lax.div(stop + (KB - 1), KB)

    def halves(values, axis, h):
        place = lax.broadcasted_iota(jnp.int32, values.shape, axis)
        return jnp.where(place >= hd if h % 2 else place < hd, values, jnp.zeros_like(values))

    def put_masked(rows, rows_t, natural, transposed):
        for h in range(H):
            pair = slice((h // 2) * 2 * hd, (h // 2) * 2 * hd + 2 * hd)
            natural[h] = halves(rows[:, pair], 1, h)
            transposed[h] = halves(rows_t[pair, :], 0, h)

    def attend(qtm, k, vt, p, ot, lo, hi, start, stop):
        j_from, j_to = block_range(start, stop)

        def bias_of(j):
            kpos = j * KB + lax.broadcasted_iota(jnp.int32, (KB, RB), 0)
            return jnp.where((kpos >= lo) & (kpos < hi), 0.0, -1e30).astype(F32)

        def scores(h, at, bias):
            pair = slice((h // 2) * 2 * hd, (h // 2) * 2 * hd + 2 * hd)
            return mm(k[at, pair], qtm[h]) + bias

        def top(j, highest):
            at = pl.ds(pl.multiple_of(j * KB, KB), KB)
            bias = bias_of(j)
            return tuple(jnp.maximum(highest[h], fold(scores(h, at, bias), jnp.max)) for h in range(H))

        highest = lax.fori_loop(j_from, j_to, top, tuple(jnp.full((8, RB), -1e30, F32) for _ in range(H)))
        highest = [jnp.max(part, axis=0, keepdims=True) for part in highest]
        ot[...] = jnp.zeros_like(ot)

        def gather(j, totals):
            at = pl.ds(pl.multiple_of(j * KB, KB), KB)
            bias = bias_of(j)
            out = []
            sc = [scores(h, at, bias) for h in range(H)]
            lows = []
            for h in range(H):
                weights = jnp.exp(sc[h] - highest[h])
                low = weights.astype(BF16)
                lows.append(low)
                p[h, at, :] = low
                out.append(totals[h] + fold(weights, jnp.sum))
            for h in range(H):
                head = slice(h * hd, (h + 1) * hd)
                ot[head, :] += mm(vt[head, at], lows[h])
            return tuple(out)

        totals = lax.fori_loop(j_from, j_to, gather, tuple(jnp.zeros((8, RB), F32) for _ in range(H)))
        inverse = []
        for h in range(H):
            inv = 1.0 / jnp.sum(totals[h], axis=0, keepdims=True)
            head = slice(h * hd, (h + 1) * hd)
            ot[head, :] = ot[head, :] * inv
            inverse.append(inv)
        return inverse

    def attend_back(grad_rows, inverse, qm, k, kt, v, p, ot, dk, dv, start, stop):
        j_from, j_to = block_range(start, stop)
        grad_t = grad_rows.T.astype(F32)
        scaled_t = []
        spread = []
        for h in range(H):
            head = slice(h * hd, (h + 1) * hd)
            low_t = (grad_t[head] * inverse[h]).astype(BF16)
            scaled_t.append(low_t)
            spread.append(jnp.sum(ot[head, :] * low_t.astype(F32), axis=0, keepdims=True))
        scaled_t = jnp.concatenate(scaled_t, axis=0)
        put_masked(scaled_t.T, scaled_t, gm, gtm)
        dqt[...] = jnp.zeros_like(dqt)

        def body(j, carry):
            at = pl.ds(pl.multiple_of(j * KB, KB), KB)
            pairs = [slice((h // 2) * 2 * hd, (h // 2 + 1) * 2 * hd) for h in range(H)]
            prob_grads = [mm(v[at, pairs[h]], gtm[h]) for h in range(H)]
            for h in range(0, H, 2):
                dv[at, pairs[h]] += mm(p[h, at, :], gm[h]) + mm(p[h + 1, at, :], gm[h + 1])
            lows = [(p[h, at, :].astype(F32) * (prob_grads[h] - spread[h])).astype(BF16) for h in range(H)]
            for h in range(0, H, 2):
                dk[at, pairs[h]] += mm(lows[h], qm[h]) + mm(lows[h + 1], qm[h + 1])
            for h in range(H):
                head = slice(h * hd, (h + 1) * hd)
                dqt[head, :] += mm(kt[head, at], lows[h])
            return carry

        lax.fori_loop(j_from, j_to, body, 0)
        return dqt[...].astype(BF16).T

    def add_vec(row, values):
        vecg_out[row:row + 1, :] += jnp.sum(values, axis=0, keepdims=True)

    x_rows = x_ref[...]
    q = ((mm(x_rows, wqkv[:, :d_model]) + vec[0:1]) * 0.125).astype(BF16)
    put_masked(q, q.T, qm_s, gtm)
    inv_s = attend(gtm, k_s, vt_s, p_s, ot_s, lo_s, hi_s, s_from, s_to)
    mixed = ot_s[...].astype(BF16).T
    mixed_out[...] = mixed
    first_norm, unit1, scale1 = normalize(
        x_rows.astype(F32) + (mm(mixed, wout[...]) + vec[2:3]), vec[11:12], vec[14:15])
    first_low = first_norm.astype(BF16)
    first_low_out[...] = first_low
    cq = ((mm(first_low, wcq[...]) + vec[3:4]) * 0.125).astype(BF16)
    put_masked(cq, cq.T, qm_c, gtm)
    inv_c = attend(gtm, k_c, vt_c, p_c, ot_c, lo_c, hi_c, c_from, c_to)
    cmixed = ot_c[...].astype(BF16).T
    cmixed_out[...] = cmixed
    second, unit2, scale2 = normalize(
        first_norm + (mm(cmixed, wcout[...]) + vec[5:6]), vec[12:13], vec[15:16])
    second_low = second.astype(BF16)
    second_low_out[...] = second_low
    tile = d_model
    ffn = None
    for t in range(ff // tile):
        cols = slice(t * tile, (t + 1) * tile)
        hidden = mm(second_low, wup[:, cols]) + vec[7 + t:8 + t]
        smooth, slope = gelu_parts(hidden)
        active = smooth.astype(BF16)
        active_out[:, cols] = active
        slope_s[:, cols] = slope
        part = mm(active, wdown[cols, :])
        ffn = part if ffn is None else ffn + part
    third, unit3, scale3 = normalize(second + (ffn + vec[6:7]), vec[13:14], vec[16:17])
    layer_out[...] = third.astype(BF16)

    grad = ct_ref[...].astype(F32)
    add_vec(13, grad * unit3)
    add_vec(16, grad)
    grad_third = normalize_back(unit3, scale3, vec[13:14], grad)
    down_low = grad_third.astype(BF16)
    down_low_out[...] = down_low
    add_vec(6, down_low.astype(F32))
    back = grad_third
    for t in range(ff // tile):
        cols = slice(t * tile, (t + 1) * tile)
        up_low = (mm_nt(down_low, wdown[cols, :]) * slope_s[:, cols]).astype(BF16)
        up_low_out[:, cols] = up_low
        add_vec(7 + t, up_low.astype(F32))
        back = back + mm_nt(up_low, wup[:, cols])
    add_vec(12, back * unit2)
    add_vec(15, back)
    grad_mid = normalize_back(unit2, scale2, vec[12:13], back)
    cross_low = grad_mid.astype(BF16)
    cross_low_out[...] = cross_low
    add_vec(5, cross_low.astype(F32))
    cross_grad = mm_nt(cross_low, wcout[...]).astype(BF16)
    cdq = attend_back(cross_grad, inv_c, qm_c, k_c, kt_c, v_c, p_c, ot_c, dk_c, dv_c, c_from, c_to) * 0.125
    cdq_out[...] = cdq
    add_vec(3, cdq.astype(F32))
    grad_first = grad_mid + mm_nt(cdq, wcq[...])
    add_vec(11, grad_first * unit1)
    add_vec(14, grad_first)
    grad_in = normalize_back(unit1, scale1, vec[11:12], grad_first)
    self_low = grad_in.astype(BF16)
    self_low_out[...] = self_low
    add_vec(2, self_low.astype(F32))
    self_grad = mm_nt(self_low, wout[...]).astype(BF16)
    dq = attend_back(self_grad, inv_s, qm_s, k_s, kt_s, v_s, p_s, ot_s, dk_s, dv_s, s_from, s_to) * 0.125
    dq_out[...] = dq
    add_vec(0, dq.astype(F32))
    part_out[...] = grad_in + mm_nt(dq, wqkv[:, :d_model])

    @pl.when(step == steps - 1)
    def _():
        add_vec(1, dv_s[...])
        add_vec(4, dv_c[...])
        for n in range(2):
            cols = slice(n * 256, (n + 1) * 256)
            p_s[n] = dk_s[:, cols].astype(BF16)
            p_s[2 + n] = dv_s[:, cols].astype(BF16)
            p_c[n] = dk_c[:, cols].astype(BF16)
            p_c[2 + n] = dv_c[:, cols].astype(BF16)
        stores = [
            pltpu.make_async_copy(p_s.at[0:4], dkv_hbm, sems.at[0]),
            pltpu.make_async_copy(p_c.at[0:4], dckv_hbm, sems.at[1]),
        ]
        for store in stores:
            store.start()
        for store in stores:
            store.wait()


def run_layer(bounds, x_full, m_full, ct_full, vec_all, w_all, w_down):
    t_len, d_model = x_full.shape
    s_len = m_full.shape[0]
    ff = w_down.shape[0]
    steps = t_len // (2 * RB)
    own = t_len // 2
    any_spec = pl.BlockSpec(memory_space=pl.ANY)

    def rows(cols):
        return pl.BlockSpec((RB, cols), lambda i, b: (i, 0))

    def arr(cols, dtype=BF16):
        return jax.ShapeDtypeStruct((own, cols), dtype)

    out_shape = [arr(d_model) for _ in range(8)] + [arr(ff), arr(ff), arr(d_model), arr(d_model), arr(d_model, F32)]
    out_specs = [rows(s.shape[1]) for s in out_shape]
    out_shape += [
        jax.ShapeDtypeStruct((4, t_len, 256), BF16),
        jax.ShapeDtypeStruct((4, s_len, 256), BF16),
        jax.ShapeDtypeStruct((32, d_model), F32),
    ]
    out_specs += [any_spec, any_spec, pl.BlockSpec((32, d_model), lambda i, b: (0, 0))]
    bf = lambda *shape: pltpu.VMEM(shape, BF16)
    fl = lambda *shape: pltpu.VMEM(shape, F32)
    scratch = [bf(d_model, n * d_model) for n in (3, 1, 1, 2, 1)] + [bf(d_model, ff), bf(ff, d_model)] + [
        bf(t_len, d_model), bf(d_model, t_len), bf(t_len, d_model), bf(d_model, t_len),
        bf(s_len, d_model), bf(d_model, s_len), bf(s_len, d_model), bf(d_model, s_len),
        bf(H, t_len, RB), bf(H, s_len, RB),
        fl(t_len, d_model), fl(t_len, d_model), fl(s_len, d_model), fl(s_len, d_model),
        bf(H, RB, 128), bf(H, RB, 128), bf(H, 128, RB), bf(H, RB, 128),
        fl(d_model, RB), fl(d_model, RB), fl(d_model, RB), fl(RB, ff), fl(32, d_model),
        pltpu.SemaphoreType.DMA((11,)),
    ]
    return pl.pallas_call(
        layer_kernel,
        out_shape=out_shape,
        grid_spec=pltpu.PrefetchScalarGridSpec(
            num_scalar_prefetch=1,
            grid=(steps,),
            in_specs=[any_spec, any_spec] + [pl.BlockSpec((RB, d_model), lambda i, b: (2 * i + b[0], 0))] * 2 + [
                      pl.BlockSpec(vec_all.shape, lambda i, b: (0, 0, 0)), any_spec, any_spec],
            out_specs=out_specs,
            scratch_shapes=scratch,
        ),
        compiler_params=pltpu.CompilerParams(vmem_limit_bytes=64 * 1024 * 1024 - 512 * 1024),
        name="layer",
    )(bounds, x_full, m_full, x_full, ct_full, vec_all, w_all, w_down)


def ring_neighbours(at, size):
    odd = lax.rem(at, 2)
    after = jnp.where(odd == 0, jnp.where(at + 2 < size, at + 2, at + 1), jnp.where(at >= 3, at - 2, at - 1))
    before = jnp.where(odd == 0, jnp.where(at >= 2, at - 2, at + 1), jnp.where(at + 2 < size, at + 2, at - 1))
    return after, before


def ring_place(at, size):
    return jnp.where(lax.rem(at, 2) == 0, lax.div(at, 2), size - 1 - lax.div(at, 2))


def ring_member(place, size):
    place = lax.rem(place + 2 * size, size)
    return jnp.where(place < lax.div(size, 2), 2 * place, 2 * (size - 1 - place) + 1)


def gather_kernel(
    size, splits,
    tokens, memory, cotangent, counts, packed, w_qkv, w_out, w_cq, w_ckv, w_cout, w_up, w_down,
    x_full, m_full, c_full, counts_all, vec_all, w_all, d_all,
    send_ring, recv_ring, send_core, recv_core, local_sems, send_rows, recv_rows,
):
    at, place = lax.axis_index("dp"), lax.axis_index("seq")
    micro, core = lax.div(place, 2), lax.rem(place, 2)
    after, before = ring_neighbours(at, size)
    mine = ring_place(at, size)
    core_peer = {"seq": place + 1 - 2 * core}
    chip_peer = {"seq": place + 2 - 4 * micro}
    peers = ({"dp": after}, {"dp": before}, core_peer, chip_peer)

    barrier = pltpu.get_barrier_semaphore()
    for peer in peers:
        pl.semaphore_signal(barrier, inc=1, device_id=peer, device_id_type=pl.DeviceIdType.MESH)

    wide, tall = w_qkv.shape[0], w_down.shape[0]
    local = []
    for n, (shard, column) in enumerate(zip((w_qkv, w_out, w_cq, w_ckv, w_cout, w_up), splits)):
        local.append(pltpu.make_async_copy(
            shard, w_all.at[pl.ds(at * wide, wide), pl.ds(column, shard.shape[1])], local_sems.at[n]))
    local.append(pltpu.make_async_copy(w_down, d_all.at[pl.ds(at * tall, tall)], local_sems.at[6]))
    local.append(pltpu.make_async_copy(packed, vec_all.at[at], local_sems.at[7]))
    for copy in local:
        copy.start()

    pairs = ((tokens, x_full), (memory, m_full), (cotangent, c_full), (counts, counts_all))

    def chunk(n, owner):
        source, full = pairs[n]
        rows = source.shape[-2]
        return full.at[pl.ds(owner * rows, rows)]

    def rows_of(n, index):
        source = pairs[n][0]
        return source.at[index, 0]

    pl.semaphore_wait(barrier, 4)
    across, near, own = [], [], []
    for n in range(4):
        copy = pltpu.make_async_remote_copy(
            rows_of(n, 1 - micro), chunk(n, place), send_rows.at[n, 0], recv_rows.at[n, 0],
            device_id=chip_peer, device_id_type=pl.DeviceIdType.MESH)
        copy.start()
        across.append(copy)
    for n in range(4):
        copy = pltpu.make_async_remote_copy(
            rows_of(n, micro), chunk(n, place), send_rows.at[n, 1], recv_rows.at[n, 1],
            device_id=core_peer, device_id_type=pl.DeviceIdType.MESH)
        copy.start()
        near.append(copy)
        copy = pltpu.make_async_copy(rows_of(n, micro), chunk(n, place), local_sems.at[8 + n])
        copy.start()
        own.append(copy)
    for copy in local:
        copy.wait()

    def piece(stream, way, owner):
        if stream == 2:
            return vec_all.at[owner, pl.ds(16 * way, 16)]
        full, rows = ((w_all, wide), (d_all, tall))[stream]
        quarter = rows // 4
        return full.at[pl.ds(owner * rows + (2 * core + way) * quarter, quarter)]

    ring_sends, core_copies = [], []

    def ring_send(stream, way, step, owner):
        copy = pltpu.make_async_remote_copy(
            piece(stream, way, owner), piece(stream, way, owner), send_ring.at[stream, way, step],
            recv_ring.at[stream, way, step], device_id={"dp": after if way == 0 else before},
            device_id_type=pl.DeviceIdType.MESH)
        copy.start()
        ring_sends.append(copy)
        return copy

    current = {}
    for stream in (2, 0, 1):
        for way in range(2):
            current[stream, way] = ring_send(stream, way, 0, at)
    for step in range(1, size):
        for stream in (2, 0, 1):
            for way in range(2):
                owner = ring_member(mine - step if way == 0 else mine + step, size)
                current[stream, way].wait_recv()
                if step < size - 1:
                    current[stream, way] = ring_send(stream, way, step, owner)
                if stream < 2:
                    copy = pltpu.make_async_remote_copy(
                        piece(stream, way, owner), piece(stream, way, owner), send_core.at[stream, way, step - 1],
                        recv_core.at[stream, way, step - 1], device_id=core_peer,
                        device_id_type=pl.DeviceIdType.MESH)
                    copy.start()
                    core_copies.append(copy)
        if step <= 4:
            n = step - 1
            across[n].wait_recv()
            other = chunk(n, place + 2 - 4 * micro)
            copy = pltpu.make_async_remote_copy(
                other, other, send_rows.at[n, 2], recv_rows.at[n, 2],
                device_id=core_peer, device_id_type=pl.DeviceIdType.MESH)
            copy.start()
            core_copies.append(copy)
    for copy in own:
        copy.wait()
    for copy in near + core_copies:
        copy.wait()
    for copy in across + ring_sends:
        copy.wait_send()


def gather_fused(tokens, memory, cotangent, counts, packed, shards):
    size = lax.axis_size("dp")
    d_model = tokens.shape[3]
    widths = [shard.shape[1] for shard in shards[:6]]
    splits = [sum(widths[:n]) for n in range(6)]
    seq = lax.axis_size("seq")
    any_spec = pl.BlockSpec(memory_space=pl.ANY)
    out_shape = [jax.ShapeDtypeStruct((seq * a.shape[2], d_model), BF16) for a in (tokens, memory, cotangent)]
    out_shape += [
        jax.ShapeDtypeStruct((seq * 8, 128), jnp.int32),
        jax.ShapeDtypeStruct((size, 32, d_model), BF16),
        jax.ShapeDtypeStruct((size * shards[0].shape[0], sum(widths)), BF16),
        jax.ShapeDtypeStruct((size * shards[6].shape[0], d_model), BF16),
    ]
    dma = pltpu.SemaphoreType.DMA
    return pl.pallas_call(
        functools.partial(gather_kernel, size, splits),
        out_shape=out_shape,
        in_specs=[pl.BlockSpec(memory_space=pltpu.VMEM)] * 12,
        out_specs=[any_spec] * 7,
        scratch_shapes=[dma((3, 2, size)), dma((3, 2, size)), dma((2, 2, size)), dma((2, 2, size)), dma((12,)),
                        dma((4, 3)), dma((4, 3))],
        compiler_params=pltpu.CompilerParams(collective_id=0, has_side_effects=True),
        name="gather",
    )(tokens, memory, cotangent, counts, packed, *shards)


MESH = pl.DeviceIdType.MESH
STREAMS = ("down", "up", "qkv", "pair", "outs")


def stream_shapes(d_model, ff, size):
    quarters = (d_model // 4, ff // 4, 3 * d_model // 4, 2 * d_model // 4, 3 * d_model // 4)
    rows = (ff, d_model, d_model, d_model, d_model)
    return [(r, r // size, q) for r, q in zip(rows, quarters)]


def settle_kernel(size, shapes, *refs):
    n_in, n_out, count = 18, 4 + 2 * len(shapes), len(shapes)
    (x_hbm, m_hbm, w_hbm, lo_hbm, mixed_hbm, self_low_hbm, first_low_hbm, cdq_hbm, cmixed_hbm, cross_low_hbm,
     second_low_hbm, up_low_hbm, active_hbm, down_low_hbm, dq_hbm, part_hbm, dkv_hbm, dckv_hbm) = refs[:n_in]
    vec_hbm = refs[n_in]
    outs = refs[n_in + 1:n_in + 1 + n_out]
    lo_home, dt_home, dm_home, vec_out = outs[:4]
    ga, gb = outs[4:4 + count], outs[4 + count:]
    scratch = refs[n_in + 1 + n_out:]
    (xf, mf, wkv, wpair, xo, mixed, self_low, first_low, cdq, cmixed, cross_low, second_low, up_low, active,
     down_low, dq, part, dkv, dckv) = scratch[:19]
    (tz, tz_low, tz_got, mz, mz_low, mz_got, lo_buf, vec_run, vec_got) = scratch[19:28]
    rest = scratch[28:]
    acc, stage, other, ring_out, ring_in, fin = (rest[n * count:(n + 1) * count] for n in range(6))
    (load_sems, store_sems, ring_ss, ring_rs, core_ss, core_rs, fin_ss, fin_rs, row_ss, row_rs, vec_ss, vec_rs,
     lo_ss, lo_rs) = rest[6 * count:]

    at, place = lax.axis_index("dp"), lax.axis_index("seq")
    micro, core = lax.div(place, 2), lax.rem(place, 2)
    after, before = ring_neighbours(at, size)
    mine = ring_place(at, size)
    core_peer = {"seq": place + 1 - 2 * core}
    chip_peer = {"seq": place + 2 - 4 * micro}
    levels = size.bit_length() - 1
    flips = [{"dp": at + (1 << n) * (1 - 2 * lax.rem(lax.div(at, 1 << n), 2))} for n in range(levels)]
    vec_peers = [core_peer, chip_peer] + flips
    d_model = xf.shape[1]
    half = d_model // 2
    t_len, s_len = xf.shape[0], mf.shape[0]

    barrier = pltpu.get_barrier_semaphore()
    greeted = [{"dp": after}, {"dp": before}, core_peer, chip_peer] + flips
    for peer in greeted:
        pl.semaphore_signal(barrier, inc=1, device_id=peer, device_id_type=MESH)

    loads = {}

    def load(name, src, dst):
        copy = pltpu.make_async_copy(src, dst, load_sems.at[len(loads)])
        copy.start()
        loads[name] = copy

    load("vec", vec_hbm.at[pl.ds(0, 24)], vec_run.at[0])
    load("active", active_hbm, active)
    load("down_low", down_low_hbm, down_low)
    load("second_low", second_low_hbm, second_low)
    load("up_low", up_low_hbm, up_low)
    load("dkv", dkv_hbm, dkv)
    load("wkv", w_hbm.at[:, pl.ds(d_model, 2 * d_model)], wkv)
    load("part", part_hbm, part)
    load("dckv", dckv_hbm, dckv)
    load("wpair", w_hbm.at[:, pl.ds(5 * d_model, 2 * d_model)], wpair)
    load("xf", x_hbm, xf)
    for n in range(t_len // (2 * RB)):
        load(("xo", n), x_hbm.at[pl.ds((2 * n + core) * RB, RB)], xo.at[pl.ds(n * RB, RB)])
    load("dq", dq_hbm, dq)
    load("mf", m_hbm, mf)
    for name, src, dst in (("mixed", mixed_hbm, mixed), ("self_low", self_low_hbm, self_low),
                           ("first_low", first_low_hbm, first_low), ("cdq", cdq_hbm, cdq),
                           ("cmixed", cmixed_hbm, cmixed), ("cross_low", cross_low_hbm, cross_low)):
        load(name, src, dst)

    pending = []

    def send(src, dst, send_sem, recv_sem, peer):
        copy = pltpu.make_async_remote_copy(src, dst, send_sem, recv_sem, device_id=peer, device_id_type=MESH)
        copy.start()
        pending.append(copy)
        return copy

    stores = []

    def store(src, dst):
        copy = pltpu.make_async_copy(src, dst, store_sems.at[len(stores)])
        copy.start()
        stores.append(copy)

    pl.semaphore_wait(barrier, len(greeted))

    piece = t_len // 12
    keep, give = [], []

    def pieces_of(index0, slot0, index1, slot1):
        index, slot = jnp.where(core == 0, index0, index1), jnp.where(core == 0, slot0, slot1)
        source = lo_hbm.at[pl.ds(pl.multiple_of(index * piece, 128), piece)]
        return source, lo_buf.at[lax.div(slot, 3), pl.ds(pl.multiple_of(lax.rem(slot, 3) * piece, 128), piece)]

    for n, row in enumerate(((0, 0, 1, 0), (1, 1, 4, 4), (4, 5, 5, 5))):
        copy = pltpu.make_async_copy(*pieces_of(*row), lo_ss.at[n])
        copy.start()
        keep.append(copy)
    for n, row in enumerate(((2, 1, 0, 2), (3, 2, 2, 3), (5, 3, 3, 4))):
        source, target = pieces_of(*row)
        give.append(send(source, target, lo_ss.at[3 + n], lo_rs.at[n], core_peer))

    vec_state = {"level": 0, "copy": None}

    def vec_send():
        level = vec_state["level"]
        vec_state["copy"] = send(vec_run.at[level], vec_got.at[level], vec_ss.at[level], vec_rs.at[level],
                                 vec_peers[level])

    def vec_step():
        level = vec_state["level"]
        vec_state["copy"].wait_recv()
        vec_run[level + 1] = vec_run[level] + vec_got[level]
        vec_state["level"] = level + 1
        if level + 1 < len(vec_peers):
            vec_send()
        else:
            store(vec_run.at[level + 1], vec_out)

    loads["vec"].wait()
    vec_send()

    row_waits = []

    def home_rows(n, rows_of, home):
        store(rows_of(micro), home.at[micro])
        row_waits.append(send(rows_of(1 - micro), home.at[micro], row_ss.at[n], row_rs.at[n], chip_peer))

    def split(values, pieces, s, rows):
        width = values.shape[1] // pieces
        quarter = width // 4
        for p in range(pieces):
            lower = values[:, p * width:p * width + 2 * quarter]
            upper = values[:, p * width + 2 * quarter:(p + 1) * width]
            own = jnp.where(core == 0, lower, upper)
            away = jnp.where(core == 0, upper, lower).astype(BF16)
            for way in range(2):
                acc[s][way, rows, p * quarter:(p + 1) * quarter] = own[:, way * quarter:(way + 1) * quarter]
                stage[s][way, rows, p * quarter:(p + 1) * quarter] = away[:, way * quarter:(way + 1) * quarter]

    core_waits = {}

    def compute(s):
        tile = 256
        if s == 0:
            loads["active"].wait()
            loads["down_low"].wait()

            def one(m, carry):
                rows = pl.ds(pl.multiple_of(m * tile, tile), tile)
                split(mm_tn(active[:, rows], down_low[...]), 1, s, rows)
                return carry

            lax.fori_loop(0, active.shape[1] // tile, one, 0)
        elif s == 1:
            loads["second_low"].wait()
            loads["up_low"].wait()

            def one(m, carry):
                rows = pl.ds(pl.multiple_of(m * tile, tile), tile)
                split(mm_tn(second_low[:, rows], up_low[...]), 1, s, rows)
                return carry

            lax.fori_loop(0, d_model // tile, one, 0)
        elif s == 2:
            loads["xf"].wait()
            for n in range(t_len // (2 * RB)):
                loads["xo", n].wait()
            loads["dq"].wait()

            def one(m, carry):
                rows = pl.ds(pl.multiple_of(m * tile, tile), tile)
                parts = [mm_tn(xo[:, rows], dq[...])]
                whole = xf[:, rows]
                parts += [mm_tn(whole, dkv[n]) for n in range(4)]
                split(jnp.concatenate(parts, axis=1), 3, s, rows)
                return carry

            lax.fori_loop(0, d_model // tile, one, 0)
        elif s == 3:
            loads["mf"].wait()

            def one(m, carry):
                rows = pl.ds(pl.multiple_of(m * tile, tile), tile)
                whole = mf[:, rows]
                split(jnp.concatenate([mm_tn(whole, dckv[n]) for n in range(4)], axis=1), 2, s, rows)
                return carry

            lax.fori_loop(0, d_model // tile, one, 0)
        else:
            for name in ("mixed", "self_low", "first_low", "cdq", "cmixed", "cross_low"):
                loads[name].wait()

            def one(m, carry):
                rows = pl.ds(pl.multiple_of(m * tile, tile), tile)
                parts = [mm_tn(mixed[:, rows], self_low[...]), mm_tn(first_low[:, rows], cdq[...]),
                         mm_tn(cmixed[:, rows], cross_low[...])]
                split(jnp.concatenate(parts, axis=1), 3, s, rows)
                return carry

            lax.fori_loop(0, d_model // tile, one, 0)
        core_waits[s] = send(stage[s], other[s], core_ss.at[s], core_rs.at[s], core_peer)

    ring_waits = {}

    def ring(s, step):
        block = shapes[s][1]
        if step == 0:
            core_waits[s].wait_recv()
        for way in range(2):
            owner = ring_member(mine - 1 - step if way == 0 else mine + 1 + step, size)
            rows = pl.ds(owner * block, block)
            total = acc[s][way, rows, :] + other[s][way, rows, :].astype(F32)
            if step > 0:
                ring_waits[s, way].wait_recv()
                total = total + ring_in[s][way, step - 1].astype(F32)
            if step < size - 1:
                ring_out[s][way, step] = total.astype(BF16)
                ring_waits[s, way] = send(
                    ring_out[s].at[way, step], ring_in[s].at[way, step], ring_ss.at[s, way, step],
                    ring_rs.at[s, way, step], {"dp": after if way == 0 else before})
            else:
                fin[s][way] = total.astype(BF16)

    chip_waits, tail = {}, []

    def finish(s):
        store(fin[s], ga[s].at[core])
        chip_waits[s] = send(fin[s], gb[s].at[core], fin_ss.at[s, 0], fin_rs.at[s, 0], chip_peer)
        tail.append(send(fin[s], ga[s].at[core], fin_ss.at[s, 1], fin_rs.at[s, 1], core_peer))

    def forward(s):
        chip_waits[s].wait_recv()
        tail.append(send(gb[s].at[core], gb[s].at[core], fin_ss.at[s, 2], fin_rs.at[s, 2], core_peer))

    def row_products():
        for name in ("dkv", "wkv", "part", "dckv", "wpair"):
            loads[name].wait()

        def tokens(b, carry):
            rows = pl.ds(pl.multiple_of(b * RB, RB), RB)
            total = None
            for n in range(4):
                product = mm_nt(dkv[n, rows, :], wkv[:, n * 256:(n + 1) * 256])
                total = product if total is None else total + product
            own = part[pl.ds(pl.multiple_of(lax.div(b, 2) * RB, RB), RB), :]
            total = total + jnp.where(lax.rem(b, 2) == core, own, jnp.zeros_like(own))
            tz[rows, :] = total
            tz_low[rows, :] = total.astype(BF16)
            return carry

        lax.fori_loop(0, t_len // RB, tokens, 0)

        def memories(b, carry):
            rows = pl.ds(pl.multiple_of(b * RB, RB), RB)
            total = None
            for n in range(4):
                product = mm_nt(dckv[n, rows, :], wpair[:, n * 256:(n + 1) * 256])
                total = product if total is None else total + product
            mz[rows, :] = total
            mz_low[rows, :] = total.astype(BF16)
            return carry

        lax.fori_loop(0, s_len // RB, memories, 0)
        copies = []
        for n, (low, got, length) in enumerate(((tz_low, tz_got, t_len // 4), (mz_low, mz_got, s_len // 4))):
            for k in range(2):
                start = pl.multiple_of((1 - core + 2 * k) * length, 128)
                copies.append(send(low.at[pl.ds(start, length)], got.at[k], row_ss.at[3 + 2 * n + k],
                                   row_rs.at[3 + 2 * n + k], core_peer))
        return copies

    def row_finish(copies):
        for copy in copies:
            copy.wait_recv()
        for n, (full, got, done, length, home) in enumerate((
                (tz, tz_got, tz_low, t_len // 4, dt_home), (mz, mz_got, mz_low, s_len // 4, dm_home))):

            def rows_at(k, length=length):
                return pl.ds(pl.multiple_of((core + 2 * k) * length, 128), length)

            for k in range(2):
                done[rows_at(k), :] = (full[rows_at(k), :] + got[k].astype(F32)).astype(BF16)
            home_rows(1 + n, lambda k, done=done, rows_at=rows_at: done.at[rows_at(k)], home)

    compute(0)
    ring(0, 0)
    for copy in keep:
        copy.wait()
    for copy in give:
        copy.wait_recv()
    home_rows(0, lambda k: lo_buf.at[k], lo_home)
    vec_step()
    compute(1)
    ring(1, 0)
    ring(0, 1)
    vec_step()
    row_copies = row_products()
    ring(0, 2)
    row_finish(row_copies)
    vec_step()
    compute(2)
    ring(2, 0)
    ring(1, 1)
    ring(0, 3)
    vec_step()
    compute(3)
    ring(3, 0)
    ring(2, 1)
    ring(1, 2)
    ring(0, 4)
    vec_step()
    compute(4)
    ring(4, 0)
    done = {0: 4, 1: 2, 2: 1, 3: 0, 4: 0}
    while any(done[s] < size - 1 for s in range(count)):
        for s in range(count - 1, -1, -1):
            if done[s] < size - 1:
                done[s] += 1
                ring(s, done[s])
                if done[s] == size - 1:
                    finish(s)
        while vec_state["level"] < len(vec_peers):
            vec_step()
    for s in range(count):
        forward(s)
    for copy in row_waits + tail:
        copy.wait_recv()
    for copy in pending:
        copy.wait_send()
    for copy in stores:
        copy.wait()


def settle_fused(x_full, m_full, w_all, results):
    size = lax.axis_size("dp")
    (layer_rows, mixed, self_low, first_low, cdq, cmixed, cross_low, second_low, up_low, active, down_low, dq,
     part, dkv, dckv, vec_sums) = results
    t_len, d_model = x_full.shape
    s_len, ff, own = m_full.shape[0], up_low.shape[1], dq.shape[0]
    shapes = stream_shapes(d_model, ff, size)
    any_spec = pl.BlockSpec(memory_space=pl.ANY)
    out_shape = [
        jax.ShapeDtypeStruct((2, t_len // 4, d_model), BF16),
        jax.ShapeDtypeStruct((2, t_len // 4, d_model), BF16),
        jax.ShapeDtypeStruct((2, s_len // 4, d_model), BF16),
        jax.ShapeDtypeStruct((24, d_model), F32),
    ]
    out_shape += [jax.ShapeDtypeStruct((2, 2, block, q), BF16) for _, block, q in shapes] * 2
    bf = lambda *shape: pltpu.VMEM(shape, BF16)
    fl = lambda *shape: pltpu.VMEM(shape, F32)
    dma = pltpu.SemaphoreType.DMA
    levels = 2 + size.bit_length() - 1
    count = len(shapes)
    scratch = [bf(t_len, d_model), bf(s_len, d_model), bf(d_model, 2 * d_model), bf(d_model, 2 * d_model)]
    scratch += [bf(own, d_model)] * 8 + [bf(own, ff)] * 2 + [bf(own, d_model)] * 2 + [
        fl(own, d_model), bf(4, t_len, 256), bf(4, s_len, 256),
        fl(t_len, d_model), bf(t_len, d_model), bf(2, t_len // 4, d_model),
        fl(s_len, d_model), bf(s_len, d_model), bf(2, s_len // 4, d_model),
        bf(2, t_len // 4, d_model), fl(levels + 1, 24, d_model), fl(levels, 24, d_model),
    ]
    scratch += [fl(2, rows, q) for rows, _, q in shapes]
    scratch += [bf(2, rows, q) for rows, _, q in shapes] * 2
    scratch += [bf(2, size - 1, block, q) for _, block, q in shapes] * 2
    scratch += [bf(2, block, q) for _, block, q in shapes]
    scratch += [dma((24,)), dma((16,)), dma((count, 2, size)), dma((count, 2, size)), dma((count,)), dma((count,)),
                dma((count, 3)), dma((count, 3)), dma((7,)), dma((7,)), dma((levels,)), dma((levels,)), dma((6,)),
                dma((3,))]
    return pl.pallas_call(
        functools.partial(settle_kernel, size, shapes),
        out_shape=out_shape,
        in_specs=[any_spec] * 19,
        out_specs=[any_spec] * len(out_shape),
        scratch_shapes=scratch,
        compiler_params=pltpu.CompilerParams(
            collective_id=1, has_side_effects=True, vmem_limit_bytes=64 * 1024 * 1024 - 512 * 1024),
        name="settle",
    )(x_full, m_full, w_all, layer_rows, mixed, self_low, first_low, cdq, cmixed, cross_low, second_low, up_low,
      active, down_low, dq, part, dkv, dckv, vec_sums)


def finish_kernel(factor, lo, dt, dm, *refs):
    ga, gb = refs[:5], refs[5:10]
    lo_out, dt_out, dm_out, qkv, out, cq, pair, cout, up, down = refs[10:]
    lo_out[...] = lo[...]
    dt_out[...] = dt[...]
    dm_out[...] = dm[...]
    targets = ([down], [up], [(qkv, 0), (qkv, 1), (qkv, 2)], [(pair, 0), (pair, 1)], [out, cq, cout])
    for s, pieces in enumerate(targets):
        for half in range(2):
            for way in range(2):
                total = (ga[s][half, way].astype(F32) + gb[s][half, way].astype(F32)) * factor
                width = total.shape[1] // len(pieces)
                for p, target in enumerate(pieces):
                    ref, slot = target if isinstance(target, tuple) else (target, 0)
                    column = slot * 4 * width + (2 * half + way) * width
                    ref[:, column:column + width] = total[:, p * width:(p + 1) * width]


def finish_fused(settled, factor, d_model, ff):
    lo, dt, dm, vec_sums = settled[:4]
    size = lax.axis_size("dp")
    block = d_model // size
    rows = [jax.ShapeDtypeStruct(a.shape, BF16) for a in (lo, dt, dm)]
    grads = [jax.ShapeDtypeStruct((block, n * d_model), F32) for n in (3, 1, 1, 2, 1)]
    grads += [jax.ShapeDtypeStruct((block, ff), F32), jax.ShapeDtypeStruct((ff // size, d_model), F32)]
    vmem = pl.BlockSpec(memory_space=pltpu.VMEM)
    done = pl.pallas_call(
        functools.partial(finish_kernel, factor),
        out_shape=rows + grads,
        in_specs=[vmem] * 13,
        out_specs=[vmem] * 10,
        compiler_params=pltpu.CompilerParams(vmem_limit_bytes=32 * 1024 * 1024),
        name="finish",
    )(lo, dt, dm, *settled[4:])
    vec_sums = jnp.concatenate([vec_sums, jnp.zeros((8, d_model), F32)], axis=0) * factor
    return (done[0][:, None], done[1][:, None], done[2][:, None], *done[3:], *unpack_vectors(vec_sums, d_model))


def pack_vectors(proj_bias, up_bias, norm_gain, norm_bias, d_model):
    size, at = lax.axis_size("dp"), lax.axis_index("dp")
    width = d_model // size
    rows = jnp.concatenate([proj_bias, jnp.zeros((4, width), BF16), norm_gain, norm_bias], axis=0)
    packed = lax.dynamic_update_slice(jnp.zeros((32, d_model), BF16), rows, (0, at * width))
    flat = lax.dynamic_update_slice(jnp.zeros((4 * d_model,), BF16), up_bias, (at * up_bias.shape[0],))
    return lax.dynamic_update_slice(packed, flat.reshape(4, d_model), (7, 0))


def unpack_vectors(sums, d_model):
    size, at = lax.axis_size("dp"), lax.axis_index("dp")
    width = d_model // size
    own = lax.dynamic_slice(sums, (0, at * width), (32, width))
    up = lax.dynamic_slice(sums[7:11].reshape(-1), (at * 4 * width,), (4 * width,))
    return own[:7], up, own[11:14], own[14:17]


def gather_plain(tokens, memory, cotangent, counts, packed, shards):
    micro = lax.axis_index("seq") // MB

    def whole(rows):
        return lax.all_gather(lax.squeeze(rows, (1,)), "seq", axis=1, tiled=True)[micro]

    weights = [lax.all_gather(shard, "dp", axis=0, tiled=True) for shard in shards]
    vec_all = lax.psum(packed, "dp")[None]
    bounds = lax.psum(counts[:, 0, 0], "seq")[micro]
    w_all = jnp.concatenate(weights[:6], axis=1)
    return whole(tokens), whole(memory), whole(cotangent), bounds, vec_all, w_all, weights[6]


def own_rows(rows, core):
    blocks = rows.reshape(rows.shape[0] // (2 * RB), 2, RB, rows.shape[1])
    return blocks[:, core].reshape(rows.shape[0] // 2, rows.shape[1])


def spread_rows(rows, core):
    blocks = rows.reshape(rows.shape[0] // RB, 1, RB, rows.shape[1])
    blocks = jnp.concatenate([blocks, jnp.zeros_like(blocks)], axis=1)
    blocks = jnp.where(core == 0, blocks, blocks[:, ::-1])
    return blocks.reshape(rows.shape[0] * 2, rows.shape[1])


def settle_plain(x_full, m_full, w_all, results, factor):
    (layer_rows, mixed, self_low, first_low, cdq, cmixed, cross_low, second_low, up_low, active, down_low, dq,
     part, dkv, dckv, vec_sums) = results
    place = lax.axis_index("seq")
    micro, core = place // MB, place % MB
    d_model = x_full.shape[1]
    dkv = jnp.moveaxis(dkv, 0, 1).reshape(x_full.shape[0], 2 * d_model)
    dckv = jnp.moveaxis(dckv, 0, 1).reshape(m_full.shape[0], 2 * d_model)
    input_rows = spread_rows(part, core) + mm_nt(dkv, w_all[:, d_model:3 * d_model])
    memory_rows = mm_nt(dckv, w_all[:, 5 * d_model:7 * d_model])

    def home(rows):
        both = jnp.stack([rows, jnp.zeros_like(rows)])
        both = jnp.where(micro == 0, both, both[::-1])
        return lax.psum_scatter(both, "seq", scatter_dimension=1, tiled=True).astype(BF16)[:, None]

    grads = [
        jnp.concatenate([mm_tn(own_rows(x_full, core), dq), mm_tn(x_full, dkv)], axis=1),
        mm_tn(mixed, self_low), mm_tn(first_low, cdq), mm_tn(m_full, dckv), mm_tn(cmixed, cross_low),
        mm_tn(second_low, up_low), mm_tn(active, down_low),
    ]
    grads = [
        lax.psum(lax.psum_scatter(grad, "dp", scatter_dimension=0, tiled=True), "seq") * factor for grad in grads
    ]
    vec_sums = lax.psum(vec_sums, ("dp", "seq")) * factor
    return (home(spread_rows(layer_rows.astype(F32), core)), home(input_rows), home(memory_rows), *grads,
            *unpack_vectors(vec_sums, d_model))


def per_device(
    tokens, memory, cotangent, tgt_segments, src_segments,
    self_qkv, self_out, cross_q, cross_kv, cross_out, ffn_up, ffn_down, proj_bias, up_bias, norm_gain, norm_bias,
):
    d_model = tokens.shape[3]
    place = lax.axis_index("seq")
    core = place % MB
    shards = (self_qkv, self_out, cross_q, cross_kv, cross_out, ffn_up, ffn_down)
    docs = jnp.arange(9)
    tgt_counts = jnp.sum(tgt_segments[:, 0, :, None] < docs, axis=1, dtype=jnp.int32)
    src_counts = jnp.sum(src_segments[:, 0, :, None] < docs[1:], axis=1, dtype=jnp.int32)
    counts = jnp.concatenate([tgt_counts, src_counts], axis=1)
    counts = jnp.pad(counts[:, None, None], ((0, 0), (0, 0), (0, 7), (0, 128 - counts.shape[1])))
    packed = pack_vectors(proj_bias, up_bias, norm_gain, norm_bias, d_model)
    size, rows = lax.axis_size("dp"), self_qkv.shape[0]
    fused = rows % 64 == 0 and size & (size - 1) == 0 and size > 2
    factor = 1.0 / math.sqrt(MB * size * tokens.shape[2] * lax.axis_size("seq"))
    if fused:
        x_full, m_full, ct_full, counts, vec_all, w_all, w_down = gather_fused(
            tokens, memory, cotangent, counts, packed, shards)
        bounds = jnp.sum(counts.reshape(-1, 8, 128), axis=0)[0]
    else:
        x_full, m_full, ct_full, bounds, vec_all, w_all, w_down = gather_plain(
            tokens, memory, cotangent, counts, packed, shards)
    bounds = jnp.concatenate([core.astype(jnp.int32)[None], bounds[:19]])
    results = run_layer(bounds, x_full, m_full, ct_full, vec_all, w_all, w_down)
    if fused:
        return finish_fused(settle_fused(x_full, m_full, w_all, results), factor, d_model, ffn_up.shape[1])
    return settle_plain(x_full, m_full, w_all, results, factor)


def solution(mesh):
    rows = P(None, "dp", "seq", None)
    ids = P(None, "dp", "seq")
    sharded = P("dp", None)
    columns = P(None, "dp")
    return jax.shard_map(
        per_device,
        mesh=mesh,
        in_specs=(rows, rows, rows, ids, ids) + (sharded,) * 7 + (columns, P("dp"), columns, columns),
        out_specs=(rows, rows, rows) + (sharded,) * 7 + (columns, P("dp"), columns, columns),
        check_vma=False,
    )
```

```python
import functools
import math

import jax
import jax.numpy as jnp
from jax import lax
from jax.experimental import pallas as pl
from jax.experimental.pallas import tpu as pltpu
from jax.sharding import PartitionSpec as P

H = 8
MB = 2
RB = 256
KB = 256
F32 = jnp.float32
BF16 = jnp.bfloat16


def mm(left, right):
    return jnp.dot(left, right, preferred_element_type=F32)


def mm_nt(left, right):
    return lax.dot_general(left, right, (((1,), (1,)), ((), ())), preferred_element_type=F32)


def mm_tn(left, right):
    return lax.dot_general(left, right, (((0,), (0,)), ((), ())), preferred_element_type=F32)


def gelu_parts(values):
    cumulative = 0.5 * (1.0 + lax.erf(values * 0.7071067811865476))
    density = jnp.exp(-0.5 * values * values) * 0.3989422804014327
    return values * cumulative, cumulative + values * density


def normalize(summed, gain, shift):
    center = summed - jnp.mean(summed, axis=-1, keepdims=True)
    scale_inv = lax.rsqrt(jnp.mean(center * center, axis=-1, keepdims=True) + 1e-05)
    unit_rows = center * scale_inv
    return unit_rows * gain + shift, unit_rows, scale_inv


def normalize_back(unit_rows, scale_inv, gain, grad_rows):
    scaled = grad_rows * gain
    return scale_inv * (
        scaled
        - jnp.mean(scaled, axis=-1, keepdims=True)
        - unit_rows * jnp.mean(scaled * unit_rows, axis=-1, keepdims=True)
    )


def fold(values, op):
    rows, cols = values.shape
    return op(values.reshape(rows // 8, 8, cols), axis=0)


def layer_kernel(
    counts,
    x_hbm, m_hbm, x_ref, ct_ref, vec_all, w_hbm, wdown_hbm,
    layer_out, mixed_out, self_low_out, first_low_out, cdq_out, cmixed_out, cross_low_out,
    second_low_out, up_low_out, active_out, down_low_out, dq_out, part_out,
    dkv_hbm, dckv_hbm, vecg_out,
    wqkv, wout, wcq, wckv, wcout, wup, wdown,
    k_s, kt_s, v_s, vt_s, k_c, kt_c, v_c, vt_c,
    p_s, p_c, dk_s, dv_s, dk_c, dv_c,
    qm_s, qm_c, gtm, gm, ot_s, ot_c, dqt, slope_s, vec_ref, kn_s, kn_c, sems,
):
    step = pl.program_id(0)
    steps = pl.num_programs(0)
    t_len, d_model = k_s.shape
    s_len = k_c.shape[0]
    ff = wup.shape[1]
    hd = d_model // H
    core = counts[32, 0]
    tgt_starts = [0] + [counts[0, d] + counts[8, d] + counts[16, d] + counts[24, d] for d in range(1, 9)]
    src_starts = [0] + [counts[0, d] + counts[8, d] + counts[16, d] + counts[24, d] for d in range(9, 17)]
    block = 2 * step + core

    def columns(start, count):
        return w_hbm.at[:, pl.ds(start * d_model, count * d_model)]

    loads = [
        pltpu.make_async_copy(src, dst, sems.at[n])
        for n, (src, dst) in enumerate((
            (columns(0, 3), wqkv), (x_hbm.at[:, pl.ds(0, 256)], p_s.at[0]), (x_hbm.at[:, pl.ds(256, 256)], p_s.at[1]),
            (columns(5, 2), wckv), (m_hbm.at[:, pl.ds(0, 256)], p_c.at[0]), (m_hbm.at[:, pl.ds(256, 256)], p_c.at[1]),
            (columns(3, 1), wout), (columns(4, 1), wcq), (columns(7, 1), wcout), (columns(8, ff // d_model), wup),
            (wdown_hbm, wdown),
        ))
    ]

    @pl.when(step == 0)
    def _():
        for load in loads[:6]:
            load.start()
        dk_s[...] = jnp.zeros_like(dk_s)
        dv_s[...] = jnp.zeros_like(dv_s)
        dk_c[...] = jnp.zeros_like(dk_c)
        dv_c[...] = jnp.zeros_like(dv_c)
        vecg_out[...] = jnp.zeros_like(vecg_out)
        vec_ref[...] = jnp.sum(vec_all[...].astype(F32), axis=0)
        vec = vec_ref[...]
        vec_t = vec.T

        def project(rows_ref, w_ref, k_at, kt, k, vt, v, norms, bias_row, bias_row_t, count):
            norms[...] = jnp.zeros_like(norms)
            wk = w_ref[:, k_at:k_at + d_model]
            wv = w_ref[:, k_at + d_model:k_at + 2 * d_model]
            wk_t = wk.T
            wv_t = wv.T

            def one(r, carry):
                at = pl.ds(pl.multiple_of(r * RB, RB), RB)
                rows = jnp.concatenate([rows_ref[0, at, :], rows_ref[1, at, :]], axis=1)
                k[at, :] = mm(rows, wk).astype(BF16)
                v[at, :] = (mm(rows, wv) + bias_row).astype(BF16)
                keys_t = mm_nt(wk_t, rows)
                kt[:, at] = keys_t.astype(BF16)
                squares = keys_t * keys_t
                for h in range(H):
                    own = jnp.sum(fold(squares[h * hd:(h + 1) * hd], jnp.sum), axis=0, keepdims=True)
                    norms[h:h + 1, :] = jnp.maximum(norms[h:h + 1, :], own)
                vt[:, at] = (mm_nt(wv_t, rows) + bias_row_t).astype(BF16)
                return carry

            lax.fori_loop(0, count // RB, one, 0)

        for load in loads[:3]:
            load.wait()
        for load in loads[6:]:
            load.start()
        project(p_s, wqkv, d_model, kt_s, k_s, vt_s, v_s, kn_s, vec[1:2], vec_t[:, 1:2], t_len)
        for load in loads[3:6]:
            load.wait()
        project(p_c, wckv, 0, kt_c, k_c, vt_c, v_c, kn_c, vec[4:5], vec_t[:, 4:5], s_len)
        for load in loads[6:]:
            load.wait()

    vec = vec_ref[...]

    qpos = block * RB + lax.broadcasted_iota(jnp.int32, (1, RB), 1)
    lo_s = jnp.zeros((1, RB), jnp.int32)
    hi_s = jnp.full((1, RB), tgt_starts[1], jnp.int32)
    lo_c = jnp.zeros((1, RB), jnp.int32)
    hi_c = jnp.full((1, RB), src_starts[1], jnp.int32)
    for doc in range(1, 8):
        inside = qpos >= tgt_starts[doc]
        lo_s = jnp.where(inside, tgt_starts[doc], lo_s)
        hi_s = jnp.where(inside, tgt_starts[doc + 1], hi_s)
        lo_c = jnp.where(inside, src_starts[doc], lo_c)
        hi_c = jnp.where(inside, src_starts[doc + 1], hi_c)
    first = block * RB
    last = first + RB - 1
    s_from, s_to, c_from, c_to = 0, tgt_starts[1], 0, src_starts[1]
    for doc in range(1, 8):
        in_first = first >= tgt_starts[doc]
        in_last = last >= tgt_starts[doc]
        s_from = jnp.where(in_first, tgt_starts[doc], s_from)
        c_from = jnp.where(in_first, src_starts[doc], c_from)
        s_to = jnp.where(in_last, tgt_starts[doc + 1], s_to)
        c_to = jnp.where(in_last, src_starts[doc + 1], c_to)

    def block_range(start, stop, length):
        base = lax.div(start, 128) * 128
        count = lax.div(stop - base + (KB - 1), KB)
        return jnp.minimum(base, length - count * KB), count

    def halves(values, axis, h):
        place = lax.broadcasted_iota(jnp.int32, values.shape, axis)
        return jnp.where(place >= hd if h % 2 else place < hd, values, jnp.zeros_like(values))

    def put_masked(rows, rows_t, natural, transposed):
        for h in range(H):
            pair = slice((h // 2) * 2 * hd, (h // 2) * 2 * hd + 2 * hd)
            natural[h] = halves(rows[:, pair], 1, h)
            transposed[h] = halves(rows_t[pair, :], 0, h)

    def key_rows(base, j):
        return pl.ds(pl.multiple_of(base + j * KB, 128), KB)

    def attend(query_t, qtm, k, vt, p, ot, norms, lo, hi, start, stop):
        base, count = block_range(start, stop, k.shape[0])
        squares = query_t.astype(F32)
        squares = squares * squares
        bound = None
        for h in range(H):
            own = jnp.sum(fold(squares[h * hd:(h + 1) * hd], jnp.sum), axis=0, keepdims=True)
            own = own * jnp.max(norms[h:h + 1, :], axis=1, keepdims=True)
            bound = own if bound is None else jnp.maximum(bound, own)
        small = jnp.max(bound) <= 3600.0
        shifts = jnp.where(small, 0, count)

        def bias_of(j):
            kpos = base + j * KB + lax.broadcasted_iota(jnp.int32, (KB, RB), 0)
            return jnp.where((kpos >= lo) & (kpos < hi), 0.0, -1e30).astype(F32)

        def scores(h, at, bias):
            pair = slice((h // 2) * 2 * hd, (h // 2) * 2 * hd + 2 * hd)
            return mm(k[at, pair], qtm[h]) + bias

        def top(j, highest):
            at = key_rows(base, j)
            bias = bias_of(j)
            return tuple(jnp.maximum(highest[h], fold(scores(h, at, bias), jnp.max)) for h in range(H))

        lowest = jnp.full((8, RB), jnp.where(small, 0.0, -1e30), F32)
        highest = lax.fori_loop(0, shifts, top, (lowest,) * H)
        highest = [jnp.max(part, axis=0, keepdims=True) for part in highest]
        ot[...] = jnp.zeros_like(ot)

        def gather(j, totals):
            at = key_rows(base, j)
            bias = bias_of(j)
            out = []
            sc = [scores(h, at, bias) for h in range(H)]
            lows = []
            for h in range(H):
                weights = jnp.exp(sc[h] - highest[h])
                low = weights.astype(BF16)
                lows.append(low)
                p[h, at, :] = low
                out.append(totals[h] + fold(weights, jnp.sum))
            for h in range(H):
                head = slice(h * hd, (h + 1) * hd)
                ot[head, :] += mm(vt[head, at], lows[h])
            return tuple(out)

        totals = lax.fori_loop(0, count, gather, (jnp.zeros((8, RB), F32),) * H)
        inverse = []
        for h in range(H):
            inv = 1.0 / jnp.sum(totals[h], axis=0, keepdims=True)
            head = slice(h * hd, (h + 1) * hd)
            ot[head, :] = ot[head, :] * inv
            inverse.append(inv)
        return inverse

    def attend_back(grad_rows, inverse, qm, k, kt, v, p, ot, dk, dv, start, stop):
        base, count = block_range(start, stop, k.shape[0])
        grad_t = grad_rows.T.astype(F32)
        scaled_t = []
        spread = []
        for h in range(H):
            head = slice(h * hd, (h + 1) * hd)
            low_t = (grad_t[head] * inverse[h]).astype(BF16)
            scaled_t.append(low_t)
            spread.append(jnp.sum(ot[head, :] * low_t.astype(F32), axis=0, keepdims=True))
        scaled_t = jnp.concatenate(scaled_t, axis=0)
        put_masked(scaled_t.T, scaled_t, gm, gtm)
        dqt[...] = jnp.zeros_like(dqt)

        def body(j, carry):
            at = key_rows(base, j)
            pairs = [slice((h // 2) * 2 * hd, (h // 2 + 1) * 2 * hd) for h in range(H)]
            prob_grads = [mm(v[at, pairs[h]], gtm[h]) for h in range(H)]
            for h in range(0, H, 2):
                dv[at, pairs[h]] += mm(p[h, at, :], gm[h]) + mm(p[h + 1, at, :], gm[h + 1])
            lows = [(p[h, at, :].astype(F32) * (prob_grads[h] - spread[h])).astype(BF16) for h in range(H)]
            for h in range(0, H, 2):
                dk[at, pairs[h]] += mm(lows[h], qm[h]) + mm(lows[h + 1], qm[h + 1])
            for h in range(H):
                head = slice(h * hd, (h + 1) * hd)
                dqt[head, :] += mm(kt[head, at], lows[h])
            return carry

        lax.fori_loop(0, count, body, 0)
        return dqt[...].astype(BF16).T

    def add_vec(row, values):
        vecg_out[row:row + 1, :] += jnp.sum(values, axis=0, keepdims=True)

    x_rows = x_ref[...]
    q = ((mm(x_rows, wqkv[:, :d_model]) + vec[0:1]) * 0.125).astype(BF16)
    q_t = q.T
    put_masked(q, q_t, qm_s, gtm)
    inv_s = attend(q_t, gtm, k_s, vt_s, p_s, ot_s, kn_s, lo_s, hi_s, s_from, s_to)
    mixed = ot_s[...].astype(BF16).T
    mixed_out[...] = mixed
    first_norm, unit1, scale1 = normalize(
        x_rows.astype(F32) + (mm(mixed, wout[...]) + vec[2:3]), vec[11:12], vec[14:15])
    first_low = first_norm.astype(BF16)
    first_low_out[...] = first_low
    cq = ((mm(first_low, wcq[...]) + vec[3:4]) * 0.125).astype(BF16)
    cq_t = cq.T
    put_masked(cq, cq_t, qm_c, gtm)
    inv_c = attend(cq_t, gtm, k_c, vt_c, p_c, ot_c, kn_c, lo_c, hi_c, c_from, c_to)
    cmixed = ot_c[...].astype(BF16).T
    cmixed_out[...] = cmixed
    second, unit2, scale2 = normalize(
        first_norm + (mm(cmixed, wcout[...]) + vec[5:6]), vec[12:13], vec[15:16])
    second_low = second.astype(BF16)
    second_low_out[...] = second_low
    tile = d_model
    ffn = None
    for t in range(ff // tile):
        cols = slice(t * tile, (t + 1) * tile)
        hidden = mm(second_low, wup[:, cols]) + vec[7 + t:8 + t]
        smooth, slope = gelu_parts(hidden)
        active = smooth.astype(BF16)
        active_out[:, cols] = active
        slope_s[:, cols] = slope
        part = mm(active, wdown[cols, :])
        ffn = part if ffn is None else ffn + part
    third, unit3, scale3 = normalize(second + (ffn + vec[6:7]), vec[13:14], vec[16:17])
    layer_out[...] = third.astype(BF16)

    grad = ct_ref[...].astype(F32)
    add_vec(13, grad * unit3)
    add_vec(16, grad)
    grad_third = normalize_back(unit3, scale3, vec[13:14], grad)
    down_low = grad_third.astype(BF16)
    down_low_out[...] = down_low
    add_vec(6, down_low.astype(F32))
    back = grad_third
    for t in range(ff // tile):
        cols = slice(t * tile, (t + 1) * tile)
        up_low = (mm_nt(down_low, wdown[cols, :]) * slope_s[:, cols]).astype(BF16)
        up_low_out[:, cols] = up_low
        add_vec(7 + t, up_low.astype(F32))
        back = back + mm_nt(up_low, wup[:, cols])
    add_vec(12, back * unit2)
    add_vec(15, back)
    grad_mid = normalize_back(unit2, scale2, vec[12:13], back)
    cross_low = grad_mid.astype(BF16)
    cross_low_out[...] = cross_low
    add_vec(5, cross_low.astype(F32))
    cross_grad = mm_nt(cross_low, wcout[...]).astype(BF16)
    cdq = attend_back(cross_grad, inv_c, qm_c, k_c, kt_c, v_c, p_c, ot_c, dk_c, dv_c, c_from, c_to) * 0.125
    cdq_out[...] = cdq

    def put_out(slabs, dk, dv):
        for n in range(2):
            cols = slice(n * 256, (n + 1) * 256)
            slabs[n] = dk[:, cols].astype(BF16)
            slabs[2 + n] = dv[:, cols].astype(BF16)

    @pl.when(step == steps - 1)
    def _():
        add_vec(4, dv_c[...])
        put_out(p_c, dk_c, dv_c)
        pltpu.make_async_copy(p_c.at[0:4], dckv_hbm, sems.at[1]).start()

    add_vec(3, cdq.astype(F32))
    grad_first = grad_mid + mm_nt(cdq, wcq[...])
    add_vec(11, grad_first * unit1)
    add_vec(14, grad_first)
    grad_in = normalize_back(unit1, scale1, vec[11:12], grad_first)
    self_low = grad_in.astype(BF16)
    self_low_out[...] = self_low
    add_vec(2, self_low.astype(F32))
    self_grad = mm_nt(self_low, wout[...]).astype(BF16)
    dq = attend_back(self_grad, inv_s, qm_s, k_s, kt_s, v_s, p_s, ot_s, dk_s, dv_s, s_from, s_to) * 0.125
    dq_out[...] = dq
    add_vec(0, dq.astype(F32))
    part_out[...] = grad_in + mm_nt(dq, wqkv[:, :d_model])

    @pl.when(step == steps - 1)
    def _():
        add_vec(1, dv_s[...])
        put_out(p_s, dk_s, dv_s)
        pltpu.make_async_copy(p_s.at[0:4], dkv_hbm, sems.at[0]).start()
        pltpu.make_async_copy(p_s.at[0:4], dkv_hbm, sems.at[0]).wait()
        pltpu.make_async_copy(p_c.at[0:4], dckv_hbm, sems.at[1]).wait()


def run_layer(counts, x_full, m_full, ct_full, vec_all, w_all, w_down):
    t_len, d_model = x_full.shape
    s_len = m_full.shape[0]
    ff = w_down.shape[0]
    steps = t_len // (2 * RB)
    own = t_len // 2
    any_spec = pl.BlockSpec(memory_space=pl.ANY)

    def rows(cols):
        return pl.BlockSpec((RB, cols), lambda i, b: (i, 0))

    def arr(cols, dtype=BF16):
        return jax.ShapeDtypeStruct((own, cols), dtype)

    out_shape = [arr(d_model) for _ in range(8)] + [arr(ff), arr(ff), arr(d_model), arr(d_model), arr(d_model, F32)]
    out_specs = [rows(s.shape[1]) for s in out_shape]
    out_shape += [
        jax.ShapeDtypeStruct((4, t_len, 256), BF16),
        jax.ShapeDtypeStruct((4, s_len, 256), BF16),
        jax.ShapeDtypeStruct((32, d_model), F32),
    ]
    out_specs += [any_spec, any_spec, pl.BlockSpec((32, d_model), lambda i, b: (0, 0))]
    bf = lambda *shape: pltpu.VMEM(shape, BF16)
    fl = lambda *shape: pltpu.VMEM(shape, F32)
    scratch = [bf(d_model, n * d_model) for n in (3, 1, 1, 2, 1)] + [bf(d_model, ff), bf(ff, d_model)] + [
        bf(t_len, d_model), bf(d_model, t_len), bf(t_len, d_model), bf(d_model, t_len),
        bf(s_len, d_model), bf(d_model, s_len), bf(s_len, d_model), bf(d_model, s_len),
        bf(H, t_len, RB), bf(H, s_len, RB),
        fl(t_len, d_model), fl(t_len, d_model), fl(s_len, d_model), fl(s_len, d_model),
        bf(H, RB, 128), bf(H, RB, 128), bf(H, 128, RB), bf(H, RB, 128),
        fl(d_model, RB), fl(d_model, RB), fl(d_model, RB), fl(RB, ff), fl(32, d_model), fl(H, RB), fl(H, RB),
        pltpu.SemaphoreType.DMA((11,)),
    ]
    return pl.pallas_call(
        layer_kernel,
        out_shape=out_shape,
        grid_spec=pltpu.PrefetchScalarGridSpec(
            num_scalar_prefetch=1,
            grid=(steps,),
            in_specs=[any_spec, any_spec] + [pl.BlockSpec((RB, d_model), lambda i, b: (2 * i + b[32, 0], 0))] * 2 + [
                      pl.BlockSpec(vec_all.shape, lambda i, b: (0, 0, 0)), any_spec, any_spec],
            out_specs=out_specs,
            scratch_shapes=scratch,
        ),
        compiler_params=pltpu.CompilerParams(vmem_limit_bytes=64 * 1024 * 1024 - 512 * 1024),
        name="layer",
    )(counts, x_full, m_full, x_full, ct_full, vec_all, w_all, w_down)


def ring_neighbours(at, size):
    odd = lax.rem(at, 2)
    after = jnp.where(odd == 0, jnp.where(at + 2 < size, at + 2, at + 1), jnp.where(at >= 3, at - 2, at - 1))
    before = jnp.where(odd == 0, jnp.where(at >= 2, at - 2, at + 1), jnp.where(at + 2 < size, at + 2, at - 1))
    return after, before


def ring_place(at, size):
    return jnp.where(lax.rem(at, 2) == 0, lax.div(at, 2), size - 1 - lax.div(at, 2))


def ring_member(place, size):
    place = lax.rem(place + 2 * size, size)
    return jnp.where(place < lax.div(size, 2), 2 * place, 2 * (size - 1 - place) + 1)


def gather_kernel(
    size, splits,
    tokens, memory, cotangent, tgt_ids, src_ids, proj_bias, up_bias, norm_gain, norm_bias,
    w_qkv, w_out, w_cq, w_ckv, w_cout, w_up, w_down,
    x_full, m_full, c_full, counts_all, vec_all, w_all, d_all,
    counts, spread, packed, send_ring, recv_ring, send_core, recv_core, local_sems, send_rows, recv_rows,
):
    at, place = lax.axis_index("dp"), lax.axis_index("seq")
    micro, core = lax.div(place, 2), lax.rem(place, 2)
    after, before = ring_neighbours(at, size)
    mine = ring_place(at, size)
    core_peer = {"seq": place + 1 - 2 * core}
    chip_peer = {"seq": place + 2 - 4 * micro}
    peers = ({"dp": after}, {"dp": before}, core_peer, chip_peer)

    barrier = pltpu.get_barrier_semaphore()
    for peer in peers:
        pl.semaphore_signal(barrier, inc=1, device_id=peer, device_id_type=pl.DeviceIdType.MESH)

    d_model = spread.shape[1]
    width = proj_bias.shape[1]

    def put(row, values, start, length):
        cols = lax.broadcasted_iota(jnp.int32, (length, d_model), 1)
        ones = lax.broadcasted_iota(jnp.int32, (length, d_model), 0) + start == cols
        spread[row:row + values.shape[0], :] = mm(values, jnp.where(ones, 1.0, 0.0).astype(BF16))

    spread[...] = jnp.zeros_like(spread)
    put(0, proj_bias[...], at * width, width)
    for n in range(4):
        put(7 + n, up_bias[...], at * 4 * width - n * d_model, 4 * width)
    put(11, norm_gain[...], at * width, width)
    put(14, norm_bias[...], at * width, width)
    packed[...] = spread[...].astype(BF16)
    lane = lax.broadcasted_iota(jnp.int32, (8, 128), 1)
    for index in range(2):
        total = jnp.zeros((8, 128), F32)
        for ids, docs, offset in ((tgt_ids, range(1, 9), 0), (src_ids, range(1, 9), 8)):
            row = ids[index]
            for doc in docs:
                below = jnp.sum(jnp.where(row < doc, 1.0, 0.0), axis=1, keepdims=True)
                total = total + jnp.where(lane == doc + offset, below, 0.0)
        counts[index, 0] = total.astype(jnp.int32)
    counts[2, 0] = jnp.full((8, 128), core, jnp.int32)

    wide, tall = w_qkv.shape[0], w_down.shape[0]
    local = []
    for n, (shard, column) in enumerate(zip((w_qkv, w_out, w_cq, w_ckv, w_cout, w_up), splits)):
        local.append(pltpu.make_async_copy(
            shard, w_all.at[pl.ds(at * wide, wide), pl.ds(column, shard.shape[1])], local_sems.at[n]))
    local.append(pltpu.make_async_copy(w_down, d_all.at[pl.ds(at * tall, tall)], local_sems.at[6]))
    local.append(pltpu.make_async_copy(packed, vec_all.at[at], local_sems.at[7]))
    local.append(pltpu.make_async_copy(counts.at[2, 0], counts_all.at[pl.ds(32, 8)], local_sems.at[12]))
    for copy in local:
        copy.start()

    pairs = ((tokens, x_full), (memory, m_full), (cotangent, c_full), (counts, counts_all))

    def chunk(n, owner):
        source, full = pairs[n]
        rows = source.shape[-2]
        return full.at[pl.ds(owner * rows, rows)]

    def rows_of(n, index):
        source = pairs[n][0]
        return source.at[index, 0]

    pl.semaphore_wait(barrier, 4)
    across, near, own = [], [], []
    for n in range(4):
        copy = pltpu.make_async_remote_copy(
            rows_of(n, 1 - micro), chunk(n, place), send_rows.at[n, 0], recv_rows.at[n, 0],
            device_id=chip_peer, device_id_type=pl.DeviceIdType.MESH)
        copy.start()
        across.append(copy)
    for n in range(4):
        copy = pltpu.make_async_remote_copy(
            rows_of(n, micro), chunk(n, place), send_rows.at[n, 1], recv_rows.at[n, 1],
            device_id=core_peer, device_id_type=pl.DeviceIdType.MESH)
        copy.start()
        near.append(copy)
        copy = pltpu.make_async_copy(rows_of(n, micro), chunk(n, place), local_sems.at[8 + n])
        copy.start()
        own.append(copy)
    for copy in local:
        copy.wait()

    def piece(stream, way, owner):
        if stream == 2:
            return vec_all.at[owner, pl.ds(16 * way, 16)]
        full, rows = ((w_all, wide), (d_all, tall))[stream]
        quarter = rows // 4
        return full.at[pl.ds(owner * rows + (2 * core + way) * quarter, quarter)]

    ring_sends, core_copies = [], []

    def ring_send(stream, way, step, owner):
        copy = pltpu.make_async_remote_copy(
            piece(stream, way, owner), piece(stream, way, owner), send_ring.at[stream, way, step],
            recv_ring.at[stream, way, step], device_id={"dp": after if way == 0 else before},
            device_id_type=pl.DeviceIdType.MESH)
        copy.start()
        ring_sends.append(copy)
        return copy

    current = {}
    for stream in (2, 0, 1):
        for way in range(2):
            current[stream, way] = ring_send(stream, way, 0, at)
    for step in range(1, size):
        for stream in (2, 0, 1):
            for way in range(2):
                owner = ring_member(mine - step if way == 0 else mine + step, size)
                current[stream, way].wait_recv()
                if step < size - 1:
                    current[stream, way] = ring_send(stream, way, step, owner)
                if stream < 2:
                    copy = pltpu.make_async_remote_copy(
                        piece(stream, way, owner), piece(stream, way, owner), send_core.at[stream, way, step - 1],
                        recv_core.at[stream, way, step - 1], device_id=core_peer,
                        device_id_type=pl.DeviceIdType.MESH)
                    copy.start()
                    core_copies.append(copy)
        if step <= 4:
            n = step - 1
            across[n].wait_recv()
            other = chunk(n, place + 2 - 4 * micro)
            copy = pltpu.make_async_remote_copy(
                other, other, send_rows.at[n, 2], recv_rows.at[n, 2],
                device_id=core_peer, device_id_type=pl.DeviceIdType.MESH)
            copy.start()
            core_copies.append(copy)
    for copy in own:
        copy.wait()
    for copy in near + core_copies:
        copy.wait()
    for copy in across + ring_sends:
        copy.wait_send()


def gather_fused(tokens, memory, cotangent, tgt_ids, src_ids, vectors, shards):
    size = lax.axis_size("dp")
    d_model = tokens.shape[3]
    widths = [shard.shape[1] for shard in shards[:6]]
    splits = [sum(widths[:n]) for n in range(6)]
    seq = lax.axis_size("seq")
    any_spec = pl.BlockSpec(memory_space=pl.ANY)
    out_shape = [jax.ShapeDtypeStruct((seq * a.shape[2], d_model), BF16) for a in (tokens, memory, cotangent)]
    out_shape += [
        jax.ShapeDtypeStruct((seq * 8 + 8, 128), jnp.int32),
        jax.ShapeDtypeStruct((size, 32, d_model), BF16),
        jax.ShapeDtypeStruct((size * shards[0].shape[0], sum(widths)), BF16),
        jax.ShapeDtypeStruct((size * shards[6].shape[0], d_model), BF16),
    ]
    dma = pltpu.SemaphoreType.DMA
    return pl.pallas_call(
        functools.partial(gather_kernel, size, splits),
        out_shape=out_shape,
        in_specs=[pl.BlockSpec(memory_space=pltpu.VMEM)] * 16,
        out_specs=[any_spec] * 7,
        scratch_shapes=[pltpu.VMEM((3, 1, 8, 128), jnp.int32), pltpu.VMEM((32, d_model), F32), pltpu.VMEM((32, d_model), BF16),
                        dma((3, 2, size)), dma((3, 2, size)), dma((2, 2, size)), dma((2, 2, size)), dma((13,)),
                        dma((4, 3)), dma((4, 3))],
        compiler_params=pltpu.CompilerParams(collective_id=0, has_side_effects=True),
        name="gather",
    )(tokens, memory, cotangent, tgt_ids, src_ids, *vectors, *shards)


MESH = pl.DeviceIdType.MESH


SCHEDULE = "D U r0 Q r1 P a0 O r2 a01 R r3 V a0123 H E a0123 V a0123 V a0123 V a0123 V a0123 a0123"


def stream_shapes(d_model, ff, size):
    return [(d_model, d_model // size, q) for q in (ff // 4, ff // 4, 5 * d_model // 4, 3 * d_model // 4)]


def settle_kernel(size, shapes, *refs):
    n_in, n_out, count = 18, 4 + 2 * len(shapes), len(shapes)
    (x_hbm, m_hbm, w_hbm, lo_hbm, mixed_hbm, self_low_hbm, first_low_hbm, cdq_hbm, cmixed_hbm, cross_low_hbm,
     second_low_hbm, up_low_hbm, active_hbm, down_low_hbm, dq_hbm, part_hbm, dkv_hbm, dckv_hbm) = refs[:n_in]
    vec_hbm = refs[n_in]
    outs = refs[n_in + 1:n_in + 1 + n_out]
    lo_home, dt_home, dm_home, vec_out = outs[:4]
    ga, gb = outs[4:4 + count], outs[4 + count:]
    scratch = refs[n_in + 1 + n_out:]
    (xf, mf, wkv, wpair, xo, mixed, self_low, first_low, cdq, cmixed, cross_low, second_low, up_low, active,
     down_low, dq, part, dkv, dckv) = scratch[:19]
    (tz, tz_low, tz_got, mz, mz_low, mz_got, lo_buf, vec_run, vec_got) = scratch[19:28]
    rest = scratch[28:]
    acc, stage, other, ring_out, ring_in, fin = (rest[n * count:(n + 1) * count] for n in range(6))
    (load_sems, store_sems, ring_ss, ring_rs, core_ss, core_rs, fin_ss, fin_rs, row_ss, row_rs, vec_ss, vec_rs,
     lo_ss, lo_rs) = rest[6 * count:]

    at, place = lax.axis_index("dp"), lax.axis_index("seq")
    micro, core = lax.div(place, 2), lax.rem(place, 2)
    after, before = ring_neighbours(at, size)
    mine = ring_place(at, size)
    core_peer = {"seq": place + 1 - 2 * core}
    chip_peer = {"seq": place + 2 - 4 * micro}
    levels = size.bit_length() - 1
    flips = [{"dp": at + (1 << n) * (1 - 2 * lax.rem(lax.div(at, 1 << n), 2))} for n in range(levels)]
    vec_peers = [core_peer, chip_peer] + flips
    d_model = xf.shape[1]
    half = d_model // 2
    t_len, s_len = xf.shape[0], mf.shape[0]

    barrier = pltpu.get_barrier_semaphore()
    greeted = [{"dp": after}, {"dp": before}, core_peer, chip_peer] + flips
    for peer in greeted:
        pl.semaphore_signal(barrier, inc=1, device_id=peer, device_id_type=MESH)

    loads = {}

    def load(name, src, dst):
        copy = pltpu.make_async_copy(src, dst, load_sems.at[len(loads)])
        copy.start()
        loads[name] = copy

    def load_first():
        load("active", active_hbm, active)
        load("down_low", down_low_hbm, down_low)
        load("vec", vec_hbm.at[pl.ds(0, 24)], vec_run.at[0])

    def load_up():
        load("second_low", second_low_hbm, second_low)
        load("up_low", up_low_hbm, up_low)

    def load_qkv():
        load("dkv", dkv_hbm, dkv)
        load("xf", x_hbm, xf)
        for n in range(t_len // (2 * RB)):
            load(("xo", n), x_hbm.at[pl.ds((2 * n + core) * RB, RB)], xo.at[pl.ds(n * RB, RB)])
        load("dq", dq_hbm, dq)

    def load_rest():
        load("dckv", dckv_hbm, dckv)
        load("mf", m_hbm, mf)
        for name, src, dst in (("mixed", mixed_hbm, mixed), ("self_low", self_low_hbm, self_low),
                               ("first_low", first_low_hbm, first_low), ("cdq", cdq_hbm, cdq),
                               ("cmixed", cmixed_hbm, cmixed), ("cross_low", cross_low_hbm, cross_low)):
            load(name, src, dst)
        load("wkv", w_hbm.at[:, pl.ds(d_model, 2 * d_model)], wkv)
        load("part", part_hbm, part)
        load("wpair", w_hbm.at[:, pl.ds(5 * d_model, 2 * d_model)], wpair)

    load_first()
    load_up()

    pending = []

    def send(src, dst, send_sem, recv_sem, peer):
        copy = pltpu.make_async_remote_copy(src, dst, send_sem, recv_sem, device_id=peer, device_id_type=MESH)
        copy.start()
        pending.append(copy)
        return copy

    stores = []

    def store(src, dst):
        copy = pltpu.make_async_copy(src, dst, store_sems.at[len(stores)])
        copy.start()
        stores.append(copy)

    pl.semaphore_wait(barrier, len(greeted))

    piece = t_len // 12
    keep, give = [], []

    def pieces_of(index0, slot0, index1, slot1):
        index, slot = jnp.where(core == 0, index0, index1), jnp.where(core == 0, slot0, slot1)
        source = lo_hbm.at[pl.ds(pl.multiple_of(index * piece, 128), piece)]
        return source, lo_buf.at[lax.div(slot, 3), pl.ds(pl.multiple_of(lax.rem(slot, 3) * piece, 128), piece)]

    for n, row in enumerate(((0, 0, 1, 0), (1, 1, 4, 4), (4, 5, 5, 5))):
        copy = pltpu.make_async_copy(*pieces_of(*row), lo_ss.at[n])
        copy.start()
        keep.append(copy)
    for n, row in enumerate(((2, 1, 0, 2), (3, 2, 2, 3), (5, 3, 3, 4))):
        source, target = pieces_of(*row)
        give.append(send(source, target, lo_ss.at[3 + n], lo_rs.at[n], core_peer))

    vec_state = {"level": 0, "copy": None}

    def vec_send():
        level = vec_state["level"]
        vec_state["copy"] = send(vec_run.at[level], vec_got.at[level], vec_ss.at[level], vec_rs.at[level],
                                 vec_peers[level])

    def vec_step():
        level = vec_state["level"]
        vec_state["copy"].wait_recv()
        vec_run[level + 1] = vec_run[level] + vec_got[level]
        vec_state["level"] = level + 1
        if level + 1 < len(vec_peers):
            vec_send()
        else:
            store(vec_run.at[level + 1], vec_out)

    loads["vec"].wait()
    vec_send()

    row_waits = []

    def home_rows(n, rows_of, home):
        store(rows_of(micro), home.at[micro])
        row_waits.append(send(rows_of(1 - micro), home.at[micro], row_ss.at[n], row_rs.at[n], chip_peer))

    def split(values, pieces, s, rows, base=0):
        width = values.shape[1] // pieces
        quarter = width // 4
        for p in range(pieces):
            lower = values[:, p * width:p * width + 2 * quarter]
            upper = values[:, p * width + 2 * quarter:(p + 1) * width]
            own = jnp.where(core == 0, lower, upper)
            away = jnp.where(core == 0, upper, lower).astype(BF16)
            cols = slice(base + p * quarter, base + (p + 1) * quarter)
            for way in range(2):
                acc[s][way, rows, cols] = own[:, way * quarter:(way + 1) * quarter]
                stage[s][way, rows, cols] = away[:, way * quarter:(way + 1) * quarter]

    core_waits = {}
    tile = 256

    def await_loads(*names):
        for name in names:
            loads[name].wait()

    def each_tile(body):
        def one(m, carry):
            body(pl.ds(pl.multiple_of(m * tile, tile), tile))
            return carry

        lax.fori_loop(0, d_model // tile, one, 0)

    def share(s):
        core_waits[s] = send(stage[s], other[s], core_ss.at[s], core_rs.at[s], core_peer)

    def compute_down():
        await_loads("active", "down_low")
        load_qkv()
        block, tall = shapes[0][1], active.shape[1] // size
        quarter = d_model // 4

        def one(m, carry):
            values = mm_tn(active[:, pl.ds(pl.multiple_of(m * tall, tall), tall)], down_low[...])
            rows = pl.ds(pl.multiple_of(m * block, block), block)
            for n in range(tall // block):
                split(values[n * block:(n + 1) * block], 1, 0, rows, n * quarter)
            return carry

        lax.fori_loop(0, size, one, 0)
        share(0)

    def compute_up():
        await_loads("second_low", "up_low")
        load_rest()
        each_tile(lambda rows: split(mm_tn(second_low[:, rows], up_low[...]), 1, 1, rows))
        share(1)

    def compute_qkv():
        await_loads("dkv", "xf", "dq", *(("xo", n) for n in range(t_len // (2 * RB))))

        def one(rows):
            split(mm_tn(xo[:, rows], dq[...]), 1, 2, rows)
            whole = xf[:, rows]
            for n in range(2):
                parts = [mm_tn(whole, dkv[2 * n + m]) for m in range(2)]
                split(jnp.concatenate(parts, axis=1), 1, 2, rows, (1 + n) * d_model // 4)

        each_tile(one)

    def compute_pair():
        await_loads("dckv", "mf")

        def one(rows):
            whole = mf[:, rows]
            for n in range(2):
                parts = [mm_tn(whole, dckv[2 * n + m]) for m in range(2)]
                split(jnp.concatenate(parts, axis=1), 1, 2, rows, (3 + n) * d_model // 4)

        each_tile(one)
        share(2)

    def compute_outs():
        await_loads("mixed", "self_low", "first_low", "cdq", "cmixed", "cross_low")

        def one(rows):
            for n, (left, right) in enumerate(((mixed, self_low), (first_low, cdq), (cmixed, cross_low))):
                split(mm_tn(left[:, rows], right[...]), 1, 3, rows, n * d_model // 4)

        each_tile(one)
        share(3)

    ring_waits = {}

    def ring(s, step):
        block = shapes[s][1]
        if step == 0:
            core_waits[s].wait_recv()
        for way in range(2):
            owner = ring_member(mine - 1 - step if way == 0 else mine + 1 + step, size)
            rows = pl.ds(pl.multiple_of(owner * block, block), block)
            total = acc[s][way, rows, :] + other[s][way, rows, :].astype(F32)
            if step > 0:
                ring_waits[s, way].wait_recv()
                total = total + ring_in[s][way, step - 1].astype(F32)
            if step < size - 1:
                ring_out[s][way, step] = total.astype(BF16)
                ring_waits[s, way] = send(
                    ring_out[s].at[way, step], ring_in[s].at[way, step], ring_ss.at[s, way, step],
                    ring_rs.at[s, way, step], {"dp": after if way == 0 else before})
            else:
                fin[s][way] = total.astype(BF16)

    chip_waits, tail = {}, []

    def finish(s):
        store(fin[s], ga[s].at[core])
        chip_waits[s] = send(fin[s], gb[s].at[core], fin_ss.at[s, 0], fin_rs.at[s, 0], chip_peer)
        tail.append(send(fin[s], ga[s].at[core], fin_ss.at[s, 1], fin_rs.at[s, 1], core_peer))

    def forward(s):
        chip_waits[s].wait_recv()
        tail.append(send(gb[s].at[core], gb[s].at[core], fin_ss.at[s, 2], fin_rs.at[s, 2], core_peer))

    def row_products():
        await_loads("wkv", "part", "wpair")

        def tokens(b, carry):
            rows = pl.ds(pl.multiple_of(b * RB, RB), RB)
            total = None
            for n in range(4):
                product = mm_nt(dkv[n, rows, :], wkv[:, n * 256:(n + 1) * 256])
                total = product if total is None else total + product
            own = part[pl.ds(pl.multiple_of(lax.div(b, 2) * RB, RB), RB), :]
            total = total + jnp.where(lax.rem(b, 2) == core, own, jnp.zeros_like(own))
            tz[rows, :] = total
            tz_low[rows, :] = total.astype(BF16)
            return carry

        lax.fori_loop(0, t_len // RB, tokens, 0)

        def memories(b, carry):
            rows = pl.ds(pl.multiple_of(b * RB, RB), RB)
            total = None
            for n in range(4):
                product = mm_nt(dckv[n, rows, :], wpair[:, n * 256:(n + 1) * 256])
                total = product if total is None else total + product
            mz[rows, :] = total
            mz_low[rows, :] = total.astype(BF16)
            return carry

        lax.fori_loop(0, s_len // RB, memories, 0)
        copies = []
        for n, (low, got, length) in enumerate(((tz_low, tz_got, t_len // 4), (mz_low, mz_got, s_len // 4))):
            for k in range(2):
                start = pl.multiple_of((1 - core + 2 * k) * length, 128)
                copies.append(send(low.at[pl.ds(start, length)], got.at[k], row_ss.at[3 + 2 * n + k],
                                   row_rs.at[3 + 2 * n + k], core_peer))
        return copies

    def row_finish(copies):
        for copy in copies:
            copy.wait_recv()
        for n, (full, got, done, length, home) in enumerate((
                (tz, tz_got, tz_low, t_len // 4, dt_home), (mz, mz_got, mz_low, s_len // 4, dm_home))):

            def rows_at(k, length=length):
                return pl.ds(pl.multiple_of((core + 2 * k) * length, 128), length)

            for k in range(2):
                done[rows_at(k), :] = (full[rows_at(k), :] + got[k].astype(F32)).astype(BF16)
            home_rows(1 + n, lambda k, done=done, rows_at=rows_at: done.at[rows_at(k)], home)

    reached = [0] * count
    sent_home = []

    def advance(s):
        if reached[s] < size - 1:
            reached[s] += 1
            ring(s, reached[s])
            if reached[s] == size - 1:
                finish(s)
                sent_home.append(s)

    def rows_start():
        state["rows"] = row_products()

    def rows_end():
        row_finish(state["rows"])

    def layer_rows():
        for copy in keep:
            copy.wait()
        for copy in give:
            copy.wait_recv()
        home_rows(0, lambda k: lo_buf.at[k], lo_home)

    def vectors():
        if vec_state["level"] < len(vec_peers):
            vec_step()

    state = {}
    actions = {"D": compute_down, "U": compute_up, "Q": compute_qkv, "P": compute_pair, "O": compute_outs,
               "R": rows_start, "E": rows_end, "H": layer_rows, "V": vectors}
    for action in SCHEDULE.split():
        if action in actions:
            actions[action]()
        elif action[0] == "r":
            ring(int(action[1]), 0)
        else:
            for s in action[1:]:
                advance(int(s))
    for s in range(count):
        forward(s)
    for copy in row_waits + tail:
        copy.wait_recv()
    for copy in pending:
        copy.wait_send()
    for copy in stores:
        copy.wait()


def settle_fused(x_full, m_full, w_all, results):
    size = lax.axis_size("dp")
    (layer_rows, mixed, self_low, first_low, cdq, cmixed, cross_low, second_low, up_low, active, down_low, dq,
     part, dkv, dckv, vec_sums) = results
    t_len, d_model = x_full.shape
    s_len, ff, own = m_full.shape[0], up_low.shape[1], dq.shape[0]
    shapes = stream_shapes(d_model, ff, size)
    any_spec = pl.BlockSpec(memory_space=pl.ANY)
    out_shape = [
        jax.ShapeDtypeStruct((2, t_len // 4, d_model), BF16),
        jax.ShapeDtypeStruct((2, t_len // 4, d_model), BF16),
        jax.ShapeDtypeStruct((2, s_len // 4, d_model), BF16),
        jax.ShapeDtypeStruct((24, d_model), F32),
    ]
    out_shape += [jax.ShapeDtypeStruct((2, 2, block, q), BF16) for _, block, q in shapes] * 2
    bf = lambda *shape: pltpu.VMEM(shape, BF16)
    fl = lambda *shape: pltpu.VMEM(shape, F32)
    dma = pltpu.SemaphoreType.DMA
    levels = 2 + size.bit_length() - 1
    count = len(shapes)
    scratch = [bf(t_len, d_model), bf(s_len, d_model), bf(d_model, 2 * d_model), bf(d_model, 2 * d_model)]
    scratch += [bf(own, d_model)] * 8 + [bf(own, ff)] * 2 + [bf(own, d_model)] * 2 + [
        fl(own, d_model), bf(4, t_len, 256), bf(4, s_len, 256),
        fl(t_len, d_model), bf(t_len, d_model), bf(2, t_len // 4, d_model),
        fl(s_len, d_model), bf(s_len, d_model), bf(2, s_len // 4, d_model),
        bf(2, t_len // 4, d_model), fl(levels + 1, 24, d_model), fl(levels, 24, d_model),
    ]
    scratch += [fl(2, rows, q) for rows, _, q in shapes]
    scratch += [bf(2, rows, q) for rows, _, q in shapes] * 2
    scratch += [bf(2, size - 1, block, q) for _, block, q in shapes] * 2
    scratch += [bf(2, block, q) for _, block, q in shapes]
    scratch += [dma((24,)), dma((16,)), dma((count, 2, size)), dma((count, 2, size)), dma((count,)), dma((count,)),
                dma((count, 3)), dma((count, 3)), dma((7,)), dma((7,)), dma((levels,)), dma((levels,)), dma((6,)),
                dma((3,))]
    return pl.pallas_call(
        functools.partial(settle_kernel, size, shapes),
        out_shape=out_shape,
        in_specs=[any_spec] * 19,
        out_specs=[any_spec] * len(out_shape),
        scratch_shapes=scratch,
        compiler_params=pltpu.CompilerParams(
            collective_id=1, has_side_effects=True, vmem_limit_bytes=64 * 1024 * 1024 - 512 * 1024),
        name="settle",
    )(x_full, m_full, w_all, layer_rows, mixed, self_low, first_low, cdq, cmixed, cross_low, second_low, up_low,
      active, down_low, dq, part, dkv, dckv, vec_sums)


def finish_kernel(factor, lo, dt, dm, vec, *refs):
    ga, gb = refs[:4], refs[4:8]
    lo_out, dt_out, dm_out, qkv, out, cq, pair, cout, up, down, bias, up_bias, gain, shift = refs[8:]
    lo_out[:, 0] = lo[...]
    dt_out[:, 0] = dt[...]
    dm_out[:, 0] = dm[...]
    firsts = ((qkv, 0), (qkv, 1), (qkv, 2), (pair, 0), (pair, 1))
    others = ((out, 0), (cq, 0), (cout, 0))
    for half in range(2):
        for way in range(2):
            totals = [(a[half, way].astype(F32) + b[half, way].astype(F32)) * factor for a, b in zip(ga, gb)]
            block, width = totals[0].shape[0], totals[3].shape[1] // len(others)
            quarter = (2 * half + way) * width
            for n in range(totals[0].shape[1] // width):
                down[n * block:(n + 1) * block, quarter:quarter + width] = totals[0][:, n * width:(n + 1) * width]
            wide = totals[1].shape[1]
            up[:, (2 * half + way) * wide:(2 * half + way + 1) * wide] = totals[1]
            for total, places in ((totals[2], firsts), (totals[3], others)):
                for n, (ref, slot) in enumerate(places):
                    column = slot * 4 * width + quarter
                    ref[:, column:column + width] = total[:, n * width:(n + 1) * width]
    at = lax.axis_index("dp")
    d_model, width = vec.shape[1], bias.shape[1]
    sums = vec[...] * factor
    own = pltpu.roll(sums, lax.rem(d_model - at * width, d_model), 1)[:, :width]
    bias[...] = own[0:7]
    gain[...] = own[11:14]
    shift[...] = own[14:17]
    start = at * 4 * width
    rows = lax.broadcasted_iota(jnp.int32, (4, d_model), 0)
    row = jnp.sum(jnp.where(rows == lax.div(start, d_model), sums[7:11], 0.0), axis=0, keepdims=True)
    row = jnp.broadcast_to(row, (8, d_model))
    up_bias[...] = pltpu.roll(row, lax.rem(d_model - lax.rem(start, d_model), d_model), 1)[0:1, :4 * width]


def finish_fused(settled, factor, d_model, ff):
    lo, dt, dm = settled[:3]
    size = lax.axis_size("dp")
    block = d_model // size
    shapes = [jax.ShapeDtypeStruct((2, 1, *a.shape[1:]), BF16) for a in (lo, dt, dm)]
    shapes += [jax.ShapeDtypeStruct((block, n * d_model), F32) for n in (3, 1, 1, 2, 1)]
    shapes += [jax.ShapeDtypeStruct((block, ff), F32), jax.ShapeDtypeStruct((ff // size, d_model), F32)]
    shapes += [jax.ShapeDtypeStruct(s, F32) for s in ((7, block), (1, ff // size), (3, block), (3, block))]

    def whole(a):
        return pl.BlockSpec(a.shape, lambda i: (0,) * len(a.shape))

    done = pl.pallas_call(
        functools.partial(finish_kernel, factor),
        grid=(1,),
        out_shape=shapes,
        in_specs=[whole(a) for a in settled],
        out_specs=[whole(s) for s in shapes],
        compiler_params=pltpu.CompilerParams(vmem_limit_bytes=63 * 1024 * 1024),
        name="finish",
    )(*settled)
    return (*done[:11], done[11][0], *done[12:])


def pack_vectors(proj_bias, up_bias, norm_gain, norm_bias, d_model):
    size, at = lax.axis_size("dp"), lax.axis_index("dp")
    width = d_model // size
    rows = jnp.concatenate([proj_bias, jnp.zeros((4, width), BF16), norm_gain, norm_bias], axis=0)
    packed = lax.dynamic_update_slice(jnp.zeros((32, d_model), BF16), rows, (0, at * width))
    flat = lax.dynamic_update_slice(jnp.zeros((4 * d_model,), BF16), up_bias, (at * up_bias.shape[0],))
    return lax.dynamic_update_slice(packed, flat.reshape(4, d_model), (7, 0))


def unpack_vectors(sums, d_model):
    size, at = lax.axis_size("dp"), lax.axis_index("dp")
    width = d_model // size
    own = lax.dynamic_slice(sums, (0, at * width), (32, width))
    up = lax.dynamic_slice(sums[7:11].reshape(-1), (at * 4 * width,), (4 * width,))
    return own[:7], up, own[11:14], own[14:17]


def gather_plain(tokens, memory, cotangent, counts, packed, shards):
    micro = lax.axis_index("seq") // MB

    def whole(rows):
        return lax.all_gather(lax.squeeze(rows, (1,)), "seq", axis=1, tiled=True)[micro]

    weights = [lax.all_gather(shard, "dp", axis=0, tiled=True) for shard in shards]
    vec_all = lax.psum(packed, "dp")[None]
    counts = jnp.pad(lax.psum(counts, "seq")[micro][None], ((0, 31), (0, 0)))
    place = jnp.full((8, 128), lax.axis_index("seq") % MB, jnp.int32)
    counts = jnp.concatenate([counts, place], axis=0)
    w_all = jnp.concatenate(weights[:6], axis=1)
    return whole(tokens), whole(memory), whole(cotangent), counts, vec_all, w_all, weights[6]


def own_rows(rows, core):
    blocks = rows.reshape(rows.shape[0] // (2 * RB), 2, RB, rows.shape[1])
    return blocks[:, core].reshape(rows.shape[0] // 2, rows.shape[1])


def spread_rows(rows, core):
    blocks = rows.reshape(rows.shape[0] // RB, 1, RB, rows.shape[1])
    blocks = jnp.concatenate([blocks, jnp.zeros_like(blocks)], axis=1)
    blocks = jnp.where(core == 0, blocks, blocks[:, ::-1])
    return blocks.reshape(rows.shape[0] * 2, rows.shape[1])


def settle_plain(x_full, m_full, w_all, results, factor):
    (layer_rows, mixed, self_low, first_low, cdq, cmixed, cross_low, second_low, up_low, active, down_low, dq,
     part, dkv, dckv, vec_sums) = results
    place = lax.axis_index("seq")
    micro, core = place // MB, place % MB
    d_model = x_full.shape[1]
    dkv = jnp.moveaxis(dkv, 0, 1).reshape(x_full.shape[0], 2 * d_model)
    dckv = jnp.moveaxis(dckv, 0, 1).reshape(m_full.shape[0], 2 * d_model)
    input_rows = spread_rows(part, core) + mm_nt(dkv, w_all[:, d_model:3 * d_model])
    memory_rows = mm_nt(dckv, w_all[:, 5 * d_model:7 * d_model])

    def home(rows):
        both = jnp.stack([rows, jnp.zeros_like(rows)])
        both = jnp.where(micro == 0, both, both[::-1])
        return lax.psum_scatter(both, "seq", scatter_dimension=1, tiled=True).astype(BF16)[:, None]

    grads = [
        jnp.concatenate([mm_tn(own_rows(x_full, core), dq), mm_tn(x_full, dkv)], axis=1),
        mm_tn(mixed, self_low), mm_tn(first_low, cdq), mm_tn(m_full, dckv), mm_tn(cmixed, cross_low),
        mm_tn(second_low, up_low), mm_tn(active, down_low),
    ]
    grads = [
        lax.psum(lax.psum_scatter(grad, "dp", scatter_dimension=0, tiled=True), "seq") * factor for grad in grads
    ]
    vec_sums = lax.psum(vec_sums, ("dp", "seq")) * factor
    return (home(spread_rows(layer_rows.astype(F32), core)), home(input_rows), home(memory_rows), *grads,
            *unpack_vectors(vec_sums, d_model))


def per_device(
    tokens, memory, cotangent, tgt_segments, src_segments,
    self_qkv, self_out, cross_q, cross_kv, cross_out, ffn_up, ffn_down, proj_bias, up_bias, norm_gain, norm_bias,
):
    d_model = tokens.shape[3]
    shards = (self_qkv, self_out, cross_q, cross_kv, cross_out, ffn_up, ffn_down)
    size, rows, ff = lax.axis_size("dp"), self_qkv.shape[0], ffn_up.shape[1]
    fused = rows % 64 == 0 and size & (size - 1) == 0 and size > 2
    factor = 1.0 / math.sqrt(MB * size * tokens.shape[2] * lax.axis_size("seq"))
    if fused:
        vectors = (proj_bias, up_bias[None], norm_gain, norm_bias)
        x_full, m_full, ct_full, counts, vec_all, w_all, w_down = gather_fused(
            tokens, memory, cotangent, tgt_segments, src_segments, vectors, shards)
    else:
        docs = jnp.arange(1, 9)
        tgt_counts = jnp.sum(tgt_segments[:, 0, :, None] < docs, axis=1, dtype=jnp.int32)
        src_counts = jnp.sum(src_segments[:, 0, :, None] < docs, axis=1, dtype=jnp.int32)
        counts = jnp.pad(jnp.concatenate([tgt_counts, src_counts], axis=1), ((0, 0), (1, 111)))
        packed = pack_vectors(proj_bias, up_bias, norm_gain, norm_bias, d_model)
        x_full, m_full, ct_full, counts, vec_all, w_all, w_down = gather_plain(
            tokens, memory, cotangent, counts, packed, shards)
    results = run_layer(counts, x_full, m_full, ct_full, vec_all, w_all, w_down)
    if fused:
        return finish_fused(settle_fused(x_full, m_full, w_all, results), factor, d_model, ff)
    return settle_plain(x_full, m_full, w_all, results, factor)


def solution(mesh):
    rows = P(None, "dp", "seq", None)
    ids = P(None, "dp", "seq")
    sharded = P("dp", None)
    columns = P(None, "dp")
    return jax.shard_map(
        per_device,
        mesh=mesh,
        in_specs=(rows, rows, rows, ids, ids) + (sharded,) * 7 + (columns, P("dp"), columns, columns),
        out_specs=(rows, rows, rows) + (sharded,) * 7 + (columns, P("dp"), columns, columns),
        check_vma=False,
    )
```

```python
import functools
import math

import jax
import jax.numpy as jnp
from jax import lax
from jax.experimental import pallas as pl
from jax.experimental.pallas import tpu as pltpu
from jax.sharding import PartitionSpec as P

H = 8
MB = 2
RB = 256
KB = 256
F32 = jnp.float32
BF16 = jnp.bfloat16


def mm(left, right):
    return jnp.dot(left, right, preferred_element_type=F32)


def mm_nt(left, right):
    return lax.dot_general(left, right, (((1,), (1,)), ((), ())), preferred_element_type=F32)


def mm_tn(left, right):
    return lax.dot_general(left, right, (((0,), (0,)), ((), ())), preferred_element_type=F32)


def gelu_parts(values):
    cumulative = 0.5 * (1.0 + lax.erf(values * 0.7071067811865476))
    density = jnp.exp(-0.5 * values * values) * 0.3989422804014327
    return values * cumulative, cumulative + values * density


def normalize(summed, gain, shift):
    center = summed - jnp.mean(summed, axis=-1, keepdims=True)
    scale_inv = lax.rsqrt(jnp.mean(center * center, axis=-1, keepdims=True) + 1e-05)
    unit_rows = center * scale_inv
    return unit_rows * gain + shift, unit_rows, scale_inv


def normalize_back(unit_rows, scale_inv, gain, grad_rows):
    scaled = grad_rows * gain
    return scale_inv * (
        scaled
        - jnp.mean(scaled, axis=-1, keepdims=True)
        - unit_rows * jnp.mean(scaled * unit_rows, axis=-1, keepdims=True)
    )


def fold(values, op):
    rows, cols = values.shape
    return op(values.reshape(rows // 8, 8, cols), axis=0)


def layer_kernel(
    counts,
    x_hbm, m_hbm, x_ref, ct_ref, vec_all, w_hbm, wdown_hbm,
    layer_out, mixed_out, self_low_out, first_low_out, cdq_out, cmixed_out, cross_low_out,
    second_low_out, up_low_out, active_out, down_low_out, dq_out, part_out,
    dkv_hbm, dckv_hbm, vecg_out,
    wqkv, wout, wcq, wckv, wcout, wup, wdown,
    k_s, kt_s, v_s, vt_s, k_c, kt_c, v_c, vt_c,
    p_s, p_c, dk_s, dv_s, dk_c, dv_c,
    qm_s, qm_c, gtm, gm, ot_s, ot_c, dqt, slope_s, vec_ref, kn_s, kn_c, sems,
):
    step = pl.program_id(0)
    steps = pl.num_programs(0)
    t_len, d_model = k_s.shape
    s_len = k_c.shape[0]
    ff = wup.shape[1]
    hd = d_model // H
    core = counts[32, 0]
    tgt_starts = [0] + [counts[0, d] + counts[8, d] + counts[16, d] + counts[24, d] for d in range(1, 9)]
    src_starts = [0] + [counts[0, d] + counts[8, d] + counts[16, d] + counts[24, d] for d in range(9, 17)]
    block = 2 * step + core

    def columns(start, count):
        return w_hbm.at[:, pl.ds(start * d_model, count * d_model)]

    loads = [
        pltpu.make_async_copy(src, dst, sems.at[n])
        for n, (src, dst) in enumerate((
            (columns(0, 3), wqkv), (x_hbm.at[:, pl.ds(0, 256)], p_s.at[0]), (x_hbm.at[:, pl.ds(256, 256)], p_s.at[1]),
            (columns(5, 2), wckv), (m_hbm.at[:, pl.ds(0, 256)], p_c.at[0]), (m_hbm.at[:, pl.ds(256, 256)], p_c.at[1]),
            (columns(3, 1), wout), (columns(4, 1), wcq), (columns(7, 1), wcout), (columns(8, ff // d_model), wup),
            (wdown_hbm, wdown),
        ))
    ]

    @pl.when(step == 0)
    def _():
        for load in loads[:6]:
            load.start()
        dk_s[...] = jnp.zeros_like(dk_s)
        dv_s[...] = jnp.zeros_like(dv_s)
        dk_c[...] = jnp.zeros_like(dk_c)
        dv_c[...] = jnp.zeros_like(dv_c)
        vecg_out[...] = jnp.zeros_like(vecg_out)
        parts = vec_all[...].astype(F32)
        if parts.shape[0] == 1:
            vec_ref[...] = parts[0]
        else:
            vec_ref[...] = jnp.zeros_like(vec_ref)
            width = d_model // parts.shape[0]
            for n in range(parts.shape[0]):
                cols = slice(n * width, (n + 1) * width)
                vec_ref[0:7, cols] = parts[n, 0:7, :width]
                vec_ref[11:17, cols] = parts[n, 7:13, :width]
                for m in range(4 * width // 128):
                    start = n * 4 * width + m * 128
                    row, column = 7 + start // d_model, start % d_model
                    vec_ref[row:row + 1, column:column + 128] = parts[n, 13 + m:14 + m, :]
        vec = vec_ref[...]
        vec_t = vec.T

        def project(rows_ref, w_ref, k_at, kt, k, vt, v, norms, bias_row, bias_row_t, count):
            norms[...] = jnp.zeros_like(norms)
            wk = w_ref[:, k_at:k_at + d_model]
            wv = w_ref[:, k_at + d_model:k_at + 2 * d_model]
            wk_t = wk.T
            wv_t = wv.T

            def one(r, carry):
                at = pl.ds(pl.multiple_of(r * 512, 512), 512)
                rows = jnp.concatenate([rows_ref[0, at, :], rows_ref[1, at, :]], axis=1)
                k[at, :] = mm(rows, wk).astype(BF16)
                v[at, :] = (mm(rows, wv) + bias_row).astype(BF16)
                keys_t = mm_nt(wk_t, rows)
                kt[:, at] = keys_t.astype(BF16)
                squares = keys_t * keys_t
                for h in range(H):
                    own = jnp.sum(fold(squares[h * hd:(h + 1) * hd], jnp.sum), axis=0, keepdims=True)
                    norms[h:h + 1, :] = jnp.maximum(norms[h:h + 1, :], jnp.maximum(own[:, :RB], own[:, RB:]))
                vt[:, at] = (mm_nt(wv_t, rows) + bias_row_t).astype(BF16)
                return carry

            lax.fori_loop(0, count // 512, one, 0)

        for load in loads[:3]:
            load.wait()
        for load in loads[6:]:
            load.start()
        project(p_s, wqkv, d_model, kt_s, k_s, vt_s, v_s, kn_s, vec[1:2], vec_t[:, 1:2], t_len)
        for load in loads[3:6]:
            load.wait()
        project(p_c, wckv, 0, kt_c, k_c, vt_c, v_c, kn_c, vec[4:5], vec_t[:, 4:5], s_len)
        for load in loads[6:]:
            load.wait()

    vec = vec_ref[...]

    qpos = block * RB + lax.broadcasted_iota(jnp.int32, (1, RB), 1)
    lo_s = jnp.zeros((1, RB), jnp.int32)
    hi_s = jnp.full((1, RB), tgt_starts[1], jnp.int32)
    lo_c = jnp.zeros((1, RB), jnp.int32)
    hi_c = jnp.full((1, RB), src_starts[1], jnp.int32)
    for doc in range(1, 8):
        inside = qpos >= tgt_starts[doc]
        lo_s = jnp.where(inside, tgt_starts[doc], lo_s)
        hi_s = jnp.where(inside, tgt_starts[doc + 1], hi_s)
        lo_c = jnp.where(inside, src_starts[doc], lo_c)
        hi_c = jnp.where(inside, src_starts[doc + 1], hi_c)
    first = block * RB
    last = first + RB - 1
    s_from, s_to, c_from, c_to = 0, tgt_starts[1], 0, src_starts[1]
    for doc in range(1, 8):
        in_first = first >= tgt_starts[doc]
        in_last = last >= tgt_starts[doc]
        s_from = jnp.where(in_first, tgt_starts[doc], s_from)
        c_from = jnp.where(in_first, src_starts[doc], c_from)
        s_to = jnp.where(in_last, tgt_starts[doc + 1], s_to)
        c_to = jnp.where(in_last, src_starts[doc + 1], c_to)

    def block_range(start, stop, length):
        base = lax.div(start, 128) * 128
        count = lax.div(stop - base + (KB - 1), KB)
        return jnp.minimum(base, length - count * KB), count

    def halves(values, axis, h):
        place = lax.broadcasted_iota(jnp.int32, values.shape, axis)
        return jnp.where(place >= hd if h % 2 else place < hd, values, jnp.zeros_like(values))

    def put_masked(rows, rows_t, natural, transposed):
        for h in range(H):
            pair = slice((h // 2) * 2 * hd, (h // 2) * 2 * hd + 2 * hd)
            natural[h] = halves(rows[:, pair], 1, h)
            transposed[h] = halves(rows_t[pair, :], 0, h)

    def key_rows(base, j, rows=KB):
        return pl.ds(pl.multiple_of(base + j * rows, 128), rows)

    def twice(count, base, body, carry):
        pairs = lax.div(count, 2)
        carry = lax.fori_loop(0, pairs, lambda j, c: body(base, j, c, 2 * KB, H // 2), carry)
        rest = base + pairs * 2 * KB
        return lax.fori_loop(0, count - 2 * pairs, lambda j, c: body(rest, j, c, KB, H), carry)

    def attend(query_t, qtm, k, vt, p, ot, norms, lo, hi, start, stop):
        base, count = block_range(start, stop, k.shape[0])
        squares = query_t.astype(F32)
        squares = squares * squares
        bound = None
        for h in range(H):
            own = jnp.sum(fold(squares[h * hd:(h + 1) * hd], jnp.sum), axis=0, keepdims=True)
            own = own * jnp.max(norms[h:h + 1, :], axis=1, keepdims=True)
            bound = own if bound is None else jnp.maximum(bound, own)
        small = jnp.max(bound) <= 3600.0
        shifts = jnp.where(small, 0, count)

        def bias_of(j, rows=KB, start=base):
            kpos = start + j * rows + lax.broadcasted_iota(jnp.int32, (rows, RB), 0)
            return jnp.where((kpos >= lo) & (kpos < hi), 0.0, -1e30).astype(F32)

        def scores(h, at, bias):
            pair = slice((h // 2) * 2 * hd, (h // 2) * 2 * hd + 2 * hd)
            return mm(k[at, pair], qtm[h]) + bias

        def top(j, highest):
            at = key_rows(base, j)
            bias = bias_of(j)
            return tuple(jnp.maximum(highest[h], fold(scores(h, at, bias), jnp.max)) for h in range(H))

        lowest = jnp.full((8, RB), jnp.where(small, 0.0, -1e30), F32)
        highest = lax.fori_loop(0, shifts, top, (lowest,) * H)
        highest = [jnp.max(part, axis=0, keepdims=True) for part in highest]
        ot[...] = jnp.zeros_like(ot)

        def gather(start, j, totals, rows, group):
            at = key_rows(start, j, rows)
            bias = bias_of(j, rows, start)
            out = []
            for first_head in range(0, H, group):
                heads = range(first_head, first_head + group)
                found = [scores(h, at, bias) for h in heads]
                lows = []
                for h in heads:
                    weights = jnp.exp(found[h - first_head] - highest[h])
                    low = weights.astype(BF16)
                    lows.append(low)
                    p[h, at, :] = low
                    out.append(totals[h] + fold(weights, jnp.sum))
                for h in heads:
                    head = slice(h * hd, (h + 1) * hd)
                    ot[head, :] += mm(vt[head, at], lows[h - first_head])
            return tuple(out)

        totals = twice(count, base, gather, (jnp.zeros((8, RB), F32),) * H)
        inverse = []
        for h in range(H):
            inv = 1.0 / jnp.sum(totals[h], axis=0, keepdims=True)
            head = slice(h * hd, (h + 1) * hd)
            ot[head, :] = ot[head, :] * inv
            inverse.append(inv)
        return inverse

    def attend_back(grad_rows, inverse, qm, k, kt, v, p, ot, dk, dv, start, stop):
        base, count = block_range(start, stop, k.shape[0])
        grad_t = grad_rows.T.astype(F32)
        scaled_t = []
        spread = []
        for h in range(H):
            head = slice(h * hd, (h + 1) * hd)
            low_t = (grad_t[head] * inverse[h]).astype(BF16)
            scaled_t.append(low_t)
            spread.append(jnp.sum(ot[head, :] * low_t.astype(F32), axis=0, keepdims=True))
        scaled_t = jnp.concatenate(scaled_t, axis=0)
        put_masked(scaled_t.T, scaled_t, gm, gtm)
        dqt[...] = jnp.zeros_like(dqt)

        def body(start, j, carry, rows, group):
            at = key_rows(start, j, rows)
            pairs = [slice((h // 2) * 2 * hd, (h // 2 + 1) * 2 * hd) for h in range(H)]
            for first_head in range(0, H, group):
                heads = range(first_head, first_head + group)
                prob_grads = [mm(v[at, pairs[h]], gtm[h]) for h in heads]
                for h in heads[::2]:
                    dv[at, pairs[h]] += mm(p[h, at, :], gm[h]) + mm(p[h + 1, at, :], gm[h + 1])
                lows = [(p[h, at, :].astype(F32) * (prob_grads[h - first_head] - spread[h])).astype(BF16) for h in heads]
                for h in heads[::2]:
                    n = h - first_head
                    dk[at, pairs[h]] += mm(lows[n], qm[h]) + mm(lows[n + 1], qm[h + 1])
                for h in heads:
                    head = slice(h * hd, (h + 1) * hd)
                    dqt[head, :] += mm(kt[head, at], lows[h - first_head])
            return carry

        twice(count, base, body, 0)
        return dqt[...].astype(BF16).T

    def add_vec(row, values):
        vecg_out[row:row + 1, :] += jnp.sum(values, axis=0, keepdims=True)

    x_rows = x_ref[...]
    q = ((mm(x_rows, wqkv[:, :d_model]) + vec[0:1]) * 0.125).astype(BF16)
    q_t = q.T
    put_masked(q, q_t, qm_s, gtm)
    inv_s = attend(q_t, gtm, k_s, vt_s, p_s, ot_s, kn_s, lo_s, hi_s, s_from, s_to)
    mixed = ot_s[...].astype(BF16).T
    mixed_out[...] = mixed
    first_norm, unit1, scale1 = normalize(
        x_rows.astype(F32) + (mm(mixed, wout[...]) + vec[2:3]), vec[11:12], vec[14:15])
    first_low = first_norm.astype(BF16)
    first_low_out[...] = first_low
    cq = ((mm(first_low, wcq[...]) + vec[3:4]) * 0.125).astype(BF16)
    cq_t = cq.T
    put_masked(cq, cq_t, qm_c, gtm)
    inv_c = attend(cq_t, gtm, k_c, vt_c, p_c, ot_c, kn_c, lo_c, hi_c, c_from, c_to)
    cmixed = ot_c[...].astype(BF16).T
    cmixed_out[...] = cmixed
    second, unit2, scale2 = normalize(
        first_norm + (mm(cmixed, wcout[...]) + vec[5:6]), vec[12:13], vec[15:16])
    second_low = second.astype(BF16)
    second_low_out[...] = second_low
    tile = 2 * d_model
    ffn = None
    for t in range(ff // tile):
        cols = slice(t * tile, (t + 1) * tile)
        hidden = mm(second_low, wup[:, cols]) + jnp.concatenate([vec[7 + 2*t:8 + 2*t], vec[8 + 2*t:9+2*t]], axis=1)
        smooth, slope = gelu_parts(hidden)
        active = smooth.astype(BF16)
        active_out[:, cols] = active
        slope_s[:, cols] = slope
        part = mm(active, wdown[cols, :])
        ffn = part if ffn is None else ffn + part
    third, unit3, scale3 = normalize(second + (ffn + vec[6:7]), vec[13:14], vec[16:17])
    layer_out[...] = third.astype(BF16)

    grad = ct_ref[...].astype(F32)
    add_vec(13, grad * unit3)
    add_vec(16, grad)
    grad_third = normalize_back(unit3, scale3, vec[13:14], grad)
    down_low = grad_third.astype(BF16)
    down_low_out[...] = down_low
    add_vec(6, down_low.astype(F32))
    back = grad_third
    for t in range(ff // tile):
        cols = slice(t * tile, (t + 1) * tile)
        up_low = (mm_nt(down_low, wdown[cols, :]) * slope_s[:, cols]).astype(BF16)
        up_low_out[:, cols] = up_low
        add_vec(7 + 2*t, up_low[:, :512].astype(F32))
        add_vec(8 + 2*t, up_low[:, 512:].astype(F32))
        back = back + mm_nt(up_low, wup[:, cols])
    add_vec(12, back * unit2)
    add_vec(15, back)
    grad_mid = normalize_back(unit2, scale2, vec[12:13], back)
    cross_low = grad_mid.astype(BF16)
    cross_low_out[...] = cross_low
    add_vec(5, cross_low.astype(F32))
    cross_grad = mm_nt(cross_low, wcout[...]).astype(BF16)
    cdq = attend_back(cross_grad, inv_c, qm_c, k_c, kt_c, v_c, p_c, ot_c, dk_c, dv_c, c_from, c_to) * 0.125
    cdq_out[...] = cdq

    def put_out(slabs, dk, dv):
        for n in range(2):
            cols = slice(n * 256, (n + 1) * 256)
            slabs[n] = dk[:, cols].astype(BF16)
            slabs[2 + n] = dv[:, cols].astype(BF16)

    @pl.when(step == steps - 1)
    def _():
        add_vec(4, dv_c[...])
        put_out(p_c, dk_c, dv_c)
        pltpu.make_async_copy(p_c.at[0:4], dckv_hbm, sems.at[1]).start()

    add_vec(3, cdq.astype(F32))
    grad_first = grad_mid + mm_nt(cdq, wcq[...])
    add_vec(11, grad_first * unit1)
    add_vec(14, grad_first)
    grad_in = normalize_back(unit1, scale1, vec[11:12], grad_first)
    self_low = grad_in.astype(BF16)
    self_low_out[...] = self_low
    add_vec(2, self_low.astype(F32))
    self_grad = mm_nt(self_low, wout[...]).astype(BF16)
    dq = attend_back(self_grad, inv_s, qm_s, k_s, kt_s, v_s, p_s, ot_s, dk_s, dv_s, s_from, s_to) * 0.125
    dq_out[...] = dq
    add_vec(0, dq.astype(F32))
    part_out[...] = grad_in + mm_nt(dq, wqkv[:, :d_model])

    @pl.when(step == steps - 1)
    def _():
        add_vec(1, dv_s[...])
        put_out(p_s, dk_s, dv_s)
        pltpu.make_async_copy(p_s.at[0:4], dkv_hbm, sems.at[0]).start()
        pltpu.make_async_copy(p_s.at[0:4], dkv_hbm, sems.at[0]).wait()
        pltpu.make_async_copy(p_c.at[0:4], dckv_hbm, sems.at[1]).wait()


def run_layer(counts, x_full, m_full, ct_full, vec_all, w_all, w_down):
    t_len, d_model = x_full.shape
    s_len = m_full.shape[0]
    ff = w_down.shape[0]
    steps = t_len // (2 * RB)
    own = t_len // 2
    any_spec = pl.BlockSpec(memory_space=pl.ANY)

    def rows(cols):
        return pl.BlockSpec((RB, cols), lambda i, b: (i, 0))

    def arr(cols, dtype=BF16):
        return jax.ShapeDtypeStruct((own, cols), dtype)

    out_shape = [arr(d_model) for _ in range(8)] + [arr(ff), arr(ff), arr(d_model), arr(d_model), arr(d_model, F32)]
    out_specs = [rows(s.shape[1]) for s in out_shape]
    out_shape += [
        jax.ShapeDtypeStruct((4, t_len, 256), BF16),
        jax.ShapeDtypeStruct((4, s_len, 256), BF16),
        jax.ShapeDtypeStruct((32, d_model), F32),
    ]
    out_specs += [any_spec, any_spec, pl.BlockSpec((32, d_model), lambda i, b: (0, 0))]
    bf = lambda *shape: pltpu.VMEM(shape, BF16)
    fl = lambda *shape: pltpu.VMEM(shape, F32)
    scratch = [bf(d_model, n * d_model) for n in (3, 1, 1, 2, 1)] + [bf(d_model, ff), bf(ff, d_model)] + [
        bf(t_len, d_model), bf(d_model, t_len), bf(t_len, d_model), bf(d_model, t_len),
        bf(s_len, d_model), bf(d_model, s_len), bf(s_len, d_model), bf(d_model, s_len),
        bf(H, t_len, RB), bf(H, s_len, RB),
        fl(t_len, d_model), fl(t_len, d_model), fl(s_len, d_model), fl(s_len, d_model),
        bf(H, RB, 128), bf(H, RB, 128), bf(H, 128, RB), bf(H, RB, 128),
        fl(d_model, RB), fl(d_model, RB), fl(d_model, RB), fl(RB, ff), fl(32, d_model), fl(H, RB), fl(H, RB),
        pltpu.SemaphoreType.DMA((11,)),
    ]
    return pl.pallas_call(
        layer_kernel,
        out_shape=out_shape,
        grid_spec=pltpu.PrefetchScalarGridSpec(
            num_scalar_prefetch=1,
            grid=(steps,),
            in_specs=[any_spec, any_spec] + [pl.BlockSpec((RB, d_model), lambda i, b: (2 * i + b[32, 0], 0))] * 2 + [
                      pl.BlockSpec(vec_all.shape, lambda i, b: (0, 0, 0)), any_spec, any_spec],
            out_specs=out_specs,
            scratch_shapes=scratch,
        ),
        compiler_params=pltpu.CompilerParams(vmem_limit_bytes=64 * 1024 * 1024 - 512 * 1024),
        name="layer",
    )(counts, x_full, m_full, x_full, ct_full, vec_all, w_all, w_down)


def ring_neighbours(at, size):
    odd = lax.rem(at, 2)
    after = jnp.where(odd == 0, jnp.where(at + 2 < size, at + 2, at + 1), jnp.where(at >= 3, at - 2, at - 1))
    before = jnp.where(odd == 0, jnp.where(at >= 2, at - 2, at + 1), jnp.where(at + 2 < size, at + 2, at - 1))
    return after, before


def ring_place(at, size):
    return jnp.where(lax.rem(at, 2) == 0, lax.div(at, 2), size - 1 - lax.div(at, 2))


def ring_member(place, size):
    place = lax.rem(place + 2 * size, size)
    return jnp.where(place < lax.div(size, 2), 2 * place, 2 * (size - 1 - place) + 1)


ROWS_AT = {2: (3, 0), 4: (1,), 6: (2,)}
LAG = 4


def gather_kernel(
    size, splits,
    tokens, memory, cotangent, tgt_ids, src_ids, proj_bias, up_bias, norm_gain, norm_bias,
    w_qkv, w_out, w_cq, w_ckv, w_cout, w_up, w_down,
    x_full, m_full, c_full, counts_all, vec_all, w_all, d_all,
    counts, spread, packed, stage_w, stage_d, stage_x, stage_m, stage_c,
    send_own, recv_own, send_ring, recv_ring, send_core, recv_core, send_chip, recv_chip, stage_sems, local_sems,
    send_rows, recv_rows,
):
    at, place = lax.axis_index("dp"), lax.axis_index("seq")
    micro, core = lax.div(place, 2), lax.rem(place, 2)
    after, before = ring_neighbours(at, size)
    mine = ring_place(at, size)
    core_peer = {"seq": place + 1 - 2 * core}
    chip_peer = {"seq": place + 2 - 4 * micro}
    peers = ({"dp": after}, {"dp": before}, core_peer, chip_peer)

    barrier = pltpu.get_barrier_semaphore()
    for peer in peers:
        pl.semaphore_signal(barrier, inc=1, device_id=peer, device_id_type=pl.DeviceIdType.MESH)

    wide, tall = w_qkv.shape[0], w_down.shape[0]
    shards = tuple(zip((w_qkv, w_out, w_cq, w_ckv, w_cout, w_up), splits))
    staged = [(shard, stage_w.at[:, pl.ds(column, shard.shape[1])]) for shard, column in shards]
    staged += [(w_down, stage_d)]
    staged += [(rows.at[micro, 0], stage) for rows, stage in
               ((tokens, stage_x), (memory, stage_m), (cotangent, stage_c))]
    staging = [pltpu.make_async_copy(src, dst, stage_sems.at[n]) for n, (src, dst) in enumerate(staged)]
    for copy in staging:
        copy.start()

    width = proj_bias.shape[1]
    spread[...] = jnp.zeros_like(spread)
    spread[0:7, :width] = proj_bias[...].astype(F32)
    spread[7:10, :width] = norm_gain[...].astype(F32)
    spread[10:13, :width] = norm_bias[...].astype(F32)
    for n in range(4 * width // 128):
        spread[13 + n:14 + n, :] = up_bias[pl.ds(n * 128, 128)].astype(F32).reshape(1, 128)
    packed[...] = spread[...].astype(BF16)
    lane = lax.broadcasted_iota(jnp.int32, (8, 128), 1)
    for index in range(2):
        total = jnp.zeros((8, 128), F32)
        for ids, docs, offset in ((tgt_ids, range(1, 9), 0), (src_ids, range(1, 9), 8)):
            row = ids[index]
            for doc in docs:
                below = jnp.sum(jnp.where(row < doc, 1.0, 0.0), axis=1, keepdims=True)
                total = total + jnp.where(lane == doc + offset, below, 0.0)
        counts[index, 0] = total.astype(jnp.int32)
    counts[2, 0] = jnp.full((8, 128), core, jnp.int32)

    pairs = ((tokens, x_full), (memory, m_full), (cotangent, c_full), (counts, counts_all))

    def chunk(n, owner):
        source, full = pairs[n]
        rows = source.shape[-2]
        return full.at[pl.ds(pl.multiple_of(owner * rows, 8), rows)]

    def rows_of(n, index):
        return pairs[n][0].at[index, 0]

    sent, arriving = [], []

    def send(src, dst, send_sem, recv_sem, peer):
        copy = pltpu.make_async_remote_copy(src, dst, send_sem, recv_sem, device_id=peer,
                                            device_id_type=pl.DeviceIdType.MESH)
        copy.start()
        sent.append(copy)
        return copy

    cut = splits[3]
    columns = (pl.ds(0, cut), pl.ds(cut, w_all.shape[1] - cut))

    def part(stream, way, chip):
        if stream < 2:
            return (2 * core + way) * (wide // 4), wide // 4
        return (4 * core + 2 * chip + way) * (tall // 8), tall // 8

    def piece(stream, way, owner, chip):
        if stream == 3:
            return vec_all.at[owner]
        start, length = part(stream, way, chip)
        rows = pl.ds(pl.multiple_of(owner * (wide if stream < 2 else tall) + start, 16), length)
        return w_all.at[rows, columns[stream]] if stream < 2 else d_all.at[rows]

    ways = ({"dp": after}, {"dp": before})
    pl.semaphore_wait(barrier, 4)

    first = {}
    first[3, 0] = [send(packed, vec_all.at[at], send_own.at[0, 7], recv_own.at[0, 7], ways[0])]
    for stream, way in ((0, 0), (0, 1), (1, 0), (1, 1)):
        start, length = part(stream, way, micro)
        first[stream, way] = [
            send(shard.at[pl.ds(pl.multiple_of(start, 16), length)],
                 w_all.at[pl.ds(pl.multiple_of(at * wide + start, 16), length), pl.ds(column, shard.shape[1])],
                 send_own.at[way, n], recv_own.at[way, n], ways[way])
            for n, (shard, column) in enumerate(shards) if (column >= cut) == (stream == 1)
        ]
    for way in range(2):
        start, length = part(2, way, micro)
        first[2, way] = [send(w_down.at[pl.ds(pl.multiple_of(start, 16), length)],
                              d_all.at[pl.ds(pl.multiple_of(at * tall + start, 16), length)],
                              send_own.at[way, 6], recv_own.at[way, 6], ways[way])]
    across = [send(rows_of(n, 1 - micro), chunk(n, place), send_rows.at[n, 0], recv_rows.at[n, 0], chip_peer)
              for n in (3, 0, 1, 2)]
    across = across[1:] + across[:1]
    for n in range(4):
        arriving.append(send(rows_of(n, micro), chunk(n, place), send_rows.at[n, 1], recv_rows.at[n, 1], core_peer))
    for copy in staging:
        copy.wait()
    own = [(stage_w, w_all.at[pl.ds(pl.multiple_of(at * wide, 16), wide)]),
           (stage_d, d_all.at[pl.ds(pl.multiple_of(at * tall, 16), tall)]),
           (packed, vec_all.at[at]), (counts.at[2, 0], counts_all.at[pl.ds(32, 8)]),
           (stage_x, chunk(0, place)), (stage_m, chunk(1, place)), (stage_c, chunk(2, place)),
           (counts.at[micro, 0], chunk(3, place))]
    own = [pltpu.make_async_copy(src, dst, local_sems.at[n]) for n, (src, dst) in enumerate(own)]
    for copy in own:
        copy.start()

    current, chips = {}, {}

    def owner_at(way, step):
        return ring_member(mine - step if way == 0 else mine + step, size)

    def from_chip(step):
        for way in range(2):
            chips[way, step].wait_recv()
            block = piece(2, way, owner_at(way, step), 1 - micro)
            arriving.append(send(block, block, send_core.at[3, way, step - 1], recv_core.at[3, way, step - 1], core_peer))

    for step in range(1, size):
        for stream in (3, 0, 1, 2):
            for way in range(1 if stream == 3 else 2):
                for copy in first[stream, way] if step == 1 else [current[stream, way]]:
                    copy.wait_recv()
                block = piece(stream, way, owner_at(way, step), micro)
                if step < size - 1:
                    current[stream, way] = send(block, block, send_ring.at[stream, way, step],
                                                recv_ring.at[stream, way, step], ways[way])
                if stream < 3:
                    arriving.append(send(block, block, send_core.at[stream, way, step - 1],
                                         recv_core.at[stream, way, step - 1], core_peer))
                if stream == 2:
                    chips[way, step] = send(block, block, send_chip.at[way, step - 1], recv_chip.at[way, step - 1],
                                            chip_peer)
        for n in ROWS_AT.get(step, ()):
            across[n].wait_recv()
            other = chunk(n, place + 2 - 4 * micro)
            arriving.append(send(other, other, send_rows.at[n, 2], recv_rows.at[n, 2], core_peer))
        if step > LAG:
            from_chip(step - LAG)
    for step in range(size - LAG, size):
        from_chip(step)
    for copy in arriving:
        copy.wait_recv()
    for copy in sent:
        copy.wait_send()
    for copy in own:
        copy.wait()


def gather_fused(tokens, memory, cotangent, tgt_ids, src_ids, vectors, shards):
    size = lax.axis_size("dp")
    d_model = tokens.shape[3]
    widths = [shard.shape[1] for shard in shards[:6]]
    splits = [sum(widths[:n]) for n in range(6)]
    seq = lax.axis_size("seq")
    any_spec = pl.BlockSpec(memory_space=pl.ANY)
    out_shape = [jax.ShapeDtypeStruct((seq * a.shape[2], d_model), BF16) for a in (tokens, memory, cotangent)]
    out_shape += [
        jax.ShapeDtypeStruct((seq * 8 + 8, 128), jnp.int32),
        jax.ShapeDtypeStruct((size, 16, 128), BF16),
        jax.ShapeDtypeStruct((size * shards[0].shape[0], sum(widths)), BF16),
        jax.ShapeDtypeStruct((size * shards[6].shape[0], d_model), BF16),
    ]
    dma = pltpu.SemaphoreType.DMA
    return pl.pallas_call(
        functools.partial(gather_kernel, size, splits),
        out_shape=out_shape,
        in_specs=[any_spec] * 3 + [pl.BlockSpec(memory_space=pltpu.VMEM)] * 6 + [any_spec] * 7,
        out_specs=[any_spec] * 7,
        scratch_shapes=[
            pltpu.VMEM((3, 1, 8, 128), jnp.int32), pltpu.VMEM((16, 128), F32), pltpu.VMEM((16, 128), BF16),
            pltpu.VMEM((shards[0].shape[0], sum(widths)), BF16), pltpu.VMEM(shards[6].shape, BF16),
            *(pltpu.VMEM(a.shape[2:], BF16) for a in (tokens, memory, cotangent)),
            dma((2, 8)), dma((2, 8)), dma((4, 2, size)), dma((4, 2, size)), dma((4, 2, size)), dma((4, 2, size)),
            dma((2, size)), dma((2, size)), dma((10,)), dma((8,)), dma((4, 3)), dma((4, 3)),
        ],
        compiler_params=pltpu.CompilerParams(collective_id=0, has_side_effects=True),
        name="gather",
    )(tokens, memory, cotangent, tgt_ids, src_ids, *vectors, *shards)


MESH = pl.DeviceIdType.MESH


SCHEDULE = "D U r0 Q r1 P a0 O r2 a01 R r3 V a0123 H E a0123 V a0123 V a0123 V a0123 V a0123 a0123"


def stream_shapes(d_model, ff, size):
    return [(d_model, d_model // size, q) for q in (ff // 4, ff // 4, 5 * d_model // 4, 3 * d_model // 4)]


def settle_kernel(size, shapes, *refs):
    n_in, n_out, count = 18, 4 + 2 * len(shapes), len(shapes)
    (x_hbm, m_hbm, w_hbm, lo_hbm, mixed_hbm, self_low_hbm, first_low_hbm, cdq_hbm, cmixed_hbm, cross_low_hbm,
     second_low_hbm, up_low_hbm, active_hbm, down_low_hbm, dq_hbm, part_hbm, dkv_hbm, dckv_hbm) = refs[:n_in]
    vec_hbm = refs[n_in]
    outs = refs[n_in + 1:n_in + 1 + n_out]
    lo_home, dt_home, dm_home, vec_out = outs[:4]
    ga, gb = outs[4:4 + count], outs[4 + count:]
    scratch = refs[n_in + 1 + n_out:]
    (xf, mf, wkv, wpair, xo, mixed, self_low, first_low, cdq, cmixed, cross_low, second_low, up_low, active,
     down_low, dq, part, dkv, dckv) = scratch[:19]
    (tz, tz_low, tz_got, mz, mz_low, mz_got, lo_buf, vec_run, vec_got) = scratch[19:28]
    rest = scratch[28:]
    acc, stage, other, ring_out, ring_in, fin = (rest[n * count:(n + 1) * count] for n in range(6))
    (load_sems, store_sems, ring_ss, ring_rs, core_ss, core_rs, fin_ss, fin_rs, row_ss, row_rs, vec_ss, vec_rs,
     lo_ss, lo_rs) = rest[6 * count:]

    at, place = lax.axis_index("dp"), lax.axis_index("seq")
    micro, core = lax.div(place, 2), lax.rem(place, 2)
    after, before = ring_neighbours(at, size)
    mine = ring_place(at, size)
    core_peer = {"seq": place + 1 - 2 * core}
    chip_peer = {"seq": place + 2 - 4 * micro}
    levels = size.bit_length() - 1
    flips = [{"dp": at + (1 << n) * (1 - 2 * lax.rem(lax.div(at, 1 << n), 2))} for n in range(levels)]
    vec_peers = [core_peer, chip_peer] + flips
    d_model = xf.shape[1]
    half = d_model // 2
    t_len, s_len = xf.shape[0], mf.shape[0]

    barrier = pltpu.get_barrier_semaphore()
    greeted = [{"dp": after}, {"dp": before}, core_peer, chip_peer] + flips
    for peer in greeted:
        pl.semaphore_signal(barrier, inc=1, device_id=peer, device_id_type=MESH)

    loads = {}

    def load(name, src, dst):
        copy = pltpu.make_async_copy(src, dst, load_sems.at[len(loads)])
        copy.start()
        loads[name] = copy

    def load_first():
        load("active", active_hbm, active)
        load("down_low", down_low_hbm, down_low)
        load("vec", vec_hbm.at[pl.ds(0, 24)], vec_run.at[0])

    def load_up():
        load("second_low", second_low_hbm, second_low)
        load("up_low", up_low_hbm, up_low)

    def load_qkv():
        load("dkv", dkv_hbm, dkv)
        load("xf", x_hbm, xf)
        for n in range(t_len // (2 * RB)):
            load(("xo", n), x_hbm.at[pl.ds((2 * n + core) * RB, RB)], xo.at[pl.ds(n * RB, RB)])
        load("dq", dq_hbm, dq)

    def load_rest():
        load("dckv", dckv_hbm, dckv)
        load("mf", m_hbm, mf)
        for name, src, dst in (("mixed", mixed_hbm, mixed), ("self_low", self_low_hbm, self_low),
                               ("first_low", first_low_hbm, first_low), ("cdq", cdq_hbm, cdq),
                               ("cmixed", cmixed_hbm, cmixed), ("cross_low", cross_low_hbm, cross_low)):
            load(name, src, dst)
        load("wkv", w_hbm.at[:, pl.ds(d_model, 2 * d_model)], wkv)
        load("part", part_hbm, part)
        load("wpair", w_hbm.at[:, pl.ds(5 * d_model, 2 * d_model)], wpair)

    load_first()
    load_up()

    pending = []

    def send(src, dst, send_sem, recv_sem, peer):
        copy = pltpu.make_async_remote_copy(src, dst, send_sem, recv_sem, device_id=peer, device_id_type=MESH)
        copy.start()
        pending.append(copy)
        return copy

    stores = []

    def store(src, dst):
        copy = pltpu.make_async_copy(src, dst, store_sems.at[len(stores)])
        copy.start()
        stores.append(copy)

    pl.semaphore_wait(barrier, len(greeted))

    piece = t_len // 12
    keep, give = [], []

    def pieces_of(index0, slot0, index1, slot1):
        index, slot = jnp.where(core == 0, index0, index1), jnp.where(core == 0, slot0, slot1)
        source = lo_hbm.at[pl.ds(pl.multiple_of(index * piece, 128), piece)]
        return source, lo_buf.at[lax.div(slot, 3), pl.ds(pl.multiple_of(lax.rem(slot, 3) * piece, 128), piece)]

    for n, row in enumerate(((0, 0, 1, 0), (1, 1, 4, 4), (4, 5, 5, 5))):
        copy = pltpu.make_async_copy(*pieces_of(*row), lo_ss.at[n])
        copy.start()
        keep.append(copy)
    for n, row in enumerate(((2, 1, 0, 2), (3, 2, 2, 3), (5, 3, 3, 4))):
        source, target = pieces_of(*row)
        give.append(send(source, target, lo_ss.at[3 + n], lo_rs.at[n], core_peer))

    vec_state = {"level": 0, "copy": None}

    def vec_send():
        level = vec_state["level"]
        vec_state["copy"] = send(vec_run.at[level], vec_got.at[level], vec_ss.at[level], vec_rs.at[level],
                                 vec_peers[level])

    def vec_step():
        level = vec_state["level"]
        vec_state["copy"].wait_recv()
        vec_run[level + 1] = vec_run[level] + vec_got[level]
        vec_state["level"] = level + 1
        if level + 1 < len(vec_peers):
            vec_send()
        else:
            store(vec_run.at[level + 1], vec_out)

    loads["vec"].wait()
    vec_send()

    row_waits = []

    def home_rows(n, rows_of, home):
        store(rows_of(micro), home.at[micro])
        row_waits.append(send(rows_of(1 - micro), home.at[micro], row_ss.at[n], row_rs.at[n], chip_peer))

    def split(values, pieces, s, rows, base=0):
        width = values.shape[1] // pieces
        quarter = width // 4
        for p in range(pieces):
            lower = values[:, p * width:p * width + 2 * quarter]
            upper = values[:, p * width + 2 * quarter:(p + 1) * width]
            own = jnp.where(core == 0, lower, upper)
            away = jnp.where(core == 0, upper, lower).astype(BF16)
            cols = slice(base + p * quarter, base + (p + 1) * quarter)
            for way in range(2):
                acc[s][way, rows, cols] = own[:, way * quarter:(way + 1) * quarter]
                stage[s][way, rows, cols] = away[:, way * quarter:(way + 1) * quarter]

    core_waits = {}
    tile = 256

    def await_loads(*names):
        for name in names:
            loads[name].wait()

    def each_tile(body):
        def one(m, carry):
            body(pl.ds(pl.multiple_of(m * tile, tile), tile))
            return carry

        lax.fori_loop(0, d_model // tile, one, 0)

    def share(s):
        core_waits[s] = send(stage[s], other[s], core_ss.at[s], core_rs.at[s], core_peer)

    def compute_down():
        await_loads("active", "down_low")
        load_qkv()
        block, tall = shapes[0][1], active.shape[1] // size
        quarter = d_model // 4

        def one(m, carry):
            values = mm_tn(active[:, pl.ds(pl.multiple_of(m * tall, tall), tall)], down_low[...])
            rows = pl.ds(pl.multiple_of(m * block, block), block)
            for n in range(tall // block):
                split(values[n * block:(n + 1) * block], 1, 0, rows, n * quarter)
            return carry

        lax.fori_loop(0, size, one, 0)
        share(0)

    def compute_up():
        await_loads("second_low", "up_low")
        load_rest()
        each_tile(lambda rows: split(mm_tn(second_low[:, rows], up_low[...]), 1, 1, rows))
        share(1)

    def compute_qkv():
        await_loads("dkv", "xf", "dq", *(("xo", n) for n in range(t_len // (2 * RB))))

        def one(rows):
            split(mm_tn(xo[:, rows], dq[...]), 1, 2, rows)
            whole = xf[:, rows]
            for n in range(2):
                parts = [mm_tn(whole, dkv[2 * n + m]) for m in range(2)]
                split(jnp.concatenate(parts, axis=1), 1, 2, rows, (1 + n) * d_model // 4)

        each_tile(one)

    def compute_pair():
        await_loads("dckv", "mf")

        def one(rows):
            whole = mf[:, rows]
            for n in range(2):
                parts = [mm_tn(whole, dckv[2 * n + m]) for m in range(2)]
                split(jnp.concatenate(parts, axis=1), 1, 2, rows, (3 + n) * d_model // 4)

        each_tile(one)
        share(2)

    def compute_outs():
        await_loads("mixed", "self_low", "first_low", "cdq", "cmixed", "cross_low")

        def one(rows):
            for n, (left, right) in enumerate(((mixed, self_low), (first_low, cdq), (cmixed, cross_low))):
                split(mm_tn(left[:, rows], right[...]), 1, 3, rows, n * d_model // 4)

        each_tile(one)
        share(3)

    ring_waits = {}

    def ring(s, step):
        block = shapes[s][1]
        if step == 0:
            core_waits[s].wait_recv()
        for way in range(2):
            owner = ring_member(mine - 1 - step if way == 0 else mine + 1 + step, size)
            rows = pl.ds(pl.multiple_of(owner * block, block), block)
            total = acc[s][way, rows, :] + other[s][way, rows, :].astype(F32)
            if step > 0:
                ring_waits[s, way].wait_recv()
                total = total + ring_in[s][way, step - 1].astype(F32)
            if step < size - 1:
                ring_out[s][way, step] = total.astype(BF16)
                ring_waits[s, way] = send(
                    ring_out[s].at[way, step], ring_in[s].at[way, step], ring_ss.at[s, way, step],
                    ring_rs.at[s, way, step], {"dp": after if way == 0 else before})
            else:
                fin[s][way] = total.astype(BF16)

    chip_waits, tail = {}, []

    def finish(s):
        store(fin[s], ga[s].at[core])
        chip_waits[s] = send(fin[s], gb[s].at[core], fin_ss.at[s, 0], fin_rs.at[s, 0], chip_peer)
        tail.append(send(fin[s], ga[s].at[core], fin_ss.at[s, 1], fin_rs.at[s, 1], core_peer))

    def forward(s):
        chip_waits[s].wait_recv()
        tail.append(send(gb[s].at[core], gb[s].at[core], fin_ss.at[s, 2], fin_rs.at[s, 2], core_peer))

    def row_products():
        await_loads("wkv", "part", "wpair")

        def tokens(b, carry):
            rows = pl.ds(pl.multiple_of(b * RB, RB), RB)
            total = None
            for n in range(4):
                product = mm_nt(dkv[n, rows, :], wkv[:, n * 256:(n + 1) * 256])
                total = product if total is None else total + product
            own = part[pl.ds(pl.multiple_of(lax.div(b, 2) * RB, RB), RB), :]
            total = total + jnp.where(lax.rem(b, 2) == core, own, jnp.zeros_like(own))
            tz[rows, :] = total
            tz_low[rows, :] = total.astype(BF16)
            return carry

        lax.fori_loop(0, t_len // RB, tokens, 0)

        def memories(b, carry):
            rows = pl.ds(pl.multiple_of(b * RB, RB), RB)
            total = None
            for n in range(4):
                product = mm_nt(dckv[n, rows, :], wpair[:, n * 256:(n + 1) * 256])
                total = product if total is None else total + product
            mz[rows, :] = total
            mz_low[rows, :] = total.astype(BF16)
            return carry

        lax.fori_loop(0, s_len // RB, memories, 0)
        copies = []
        for n, (low, got, length) in enumerate(((tz_low, tz_got, t_len // 4), (mz_low, mz_got, s_len // 4))):
            for k in range(2):
                start = pl.multiple_of((1 - core + 2 * k) * length, 128)
                copies.append(send(low.at[pl.ds(start, length)], got.at[k], row_ss.at[3 + 2 * n + k],
                                   row_rs.at[3 + 2 * n + k], core_peer))
        return copies

    def row_finish(copies):
        for copy in copies:
            copy.wait_recv()
        for n, (full, got, done, length, home) in enumerate((
                (tz, tz_got, tz_low, t_len // 4, dt_home), (mz, mz_got, mz_low, s_len // 4, dm_home))):

            def rows_at(k, length=length):
                return pl.ds(pl.multiple_of((core + 2 * k) * length, 128), length)

            for k in range(2):
                done[rows_at(k), :] = (full[rows_at(k), :] + got[k].astype(F32)).astype(BF16)
            home_rows(1 + n, lambda k, done=done, rows_at=rows_at: done.at[rows_at(k)], home)

    reached = [0] * count
    sent_home = []

    def advance(s):
        if reached[s] < size - 1:
            reached[s] += 1
            ring(s, reached[s])
            if reached[s] == size - 1:
                finish(s)
                sent_home.append(s)

    def rows_start():
        state["rows"] = row_products()

    def rows_end():
        row_finish(state["rows"])

    def layer_rows():
        for copy in keep:
            copy.wait()
        for copy in give:
            copy.wait_recv()
        home_rows(0, lambda k: lo_buf.at[k], lo_home)

    def vectors():
        if vec_state["level"] < len(vec_peers):
            vec_step()

    state = {}
    actions = {"D": compute_down, "U": compute_up, "Q": compute_qkv, "P": compute_pair, "O": compute_outs,
               "R": rows_start, "E": rows_end, "H": layer_rows, "V": vectors}
    for action in SCHEDULE.split():
        if action in actions:
            actions[action]()
        elif action[0] == "r":
            ring(int(action[1]), 0)
        else:
            for s in action[1:]:
                advance(int(s))
    for s in range(count):
        forward(s)
    for copy in row_waits + tail:
        copy.wait_recv()
    for copy in pending:
        copy.wait_send()
    for copy in stores:
        copy.wait()


def settle_fused(x_full, m_full, w_all, results):
    size = lax.axis_size("dp")
    (layer_rows, mixed, self_low, first_low, cdq, cmixed, cross_low, second_low, up_low, active, down_low, dq,
     part, dkv, dckv, vec_sums) = results
    t_len, d_model = x_full.shape
    s_len, ff, own = m_full.shape[0], up_low.shape[1], dq.shape[0]
    shapes = stream_shapes(d_model, ff, size)
    any_spec = pl.BlockSpec(memory_space=pl.ANY)
    out_shape = [
        jax.ShapeDtypeStruct((2, t_len // 4, d_model), BF16),
        jax.ShapeDtypeStruct((2, t_len // 4, d_model), BF16),
        jax.ShapeDtypeStruct((2, s_len // 4, d_model), BF16),
        jax.ShapeDtypeStruct((24, d_model), F32),
    ]
    out_shape += [jax.ShapeDtypeStruct((2, 2, block, q), BF16) for _, block, q in shapes] * 2
    bf = lambda *shape: pltpu.VMEM(shape, BF16)
    fl = lambda *shape: pltpu.VMEM(shape, F32)
    dma = pltpu.SemaphoreType.DMA
    levels = 2 + size.bit_length() - 1
    count = len(shapes)
    scratch = [bf(t_len, d_model), bf(s_len, d_model), bf(d_model, 2 * d_model), bf(d_model, 2 * d_model)]
    scratch += [bf(own, d_model)] * 8 + [bf(own, ff)] * 2 + [bf(own, d_model)] * 2 + [
        fl(own, d_model), bf(4, t_len, 256), bf(4, s_len, 256),
        fl(t_len, d_model), bf(t_len, d_model), bf(2, t_len // 4, d_model),
        fl(s_len, d_model), bf(s_len, d_model), bf(2, s_len // 4, d_model),
        bf(2, t_len // 4, d_model), fl(levels + 1, 24, d_model), fl(levels, 24, d_model),
    ]
    scratch += [fl(2, rows, q) for rows, _, q in shapes]
    scratch += [bf(2, rows, q) for rows, _, q in shapes] * 2
    scratch += [bf(2, size - 1, block, q) for _, block, q in shapes] * 2
    scratch += [bf(2, block, q) for _, block, q in shapes]
    scratch += [dma((24,)), dma((16,)), dma((count, 2, size)), dma((count, 2, size)), dma((count,)), dma((count,)),
                dma((count, 3)), dma((count, 3)), dma((7,)), dma((7,)), dma((levels,)), dma((levels,)), dma((6,)),
                dma((3,))]
    return pl.pallas_call(
        functools.partial(settle_kernel, size, shapes),
        out_shape=out_shape,
        in_specs=[any_spec] * 19,
        out_specs=[any_spec] * len(out_shape),
        scratch_shapes=scratch,
        compiler_params=pltpu.CompilerParams(
            collective_id=1, has_side_effects=True, vmem_limit_bytes=64 * 1024 * 1024 - 512 * 1024),
        name="settle",
    )(x_full, m_full, w_all, layer_rows, mixed, self_low, first_low, cdq, cmixed, cross_low, second_low, up_low,
      active, down_low, dq, part, dkv, dckv, vec_sums)


def finish_kernel(factor, lo, dt, dm, vec, *refs):
    ga, gb = refs[:4], refs[4:8]
    lo_out, dt_out, dm_out, qkv, out, cq, pair, cout, up, down, bias, up_bias, gain, shift = refs[8:]
    lo_out[:, 0] = lo[...]
    dt_out[:, 0] = dt[...]
    dm_out[:, 0] = dm[...]
    firsts = ((qkv, 0), (qkv, 1), (qkv, 2), (pair, 0), (pair, 1))
    others = ((out, 0), (cq, 0), (cout, 0))
    for half in range(2):
        for way in range(2):
            totals = [(a[half, way].astype(F32) + b[half, way].astype(F32)) * factor for a, b in zip(ga, gb)]
            block, width = totals[0].shape[0], totals[3].shape[1] // len(others)
            quarter = (2 * half + way) * width
            for n in range(totals[0].shape[1] // width):
                down[n * block:(n + 1) * block, quarter:quarter + width] = totals[0][:, n * width:(n + 1) * width]
            wide = totals[1].shape[1]
            up[:, (2 * half + way) * wide:(2 * half + way + 1) * wide] = totals[1]
            for total, places in ((totals[2], firsts), (totals[3], others)):
                for n, (ref, slot) in enumerate(places):
                    column = slot * 4 * width + quarter
                    ref[:, column:column + width] = total[:, n * width:(n + 1) * width]
    at = lax.axis_index("dp")
    d_model, width = vec.shape[1], bias.shape[1]
    sums = vec[...] * factor
    own = pltpu.roll(sums, lax.rem(d_model - at * width, d_model), 1)[:, :width]
    bias[...] = own[0:7]
    gain[...] = own[11:14]
    shift[...] = own[14:17]
    start = at * 4 * width
    rows = lax.broadcasted_iota(jnp.int32, (4, d_model), 0)
    row = jnp.sum(jnp.where(rows == lax.div(start, d_model), sums[7:11], 0.0), axis=0, keepdims=True)
    row = jnp.broadcast_to(row, (8, d_model))
    up_bias[...] = pltpu.roll(row, lax.rem(d_model - lax.rem(start, d_model), d_model), 1)[0:1, :4 * width]


def finish_fused(settled, factor, d_model, ff):
    lo, dt, dm = settled[:3]
    size = lax.axis_size("dp")
    block = d_model // size
    shapes = [jax.ShapeDtypeStruct((2, 1, *a.shape[1:]), BF16) for a in (lo, dt, dm)]
    shapes += [jax.ShapeDtypeStruct((block, n * d_model), F32) for n in (3, 1, 1, 2, 1)]
    shapes += [jax.ShapeDtypeStruct((block, ff), F32), jax.ShapeDtypeStruct((ff // size, d_model), F32)]
    shapes += [jax.ShapeDtypeStruct(s, F32) for s in ((7, block), (1, ff // size), (3, block), (3, block))]

    def whole(a):
        return pl.BlockSpec(a.shape, lambda i: (0,) * len(a.shape))

    done = pl.pallas_call(
        functools.partial(finish_kernel, factor),
        grid=(1,),
        out_shape=shapes,
        in_specs=[whole(a) for a in settled],
        out_specs=[whole(s) for s in shapes],
        compiler_params=pltpu.CompilerParams(vmem_limit_bytes=63 * 1024 * 1024),
        name="finish",
    )(*settled)
    return (*done[:11], done[11][0], *done[12:])


def pack_vectors(proj_bias, up_bias, norm_gain, norm_bias, d_model):
    size, at = lax.axis_size("dp"), lax.axis_index("dp")
    width = d_model // size
    rows = jnp.concatenate([proj_bias, jnp.zeros((4, width), BF16), norm_gain, norm_bias], axis=0)
    packed = lax.dynamic_update_slice(jnp.zeros((32, d_model), BF16), rows, (0, at * width))
    flat = lax.dynamic_update_slice(jnp.zeros((4 * d_model,), BF16), up_bias, (at * up_bias.shape[0],))
    return lax.dynamic_update_slice(packed, flat.reshape(4, d_model), (7, 0))


def unpack_vectors(sums, d_model):
    size, at = lax.axis_size("dp"), lax.axis_index("dp")
    width = d_model // size
    own = lax.dynamic_slice(sums, (0, at * width), (32, width))
    up = lax.dynamic_slice(sums[7:11].reshape(-1), (at * 4 * width,), (4 * width,))
    return own[:7], up, own[11:14], own[14:17]


def gather_plain(tokens, memory, cotangent, counts, packed, shards):
    micro = lax.axis_index("seq") // MB

    def whole(rows):
        return lax.all_gather(lax.squeeze(rows, (1,)), "seq", axis=1, tiled=True)[micro]

    weights = [lax.all_gather(shard, "dp", axis=0, tiled=True) for shard in shards]
    vec_all = lax.psum(packed, "dp")[None]
    counts = jnp.pad(lax.psum(counts, "seq")[micro][None], ((0, 31), (0, 0)))
    place = jnp.full((8, 128), lax.axis_index("seq") % MB, jnp.int32)
    counts = jnp.concatenate([counts, place], axis=0)
    w_all = jnp.concatenate(weights[:6], axis=1)
    return whole(tokens), whole(memory), whole(cotangent), counts, vec_all, w_all, weights[6]


def own_rows(rows, core):
    blocks = rows.reshape(rows.shape[0] // (2 * RB), 2, RB, rows.shape[1])
    return blocks[:, core].reshape(rows.shape[0] // 2, rows.shape[1])


def spread_rows(rows, core):
    blocks = rows.reshape(rows.shape[0] // RB, 1, RB, rows.shape[1])
    blocks = jnp.concatenate([blocks, jnp.zeros_like(blocks)], axis=1)
    blocks = jnp.where(core == 0, blocks, blocks[:, ::-1])
    return blocks.reshape(rows.shape[0] * 2, rows.shape[1])


def settle_plain(x_full, m_full, w_all, results, factor):
    (layer_rows, mixed, self_low, first_low, cdq, cmixed, cross_low, second_low, up_low, active, down_low, dq,
     part, dkv, dckv, vec_sums) = results
    place = lax.axis_index("seq")
    micro, core = place // MB, place % MB
    d_model = x_full.shape[1]
    dkv = jnp.moveaxis(dkv, 0, 1).reshape(x_full.shape[0], 2 * d_model)
    dckv = jnp.moveaxis(dckv, 0, 1).reshape(m_full.shape[0], 2 * d_model)
    input_rows = spread_rows(part, core) + mm_nt(dkv, w_all[:, d_model:3 * d_model])
    memory_rows = mm_nt(dckv, w_all[:, 5 * d_model:7 * d_model])

    def home(rows):
        both = jnp.stack([rows, jnp.zeros_like(rows)])
        both = jnp.where(micro == 0, both, both[::-1])
        return lax.psum_scatter(both, "seq", scatter_dimension=1, tiled=True).astype(BF16)[:, None]

    grads = [
        jnp.concatenate([mm_tn(own_rows(x_full, core), dq), mm_tn(x_full, dkv)], axis=1),
        mm_tn(mixed, self_low), mm_tn(first_low, cdq), mm_tn(m_full, dckv), mm_tn(cmixed, cross_low),
        mm_tn(second_low, up_low), mm_tn(active, down_low),
    ]
    grads = [
        lax.psum(lax.psum_scatter(grad, "dp", scatter_dimension=0, tiled=True), "seq") * factor for grad in grads
    ]
    vec_sums = lax.psum(vec_sums, ("dp", "seq")) * factor
    return (home(spread_rows(layer_rows.astype(F32), core)), home(input_rows), home(memory_rows), *grads,
            *unpack_vectors(vec_sums, d_model))


def per_device(
    tokens, memory, cotangent, tgt_segments, src_segments,
    self_qkv, self_out, cross_q, cross_kv, cross_out, ffn_up, ffn_down, proj_bias, up_bias, norm_gain, norm_bias,
):
    d_model = tokens.shape[3]
    shards = (self_qkv, self_out, cross_q, cross_kv, cross_out, ffn_up, ffn_down)
    size, rows, ff = lax.axis_size("dp"), self_qkv.shape[0], ffn_up.shape[1]
    fused = rows == 64 and size & (size - 1) == 0 and size > 2
    factor = 1.0 / math.sqrt(MB * size * tokens.shape[2] * lax.axis_size("seq"))
    if fused:
        vectors = (proj_bias, up_bias, norm_gain, norm_bias)
        x_full, m_full, ct_full, counts, vec_all, w_all, w_down = gather_fused(
            tokens, memory, cotangent, tgt_segments, src_segments, vectors, shards)
    else:
        docs = jnp.arange(1, 9)
        tgt_counts = jnp.sum(tgt_segments[:, 0, :, None] < docs, axis=1, dtype=jnp.int32)
        src_counts = jnp.sum(src_segments[:, 0, :, None] < docs, axis=1, dtype=jnp.int32)
        counts = jnp.pad(jnp.concatenate([tgt_counts, src_counts], axis=1), ((0, 0), (1, 111)))
        packed = pack_vectors(proj_bias, up_bias, norm_gain, norm_bias, d_model)
        x_full, m_full, ct_full, counts, vec_all, w_all, w_down = gather_plain(
            tokens, memory, cotangent, counts, packed, shards)
    results = run_layer(counts, x_full, m_full, ct_full, vec_all, w_all, w_down)
    if fused:
        return finish_fused(settle_fused(x_full, m_full, w_all, results), factor, d_model, ff)
    return settle_plain(x_full, m_full, w_all, results, factor)


def solution(mesh):
    rows = P(None, "dp", "seq", None)
    ids = P(None, "dp", "seq")
    sharded = P("dp", None)
    columns = P(None, "dp")
    return jax.shard_map(
        per_device,
        mesh=mesh,
        in_specs=(rows, rows, rows, ids, ids) + (sharded,) * 7 + (columns, P("dp"), columns, columns),
        out_specs=(rows, rows, rows) + (sharded,) * 7 + (columns, P("dp"), columns, columns),
        check_vma=False,
    )
```

```python
import functools
import math

import jax
import jax.numpy as jnp
from jax import lax
from jax.experimental import pallas as pl
from jax.experimental.pallas import tpu as pltpu
from jax.sharding import PartitionSpec as P

H = 8
MB = 2
RB = 256
KB = 256
F32 = jnp.float32
BF16 = jnp.bfloat16


def mm(left, right):
    return jnp.dot(left, right, preferred_element_type=F32)


def mm_nt(left, right):
    return lax.dot_general(left, right, (((1,), (1,)), ((), ())), preferred_element_type=F32)


def mm_tn(left, right):
    return lax.dot_general(left, right, (((0,), (0,)), ((), ())), preferred_element_type=F32)


def gelu_parts(values):
    cumulative = 0.5 * (1.0 + lax.erf(values * 0.7071067811865476))
    density = jnp.exp(-0.5 * values * values) * 0.3989422804014327
    return values * cumulative, cumulative + values * density


def normalize(summed, gain, shift):
    center = summed - jnp.mean(summed, axis=-1, keepdims=True)
    scale_inv = lax.rsqrt(jnp.mean(center * center, axis=-1, keepdims=True) + 1e-05)
    unit_rows = center * scale_inv
    return unit_rows * gain + shift, unit_rows, scale_inv


def normalize_back(unit_rows, scale_inv, gain, grad_rows):
    scaled = grad_rows * gain
    return scale_inv * (
        scaled
        - jnp.mean(scaled, axis=-1, keepdims=True)
        - unit_rows * jnp.mean(scaled * unit_rows, axis=-1, keepdims=True)
    )


def fold(values, op):
    rows, cols = values.shape
    return op(values.reshape(rows // 8, 8, cols), axis=0)


def layer_kernel(
    counts,
    x_hbm, m_hbm, x_ref, ct_ref, vec_all, w_hbm, wdown_hbm,
    layer_out, mixed_out, self_low_out, first_low_out, cdq_out, cmixed_out, cross_low_out,
    second_low_out, up_low_out, active_out, down_low_out, dq_out, part_out,
    dkv_hbm, dckv_hbm, vecg_out,
    wqkv, wout, wcq, wckv, wcout, wup, wdown,
    k_s, kt_s, v_s, vt_s, k_c, kt_c, v_c, vt_c,
    p_s, p_c, dk_s, dv_s, dk_c, dv_c,
    qm_s, qm_c, gtm, gm, ot_s, ot_c, dqt, slope_s, vec_ref, kn_s, kn_c, sems,
):
    step = pl.program_id(0)
    steps = pl.num_programs(0)
    t_len, d_model = k_s.shape
    s_len = k_c.shape[0]
    ff = wup.shape[1]
    hd = d_model // H
    core = counts[32, 0]
    tgt_starts = [0] + [counts[0, d] + counts[8, d] + counts[16, d] + counts[24, d] for d in range(1, 9)]
    src_starts = [0] + [counts[0, d] + counts[8, d] + counts[16, d] + counts[24, d] for d in range(9, 17)]
    block = 2 * step + core

    def columns(start, count):
        return w_hbm.at[:, pl.ds(start * d_model, count * d_model)]

    loads = [
        pltpu.make_async_copy(src, dst, sems.at[n])
        for n, (src, dst) in enumerate((
            (columns(0, 3), wqkv), (x_hbm.at[:, pl.ds(0, 256)], p_s.at[0]), (x_hbm.at[:, pl.ds(256, 256)], p_s.at[1]),
            (columns(5, 2), wckv), (m_hbm.at[:, pl.ds(0, 256)], p_c.at[0]), (m_hbm.at[:, pl.ds(256, 256)], p_c.at[1]),
            (columns(3, 1), wout), (columns(4, 1), wcq), (columns(7, 1), wcout), (columns(8, ff // d_model), wup),
            (wdown_hbm, wdown),
        ))
    ]

    @pl.when(step == 0)
    def _():
        for load in loads[:3]:
            load.start()
        dk_s[...] = jnp.zeros_like(dk_s)
        dv_s[...] = jnp.zeros_like(dv_s)
        dk_c[...] = jnp.zeros_like(dk_c)
        dv_c[...] = jnp.zeros_like(dv_c)
        vecg_out[...] = jnp.zeros_like(vecg_out)
        parts = vec_all[...].astype(F32)
        if parts.shape[0] == 1:
            vec_ref[...] = parts[0]
        else:
            vec_ref[...] = jnp.zeros_like(vec_ref)
            width = d_model // parts.shape[0]
            for n in range(parts.shape[0]):
                cols = slice(n * width, (n + 1) * width)
                vec_ref[0:7, cols] = parts[n, 0:7, :width]
                vec_ref[11:17, cols] = parts[n, 7:13, :width]
                for m in range(4 * width // 128):
                    start = n * 4 * width + m * 128
                    row, column = 7 + start // d_model, start % d_model
                    vec_ref[row:row + 1, column:column + 128] = parts[n, 13 + m:14 + m, :]
        vec = vec_ref[...]
        vec_t = vec.T

        def project(rows_ref, w_ref, k_at, kt, k, vt, v, norms, bias_row, bias_row_t, count):
            norms[...] = jnp.zeros_like(norms)
            wk = w_ref[:, k_at:k_at + d_model]
            wv = w_ref[:, k_at + d_model:k_at + 2 * d_model]
            wk_t = wk.T
            wv_t = wv.T

            def one(r, carry):
                at = pl.ds(pl.multiple_of(r * 512, 512), 512)
                rows = jnp.concatenate([rows_ref[0, at, :], rows_ref[1, at, :]], axis=1)
                k[at, :] = mm(rows, wk).astype(BF16)
                v[at, :] = (mm(rows, wv) + bias_row).astype(BF16)
                keys_t = mm_nt(wk_t, rows)
                kt[:, at] = keys_t.astype(BF16)
                squares = keys_t * keys_t
                for h in range(H):
                    own = jnp.sum(fold(squares[h * hd:(h + 1) * hd], jnp.sum), axis=0, keepdims=True)
                    norms[h:h + 1, :] = jnp.maximum(norms[h:h + 1, :], jnp.maximum(own[:, :RB], own[:, RB:]))
                vt[:, at] = (mm_nt(wv_t, rows) + bias_row_t).astype(BF16)
                return carry

            lax.fori_loop(0, count // 512, one, 0)

        for load in loads[:3]:
            load.wait()
        for load in loads[3:]:
            load.start()
        project(p_s, wqkv, d_model, kt_s, k_s, vt_s, v_s, kn_s, vec[1:2], vec_t[:, 1:2], t_len)
        for load in loads[3:6]:
            load.wait()
        project(p_c, wckv, 0, kt_c, k_c, vt_c, v_c, kn_c, vec[4:5], vec_t[:, 4:5], s_len)
        for load in loads[6:]:
            load.wait()

    vec = vec_ref[...]

    qpos = block * RB + lax.broadcasted_iota(jnp.int32, (1, RB), 1)
    lo_s = jnp.zeros((1, RB), jnp.int32)
    hi_s = jnp.full((1, RB), tgt_starts[1], jnp.int32)
    lo_c = jnp.zeros((1, RB), jnp.int32)
    hi_c = jnp.full((1, RB), src_starts[1], jnp.int32)
    for doc in range(1, 8):
        inside = qpos >= tgt_starts[doc]
        lo_s = jnp.where(inside, tgt_starts[doc], lo_s)
        hi_s = jnp.where(inside, tgt_starts[doc + 1], hi_s)
        lo_c = jnp.where(inside, src_starts[doc], lo_c)
        hi_c = jnp.where(inside, src_starts[doc + 1], hi_c)
    first = block * RB
    last = first + RB - 1
    s_from, s_to, c_from, c_to = 0, tgt_starts[1], 0, src_starts[1]
    for doc in range(1, 8):
        in_first = first >= tgt_starts[doc]
        in_last = last >= tgt_starts[doc]
        s_from = jnp.where(in_first, tgt_starts[doc], s_from)
        c_from = jnp.where(in_first, src_starts[doc], c_from)
        s_to = jnp.where(in_last, tgt_starts[doc + 1], s_to)
        c_to = jnp.where(in_last, src_starts[doc + 1], c_to)

    def block_range(start, stop, length):
        base = lax.div(start, 128) * 128
        count = lax.div(stop - base + (KB - 1), KB)
        return jnp.minimum(base, length - count * KB), count

    def halves(values, axis, h):
        place = lax.broadcasted_iota(jnp.int32, values.shape, axis)
        return jnp.where(place >= hd if h % 2 else place < hd, values, jnp.zeros_like(values))

    def put_masked(rows, rows_t, natural, transposed):
        for h in range(H):
            pair = slice((h // 2) * 2 * hd, (h // 2) * 2 * hd + 2 * hd)
            natural[h] = halves(rows[:, pair], 1, h)
            transposed[h] = halves(rows_t[pair, :], 0, h)

    def key_rows(base, j, rows=KB):
        return pl.ds(pl.multiple_of(base + j * rows, 128), rows)

    def twice(count, base, body, carry):
        pairs = lax.div(count, 2)
        carry = lax.fori_loop(0, pairs, lambda j, c: body(base, j, c, 2 * KB, H // 2), carry)
        rest = base + pairs * 2 * KB
        return lax.fori_loop(0, count - 2 * pairs, lambda j, c: body(rest, j, c, KB, H), carry)

    def attend(query_t, qtm, k, vt, p, ot, norms, lo, hi, start, stop):
        base, count = block_range(start, stop, k.shape[0])
        squares = query_t.astype(F32)
        squares = squares * squares
        bound = None
        for h in range(H):
            own = jnp.sum(fold(squares[h * hd:(h + 1) * hd], jnp.sum), axis=0, keepdims=True)
            own = own * jnp.max(norms[h:h + 1, :], axis=1, keepdims=True)
            bound = own if bound is None else jnp.maximum(bound, own)
        small = jnp.max(bound) <= 3600.0
        shifts = jnp.where(small, 0, count)

        def bias_of(j, rows=KB, start=base):
            kpos = start + j * rows + lax.broadcasted_iota(jnp.int32, (rows, RB), 0)
            return jnp.where((kpos >= lo) & (kpos < hi), 0.0, -1e30).astype(F32)

        def scores(h, at, bias):
            pair = slice((h // 2) * 2 * hd, (h // 2) * 2 * hd + 2 * hd)
            return mm(k[at, pair], qtm[h]) + bias

        def top(j, highest):
            at = key_rows(base, j)
            bias = bias_of(j)
            return tuple(jnp.maximum(highest[h], fold(scores(h, at, bias), jnp.max)) for h in range(H))

        lowest = jnp.full((8, RB), jnp.where(small, 0.0, -1e30), F32)
        highest = lax.fori_loop(0, shifts, top, (lowest,) * H)
        highest = [jnp.max(part, axis=0, keepdims=True) for part in highest]
        ot[...] = jnp.zeros_like(ot)

        def gather(start, j, totals, rows, group):
            at = key_rows(start, j, rows)
            bias = bias_of(j, rows, start)
            out = []
            for first_head in range(0, H, group):
                heads = range(first_head, first_head + group)
                found = [scores(h, at, bias) for h in heads]
                lows = []
                for h in heads:
                    weights = jnp.exp(found[h - first_head] - highest[h])
                    low = weights.astype(BF16)
                    lows.append(low)
                    p[h, at, :] = low
                    out.append(totals[h] + fold(weights, jnp.sum))
                for h in heads:
                    head = slice(h * hd, (h + 1) * hd)
                    ot[head, :] += mm(vt[head, at], lows[h - first_head])
            return tuple(out)

        totals = twice(count, base, gather, (jnp.zeros((8, RB), F32),) * H)
        inverse = []
        for h in range(H):
            inv = 1.0 / jnp.sum(totals[h], axis=0, keepdims=True)
            head = slice(h * hd, (h + 1) * hd)
            ot[head, :] = ot[head, :] * inv
            inverse.append(inv)
        return inverse

    def attend_back(grad_rows, inverse, qm, k, kt, v, p, ot, dk, dv, start, stop):
        base, count = block_range(start, stop, k.shape[0])
        grad_t = grad_rows.T.astype(F32)
        scaled_t = []
        spread = []
        for h in range(H):
            head = slice(h * hd, (h + 1) * hd)
            low_t = (grad_t[head] * inverse[h]).astype(BF16)
            scaled_t.append(low_t)
            spread.append(jnp.sum(ot[head, :] * low_t.astype(F32), axis=0, keepdims=True))
        scaled_t = jnp.concatenate(scaled_t, axis=0)
        put_masked(scaled_t.T, scaled_t, gm, gtm)
        dqt[...] = jnp.zeros_like(dqt)

        def body(start, j, carry, rows, group):
            at = key_rows(start, j, rows)
            pairs = [slice((h // 2) * 2 * hd, (h // 2 + 1) * 2 * hd) for h in range(H)]
            for first_head in range(0, H, group):
                heads = range(first_head, first_head + group)
                prob_grads = [mm(v[at, pairs[h]], gtm[h]) for h in heads]
                for h in heads[::2]:
                    dv[at, pairs[h]] += mm(p[h, at, :], gm[h]) + mm(p[h + 1, at, :], gm[h + 1])
                lows = [(p[h, at, :].astype(F32) * (prob_grads[h - first_head] - spread[h])).astype(BF16) for h in heads]
                for h in heads[::2]:
                    n = h - first_head
                    dk[at, pairs[h]] += mm(lows[n], qm[h]) + mm(lows[n + 1], qm[h + 1])
                for h in heads:
                    head = slice(h * hd, (h + 1) * hd)
                    dqt[head, :] += mm(kt[head, at], lows[h - first_head])
            return carry

        twice(count, base, body, 0)
        return dqt[...].astype(BF16).T

    def add_vec(row, values):
        vecg_out[row:row + 1, :] += jnp.sum(values, axis=0, keepdims=True)

    x_rows = x_ref[...]
    q = ((mm(x_rows, wqkv[:, :d_model]) + vec[0:1]) * 0.125).astype(BF16)
    q_t = q.T
    put_masked(q, q_t, qm_s, gtm)
    inv_s = attend(q_t, gtm, k_s, vt_s, p_s, ot_s, kn_s, lo_s, hi_s, s_from, s_to)
    mixed = ot_s[...].astype(BF16).T
    mixed_out[...] = mixed
    first_norm, unit1, scale1 = normalize(
        x_rows.astype(F32) + (mm(mixed, wout[...]) + vec[2:3]), vec[11:12], vec[14:15])
    first_low = first_norm.astype(BF16)
    first_low_out[...] = first_low
    cq = ((mm(first_low, wcq[...]) + vec[3:4]) * 0.125).astype(BF16)
    cq_t = cq.T
    put_masked(cq, cq_t, qm_c, gtm)
    inv_c = attend(cq_t, gtm, k_c, vt_c, p_c, ot_c, kn_c, lo_c, hi_c, c_from, c_to)
    cmixed = ot_c[...].astype(BF16).T
    cmixed_out[...] = cmixed
    second, unit2, scale2 = normalize(
        first_norm + (mm(cmixed, wcout[...]) + vec[5:6]), vec[12:13], vec[15:16])
    second_low = second.astype(BF16)
    second_low_out[...] = second_low
    tile = 2 * d_model
    ffn = None
    for t in range(ff // tile):
        cols = slice(t * tile, (t + 1) * tile)
        hidden = mm(second_low, wup[:, cols]) + jnp.concatenate([vec[7 + 2*t:8 + 2*t], vec[8 + 2*t:9+2*t]], axis=1)
        smooth, slope = gelu_parts(hidden)
        active = smooth.astype(BF16)
        active_out[:, cols] = active
        slope_s[:, cols] = slope
        part = mm(active, wdown[cols, :])
        ffn = part if ffn is None else ffn + part
    third, unit3, scale3 = normalize(second + (ffn + vec[6:7]), vec[13:14], vec[16:17])
    layer_out[...] = third.astype(BF16)

    grad = ct_ref[...].astype(F32)
    add_vec(13, grad * unit3)
    add_vec(16, grad)
    grad_third = normalize_back(unit3, scale3, vec[13:14], grad)
    down_low = grad_third.astype(BF16)
    down_low_out[...] = down_low
    add_vec(6, down_low.astype(F32))
    back = grad_third
    for t in range(ff // tile):
        cols = slice(t * tile, (t + 1) * tile)
        up_low = (mm_nt(down_low, wdown[cols, :]) * slope_s[:, cols]).astype(BF16)
        up_low_out[:, cols] = up_low
        add_vec(7 + 2*t, up_low[:, :512].astype(F32))
        add_vec(8 + 2*t, up_low[:, 512:].astype(F32))
        back = back + mm_nt(up_low, wup[:, cols])
    add_vec(12, back * unit2)
    add_vec(15, back)
    grad_mid = normalize_back(unit2, scale2, vec[12:13], back)
    cross_low = grad_mid.astype(BF16)
    cross_low_out[...] = cross_low
    add_vec(5, cross_low.astype(F32))
    cross_grad = mm_nt(cross_low, wcout[...]).astype(BF16)
    cdq = attend_back(cross_grad, inv_c, qm_c, k_c, kt_c, v_c, p_c, ot_c, dk_c, dv_c, c_from, c_to) * 0.125
    cdq_out[...] = cdq

    def put_out(slabs, dk, dv):
        for n in range(2):
            cols = slice(n * 256, (n + 1) * 256)
            slabs[n] = dk[:, cols].astype(BF16)
            slabs[2 + n] = dv[:, cols].astype(BF16)

    @pl.when(step == steps - 1)
    def _():
        add_vec(4, dv_c[...])
        put_out(p_c, dk_c, dv_c)
        pltpu.make_async_copy(p_c.at[0:4], dckv_hbm, sems.at[1]).start()

    add_vec(3, cdq.astype(F32))
    grad_first = grad_mid + mm_nt(cdq, wcq[...])
    add_vec(11, grad_first * unit1)
    add_vec(14, grad_first)
    grad_in = normalize_back(unit1, scale1, vec[11:12], grad_first)
    self_low = grad_in.astype(BF16)
    self_low_out[...] = self_low
    add_vec(2, self_low.astype(F32))
    self_grad = mm_nt(self_low, wout[...]).astype(BF16)
    dq = attend_back(self_grad, inv_s, qm_s, k_s, kt_s, v_s, p_s, ot_s, dk_s, dv_s, s_from, s_to) * 0.125
    dq_out[...] = dq
    add_vec(0, dq.astype(F32))
    part_out[...] = grad_in + mm_nt(dq, wqkv[:, :d_model])

    @pl.when(step == steps - 1)
    def _():
        add_vec(1, dv_s[...])
        put_out(p_s, dk_s, dv_s)
        pltpu.make_async_copy(p_s.at[0:4], dkv_hbm, sems.at[0]).start()
        pltpu.make_async_copy(p_s.at[0:4], dkv_hbm, sems.at[0]).wait()
        pltpu.make_async_copy(p_c.at[0:4], dckv_hbm, sems.at[1]).wait()


def run_layer(counts, x_full, m_full, ct_full, vec_all, w_all, w_down):
    t_len, d_model = x_full.shape
    s_len = m_full.shape[0]
    ff = w_down.shape[0]
    steps = t_len // (2 * RB)
    own = t_len // 2
    any_spec = pl.BlockSpec(memory_space=pl.ANY)

    def rows(cols):
        return pl.BlockSpec((RB, cols), lambda i, b: (i, 0))

    def arr(cols, dtype=BF16):
        return jax.ShapeDtypeStruct((own, cols), dtype)

    out_shape = [arr(d_model) for _ in range(8)] + [arr(ff), arr(ff), arr(d_model), arr(d_model), arr(d_model, F32)]
    out_specs = [rows(s.shape[1]) for s in out_shape]
    out_shape += [
        jax.ShapeDtypeStruct((4, t_len, 256), BF16),
        jax.ShapeDtypeStruct((4, s_len, 256), BF16),
        jax.ShapeDtypeStruct((32, d_model), F32),
    ]
    out_specs += [any_spec, any_spec, pl.BlockSpec((32, d_model), lambda i, b: (0, 0))]
    bf = lambda *shape: pltpu.VMEM(shape, BF16)
    fl = lambda *shape: pltpu.VMEM(shape, F32)
    scratch = [bf(d_model, n * d_model) for n in (3, 1, 1, 2, 1)] + [bf(d_model, ff), bf(ff, d_model)] + [
        bf(t_len, d_model), bf(d_model, t_len), bf(t_len, d_model), bf(d_model, t_len),
        bf(s_len, d_model), bf(d_model, s_len), bf(s_len, d_model), bf(d_model, s_len),
        bf(H, t_len, RB), bf(H, s_len, RB),
        fl(t_len, d_model), fl(t_len, d_model), fl(s_len, d_model), fl(s_len, d_model),
        bf(H, RB, 128), bf(H, RB, 128), bf(H, 128, RB), bf(H, RB, 128),
        fl(d_model, RB), fl(d_model, RB), fl(d_model, RB), fl(RB, ff), fl(32, d_model), fl(H, RB), fl(H, RB),
        pltpu.SemaphoreType.DMA((11,)),
    ]
    return pl.pallas_call(
        layer_kernel,
        out_shape=out_shape,
        grid_spec=pltpu.PrefetchScalarGridSpec(
            num_scalar_prefetch=1,
            grid=(steps,),
            in_specs=[any_spec, any_spec] + [pl.BlockSpec((RB, d_model), lambda i, b: (2 * i + b[32, 0], 0))] * 2 + [
                      pl.BlockSpec(vec_all.shape, lambda i, b: (0, 0, 0)), any_spec, any_spec],
            out_specs=out_specs,
            scratch_shapes=scratch,
        ),
        compiler_params=pltpu.CompilerParams(vmem_limit_bytes=64 * 1024 * 1024 - 512 * 1024),
        name="layer",
    )(counts, x_full, m_full, x_full, ct_full, vec_all, w_all, w_down)


def ring_neighbours(at, size):
    odd = lax.rem(at, 2)
    after = jnp.where(odd == 0, jnp.where(at + 2 < size, at + 2, at + 1), jnp.where(at >= 3, at - 2, at - 1))
    before = jnp.where(odd == 0, jnp.where(at >= 2, at - 2, at + 1), jnp.where(at + 2 < size, at + 2, at - 1))
    return after, before


def ring_place(at, size):
    return jnp.where(lax.rem(at, 2) == 0, lax.div(at, 2), size - 1 - lax.div(at, 2))


def ring_member(place, size):
    place = lax.rem(place + 2 * size, size)
    return jnp.where(place < lax.div(size, 2), 2 * place, 2 * (size - 1 - place) + 1)


ROWS_AT = {2: (3, 0), 4: (1,), 6: (2,)}
LAG = 4


def gather_kernel(
    size, splits,
    tokens, memory, cotangent, tgt_ids, src_ids, proj_bias, up_bias, norm_gain, norm_bias,
    w_qkv, w_out, w_cq, w_ckv, w_cout, w_up, w_down,
    x_full, m_full, c_full, counts_all, vec_all, w_all, d_all,
    counts, spread, packed, stage_w, stage_d, stage_x, stage_m, stage_c,
    send_own, recv_own, send_ring, recv_ring, send_core, recv_core, send_chip, recv_chip, stage_sems, local_sems,
    send_rows, recv_rows,
):
    at, place = lax.axis_index("dp"), lax.axis_index("seq")
    micro, core = lax.div(place, 2), lax.rem(place, 2)
    after, before = ring_neighbours(at, size)
    mine = ring_place(at, size)
    core_peer = {"seq": place + 1 - 2 * core}
    chip_peer = {"seq": place + 2 - 4 * micro}
    peers = ({"dp": after}, {"dp": before}, core_peer, chip_peer)

    barrier = pltpu.get_barrier_semaphore()
    for peer in peers:
        pl.semaphore_signal(barrier, inc=1, device_id=peer, device_id_type=pl.DeviceIdType.MESH)

    wide, tall = w_qkv.shape[0], w_down.shape[0]
    shards = tuple(zip((w_qkv, w_out, w_cq, w_ckv, w_cout, w_up), splits))
    staged = [(shard, stage_w.at[:, pl.ds(column, shard.shape[1])]) for shard, column in shards]
    staged += [(w_down, stage_d)]
    staged += [(rows.at[micro, 0], stage) for rows, stage in
               ((tokens, stage_x), (memory, stage_m), (cotangent, stage_c))]
    staging = [pltpu.make_async_copy(src, dst, stage_sems.at[n]) for n, (src, dst) in enumerate(staged)]
    for copy in staging:
        copy.start()

    width = proj_bias.shape[1]
    spread[...] = jnp.zeros_like(spread)
    spread[0:7, :width] = proj_bias[...].astype(F32)
    spread[7:10, :width] = norm_gain[...].astype(F32)
    spread[10:13, :width] = norm_bias[...].astype(F32)
    for n in range(4 * width // 128):
        spread[13 + n:14 + n, :] = up_bias[pl.ds(n * 128, 128)].astype(F32).reshape(1, 128)
    packed[...] = spread[...].astype(BF16)
    lane = lax.broadcasted_iota(jnp.int32, (8, 128), 1)
    for index in range(2):
        total = jnp.zeros((8, 128), F32)
        for ids, docs, offset in ((tgt_ids, range(1, 9), 0), (src_ids, range(1, 9), 8)):
            row = ids[index]
            for doc in docs:
                below = jnp.sum(jnp.where(row < doc, 1.0, 0.0), axis=1, keepdims=True)
                total = total + jnp.where(lane == doc + offset, below, 0.0)
        counts[index, 0] = total.astype(jnp.int32)
    counts[2, 0] = jnp.full((8, 128), core, jnp.int32)

    pairs = ((tokens, x_full), (memory, m_full), (cotangent, c_full), (counts, counts_all))

    def chunk(n, owner):
        source, full = pairs[n]
        rows = source.shape[-2]
        return full.at[pl.ds(pl.multiple_of(owner * rows, 8), rows)]

    def rows_of(n, index):
        return pairs[n][0].at[index, 0]

    sent, arriving = [], []

    def send(src, dst, send_sem, recv_sem, peer):
        copy = pltpu.make_async_remote_copy(src, dst, send_sem, recv_sem, device_id=peer,
                                            device_id_type=pl.DeviceIdType.MESH)
        copy.start()
        sent.append(copy)
        return copy

    cut = splits[3]
    columns = (pl.ds(0, cut), pl.ds(cut, w_all.shape[1] - cut))

    def part(stream, way, chip):
        if stream < 2:
            return (2 * core + way) * (wide // 4), wide // 4
        return (4 * core + 2 * chip + way) * (tall // 8), tall // 8

    def piece(stream, way, owner, chip):
        if stream == 3:
            return vec_all.at[owner]
        start, length = part(stream, way, chip)
        rows = pl.ds(pl.multiple_of(owner * (wide if stream < 2 else tall) + start, 16), length)
        return w_all.at[rows, columns[stream]] if stream < 2 else d_all.at[rows]

    ways = ({"dp": after}, {"dp": before})
    pl.semaphore_wait(barrier, 4)

    first = {}
    first[3, 0] = [send(packed, vec_all.at[at], send_own.at[0, 7], recv_own.at[0, 7], ways[0])]
    for stream, way in ((0, 0), (0, 1), (1, 0), (1, 1)):
        start, length = part(stream, way, micro)
        first[stream, way] = [
            send(shard.at[pl.ds(pl.multiple_of(start, 16), length)],
                 w_all.at[pl.ds(pl.multiple_of(at * wide + start, 16), length), pl.ds(column, shard.shape[1])],
                 send_own.at[way, n], recv_own.at[way, n], ways[way])
            for n, (shard, column) in enumerate(shards) if (column >= cut) == (stream == 1)
        ]
    for way in range(2):
        start, length = part(2, way, micro)
        first[2, way] = [send(w_down.at[pl.ds(pl.multiple_of(start, 16), length)],
                              d_all.at[pl.ds(pl.multiple_of(at * tall + start, 16), length)],
                              send_own.at[way, 6], recv_own.at[way, 6], ways[way])]
    across = [send(rows_of(n, 1 - micro), chunk(n, place), send_rows.at[n, 0], recv_rows.at[n, 0], chip_peer)
              for n in (3, 0, 1, 2)]
    across = across[1:] + across[:1]
    for n in range(4):
        arriving.append(send(rows_of(n, micro), chunk(n, place), send_rows.at[n, 1], recv_rows.at[n, 1], core_peer))
    for copy in staging:
        copy.wait()
    own = [(stage_w, w_all.at[pl.ds(pl.multiple_of(at * wide, 16), wide)]),
           (stage_d, d_all.at[pl.ds(pl.multiple_of(at * tall, 16), tall)]),
           (packed, vec_all.at[at]), (counts.at[2, 0], counts_all.at[pl.ds(32, 8)]),
           (stage_x, chunk(0, place)), (stage_m, chunk(1, place)), (stage_c, chunk(2, place)),
           (counts.at[micro, 0], chunk(3, place))]
    own = [pltpu.make_async_copy(src, dst, local_sems.at[n]) for n, (src, dst) in enumerate(own)]
    for copy in own:
        copy.start()

    current, chips = {}, {}

    def owner_at(way, step):
        return ring_member(mine - step if way == 0 else mine + step, size)

    def from_chip(step):
        for way in range(2):
            chips[way, step].wait_recv()
            block = piece(2, way, owner_at(way, step), 1 - micro)
            arriving.append(send(block, block, send_core.at[3, way, step - 1], recv_core.at[3, way, step - 1], core_peer))

    for step in range(1, size):
        for stream in (3, 0, 1, 2):
            for way in range(1 if stream == 3 else 2):
                for copy in first[stream, way] if step == 1 else [current[stream, way]]:
                    copy.wait_recv()
                block = piece(stream, way, owner_at(way, step), micro)
                if step < size - 1:
                    current[stream, way] = send(block, block, send_ring.at[stream, way, step],
                                                recv_ring.at[stream, way, step], ways[way])
                if stream < 3:
                    arriving.append(send(block, block, send_core.at[stream, way, step - 1],
                                         recv_core.at[stream, way, step - 1], core_peer))
                if stream == 2:
                    chips[way, step] = send(block, block, send_chip.at[way, step - 1], recv_chip.at[way, step - 1],
                                            chip_peer)
        for n in ROWS_AT.get(step, ()):
            across[n].wait_recv()
            other = chunk(n, place + 2 - 4 * micro)
            arriving.append(send(other, other, send_rows.at[n, 2], recv_rows.at[n, 2], core_peer))
        if step > LAG:
            from_chip(step - LAG)
    for step in range(size - LAG, size):
        from_chip(step)
    for copy in arriving:
        copy.wait_recv()
    for copy in sent:
        copy.wait_send()
    for copy in own:
        copy.wait()


def gather_fused(tokens, memory, cotangent, tgt_ids, src_ids, vectors, shards):
    size = lax.axis_size("dp")
    d_model = tokens.shape[3]
    widths = [shard.shape[1] for shard in shards[:6]]
    splits = [sum(widths[:n]) for n in range(6)]
    seq = lax.axis_size("seq")
    any_spec = pl.BlockSpec(memory_space=pl.ANY)
    out_shape = [jax.ShapeDtypeStruct((seq * a.shape[2], d_model), BF16) for a in (tokens, memory, cotangent)]
    out_shape += [
        jax.ShapeDtypeStruct((seq * 8 + 8, 128), jnp.int32),
        jax.ShapeDtypeStruct((size, 16, 128), BF16),
        jax.ShapeDtypeStruct((size * shards[0].shape[0], sum(widths)), BF16),
        jax.ShapeDtypeStruct((size * shards[6].shape[0], d_model), BF16),
    ]
    dma = pltpu.SemaphoreType.DMA
    return pl.pallas_call(
        functools.partial(gather_kernel, size, splits),
        out_shape=out_shape,
        in_specs=[any_spec] * 3 + [pl.BlockSpec(memory_space=pltpu.VMEM)] * 6 + [any_spec] * 7,
        out_specs=[any_spec] * 7,
        scratch_shapes=[
            pltpu.VMEM((3, 1, 8, 128), jnp.int32), pltpu.VMEM((16, 128), F32), pltpu.VMEM((16, 128), BF16),
            pltpu.VMEM((shards[0].shape[0], sum(widths)), BF16), pltpu.VMEM(shards[6].shape, BF16),
            *(pltpu.VMEM(a.shape[2:], BF16) for a in (tokens, memory, cotangent)),
            dma((2, 8)), dma((2, 8)), dma((4, 2, size)), dma((4, 2, size)), dma((4, 2, size)), dma((4, 2, size)),
            dma((2, size)), dma((2, size)), dma((10,)), dma((8,)), dma((4, 3)), dma((4, 3)),
        ],
        compiler_params=pltpu.CompilerParams(collective_id=0, has_side_effects=True),
        name="gather",
    )(tokens, memory, cotangent, tgt_ids, src_ids, *vectors, *shards)


MESH = pl.DeviceIdType.MESH


SCHEDULE = "D U r0 Q r1 P a0 O r2 a01 R r3 V a0123 H E a0123 V a0123 V a0123 V a0123 V a0123 a0123"


def stream_shapes(d_model, ff, size):
    return [(d_model, d_model // size, q) for q in (ff // 4, ff // 4, 5 * d_model // 4, 3 * d_model // 4)]


def settle_kernel(size, shapes, *refs):
    n_in, n_out, count = 18, 4 + len(shapes), len(shapes)
    (x_hbm, m_hbm, w_hbm, lo_hbm, mixed_hbm, self_low_hbm, first_low_hbm, cdq_hbm, cmixed_hbm, cross_low_hbm,
     second_low_hbm, up_low_hbm, active_hbm, down_low_hbm, dq_hbm, part_hbm, dkv_hbm, dckv_hbm) = refs[:n_in]
    vec_hbm = refs[n_in]
    outs = refs[n_in + 1:n_in + 1 + n_out]
    lo_home, dt_home, dm_home, vec_out = outs[:4]
    sums = outs[4:]
    scratch = refs[n_in + 1 + n_out:]
    (xf, mf, wkv, wpair, xo, mixed, self_low, first_low, cdq, cmixed, cross_low, second_low, up_low, active,
     down_low, dq, part, dkv, dckv) = scratch[:19]
    (tz, tz_low, tz_got, mz, mz_low, mz_got, lo_buf, vec_run, vec_got) = scratch[19:28]
    rest = scratch[28:]
    acc, stage, other, ring_out, ring_in, fin, fin_got, fin_sum = (rest[n * count:(n + 1) * count] for n in range(8))
    (load_sems, store_sems, ring_ss, ring_rs, core_ss, core_rs, fin_ss, fin_rs, row_ss, row_rs, vec_ss, vec_rs,
     lo_ss, lo_rs) = rest[8 * count:]

    at, place = lax.axis_index("dp"), lax.axis_index("seq")
    micro, core = lax.div(place, 2), lax.rem(place, 2)
    after, before = ring_neighbours(at, size)
    mine = ring_place(at, size)
    core_peer = {"seq": place + 1 - 2 * core}
    chip_peer = {"seq": place + 2 - 4 * micro}
    levels = size.bit_length() - 1
    flips = [{"dp": at + (1 << n) * (1 - 2 * lax.rem(lax.div(at, 1 << n), 2))} for n in range(levels)]
    vec_peers = [core_peer, chip_peer] + flips
    d_model = xf.shape[1]
    half = d_model // 2
    t_len, s_len = xf.shape[0], mf.shape[0]

    barrier = pltpu.get_barrier_semaphore()
    greeted = [{"dp": after}, {"dp": before}, core_peer, chip_peer] + flips
    for peer in greeted:
        pl.semaphore_signal(barrier, inc=1, device_id=peer, device_id_type=MESH)

    loads = {}

    def load(name, src, dst):
        copy = pltpu.make_async_copy(src, dst, load_sems.at[len(loads)])
        copy.start()
        loads[name] = copy

    def load_first():
        load("active", active_hbm, active)
        load("down_low", down_low_hbm, down_low)
        load("vec", vec_hbm.at[pl.ds(0, 24)], vec_run.at[0])

    def load_up():
        load("second_low", second_low_hbm, second_low)
        load("up_low", up_low_hbm, up_low)

    def load_qkv():
        load("dkv", dkv_hbm, dkv)
        load("xf", x_hbm, xf)
        for n in range(t_len // (2 * RB)):
            load(("xo", n), x_hbm.at[pl.ds((2 * n + core) * RB, RB)], xo.at[pl.ds(n * RB, RB)])
        load("dq", dq_hbm, dq)

    def load_rest():
        load("dckv", dckv_hbm, dckv)
        load("mf", m_hbm, mf)
        for name, src, dst in (("mixed", mixed_hbm, mixed), ("self_low", self_low_hbm, self_low),
                               ("first_low", first_low_hbm, first_low), ("cdq", cdq_hbm, cdq),
                               ("cmixed", cmixed_hbm, cmixed), ("cross_low", cross_low_hbm, cross_low)):
            load(name, src, dst)
        load("wkv", w_hbm.at[:, pl.ds(d_model, 2 * d_model)], wkv)
        load("part", part_hbm, part)
        load("wpair", w_hbm.at[:, pl.ds(5 * d_model, 2 * d_model)], wpair)

    load_first()
    load_up()

    pending = []

    def send(src, dst, send_sem, recv_sem, peer):
        copy = pltpu.make_async_remote_copy(src, dst, send_sem, recv_sem, device_id=peer, device_id_type=MESH)
        copy.start()
        pending.append(copy)
        return copy

    stores = []

    def store(src, dst):
        copy = pltpu.make_async_copy(src, dst, store_sems.at[len(stores)])
        copy.start()
        stores.append(copy)

    pl.semaphore_wait(barrier, len(greeted))

    piece = t_len // 12
    keep, give = [], []

    def pieces_of(index0, slot0, index1, slot1):
        index, slot = jnp.where(core == 0, index0, index1), jnp.where(core == 0, slot0, slot1)
        source = lo_hbm.at[pl.ds(pl.multiple_of(index * piece, 128), piece)]
        return source, lo_buf.at[lax.div(slot, 3), pl.ds(pl.multiple_of(lax.rem(slot, 3) * piece, 128), piece)]

    for n, row in enumerate(((0, 0, 1, 0), (1, 1, 4, 4), (4, 5, 5, 5))):
        copy = pltpu.make_async_copy(*pieces_of(*row), lo_ss.at[n])
        copy.start()
        keep.append(copy)
    for n, row in enumerate(((2, 1, 0, 2), (3, 2, 2, 3), (5, 3, 3, 4))):
        source, target = pieces_of(*row)
        give.append(send(source, target, lo_ss.at[3 + n], lo_rs.at[n], core_peer))

    vec_state = {"level": 0, "copy": None}

    def vec_send():
        level = vec_state["level"]
        vec_state["copy"] = send(vec_run.at[level], vec_got.at[level], vec_ss.at[level], vec_rs.at[level],
                                 vec_peers[level])

    def vec_step():
        level = vec_state["level"]
        vec_state["copy"].wait_recv()
        vec_run[level + 1] = vec_run[level] + vec_got[level]
        vec_state["level"] = level + 1
        if level + 1 < len(vec_peers):
            vec_send()
        else:
            store(vec_run.at[level + 1], vec_out)

    loads["vec"].wait()
    vec_send()

    row_waits = []

    def home_rows(n, rows_of, home):
        store(rows_of(micro), home.at[micro])
        row_waits.append(send(rows_of(1 - micro), home.at[micro], row_ss.at[n], row_rs.at[n], chip_peer))

    def split(values, pieces, s, rows, base=0):
        width = values.shape[1] // pieces
        quarter = width // 4
        for p in range(pieces):
            lower = values[:, p * width:p * width + 2 * quarter]
            upper = values[:, p * width + 2 * quarter:(p + 1) * width]
            own = jnp.where(core == 0, lower, upper)
            away = jnp.where(core == 0, upper, lower).astype(BF16)
            cols = slice(base + p * quarter, base + (p + 1) * quarter)
            for way in range(2):
                acc[s][way, rows, cols] = own[:, way * quarter:(way + 1) * quarter]
                stage[s][way, rows, cols] = away[:, way * quarter:(way + 1) * quarter]

    core_waits = {}
    tile = 256

    def await_loads(*names):
        for name in names:
            loads[name].wait()

    def each_tile(body):
        def one(m, carry):
            body(pl.ds(pl.multiple_of(m * tile, tile), tile))
            return carry

        lax.fori_loop(0, d_model // tile, one, 0)

    def share(s):
        core_waits[s] = send(stage[s], other[s], core_ss.at[s], core_rs.at[s], core_peer)

    def compute_down():
        await_loads("active", "down_low")
        load_qkv()
        block, tall = shapes[0][1], active.shape[1] // size
        quarter = d_model // 4

        def one(m, carry):
            values = mm_tn(active[:, pl.ds(pl.multiple_of(m * tall, tall), tall)], down_low[...])
            rows = pl.ds(pl.multiple_of(m * block, block), block)
            for n in range(tall // block):
                split(values[n * block:(n + 1) * block], 1, 0, rows, n * quarter)
            return carry

        lax.fori_loop(0, size, one, 0)
        share(0)

    def compute_up():
        await_loads("second_low", "up_low")
        load_rest()
        each_tile(lambda rows: split(mm_tn(second_low[:, rows], up_low[...]), 1, 1, rows))
        share(1)

    def compute_qkv():
        await_loads("dkv", "xf", "dq", *(("xo", n) for n in range(t_len // (2 * RB))))

        def one(rows):
            split(mm_tn(xo[:, rows], dq[...]), 1, 2, rows)
            whole = xf[:, rows]
            for n in range(2):
                parts = [mm_tn(whole, dkv[2 * n + m]) for m in range(2)]
                split(jnp.concatenate(parts, axis=1), 1, 2, rows, (1 + n) * d_model // 4)

        each_tile(one)

    def compute_pair():
        await_loads("dckv", "mf")

        def one(rows):
            whole = mf[:, rows]
            for n in range(2):
                parts = [mm_tn(whole, dckv[2 * n + m]) for m in range(2)]
                split(jnp.concatenate(parts, axis=1), 1, 2, rows, (3 + n) * d_model // 4)

        each_tile(one)
        share(2)

    def compute_outs():
        await_loads("mixed", "self_low", "first_low", "cdq", "cmixed", "cross_low")

        def one(rows):
            for n, (left, right) in enumerate(((mixed, self_low), (first_low, cdq), (cmixed, cross_low))):
                split(mm_tn(left[:, rows], right[...]), 1, 3, rows, n * d_model // 4)

        each_tile(one)
        share(3)

    ring_waits = {}

    def ring(s, step):
        block = shapes[s][1]
        if step == 0:
            core_waits[s].wait_recv()
        for way in range(2):
            owner = ring_member(mine - 1 - step if way == 0 else mine + 1 + step, size)
            rows = pl.ds(pl.multiple_of(owner * block, block), block)
            total = acc[s][way, rows, :] + other[s][way, rows, :].astype(F32)
            if step > 0:
                ring_waits[s, way].wait_recv()
                total = total + ring_in[s][way, step - 1].astype(F32)
            if step < size - 1:
                ring_out[s][way, step] = total.astype(BF16)
                ring_waits[s, way] = send(
                    ring_out[s].at[way, step], ring_in[s].at[way, step], ring_ss.at[s, way, step],
                    ring_rs.at[s, way, step], {"dp": after if way == 0 else before})
            else:
                fin[s][way] = total.astype(BF16)

    chip_waits, tail = {}, []

    def finish(s):
        chip_waits[s] = send(fin[s], fin_got[s], fin_ss.at[s, 0], fin_rs.at[s, 0], chip_peer)

    def forward(s):
        chip_waits[s].wait_recv()
        fin_sum[s][...] = (fin[s][...].astype(F32) + fin_got[s][...].astype(F32)).astype(BF16)
        store(fin_sum[s], sums[s].at[core])
        tail.append(send(fin_sum[s], sums[s].at[core], fin_ss.at[s, 1], fin_rs.at[s, 1], core_peer))

    def row_products():
        await_loads("wkv", "part", "wpair")

        def tokens(b, carry):
            rows = pl.ds(pl.multiple_of(b * RB, RB), RB)
            total = None
            for n in range(4):
                product = mm_nt(dkv[n, rows, :], wkv[:, n * 256:(n + 1) * 256])
                total = product if total is None else total + product
            own = part[pl.ds(pl.multiple_of(lax.div(b, 2) * RB, RB), RB), :]
            total = total + jnp.where(lax.rem(b, 2) == core, own, jnp.zeros_like(own))
            tz[rows, :] = total
            tz_low[rows, :] = total.astype(BF16)
            return carry

        lax.fori_loop(0, t_len // RB, tokens, 0)

        def memories(b, carry):
            rows = pl.ds(pl.multiple_of(b * RB, RB), RB)
            total = None
            for n in range(4):
                product = mm_nt(dckv[n, rows, :], wpair[:, n * 256:(n + 1) * 256])
                total = product if total is None else total + product
            mz[rows, :] = total
            mz_low[rows, :] = total.astype(BF16)
            return carry

        lax.fori_loop(0, s_len // RB, memories, 0)
        copies = []
        for n, (low, got, length) in enumerate(((tz_low, tz_got, t_len // 4), (mz_low, mz_got, s_len // 4))):
            for k in range(2):
                start = pl.multiple_of((1 - core + 2 * k) * length, 128)
                copies.append(send(low.at[pl.ds(start, length)], got.at[k], row_ss.at[3 + 2 * n + k],
                                   row_rs.at[3 + 2 * n + k], core_peer))
        return copies

    def row_finish(copies):
        for copy in copies:
            copy.wait_recv()
        for n, (full, got, done, length, home) in enumerate((
                (tz, tz_got, tz_low, t_len // 4, dt_home), (mz, mz_got, mz_low, s_len // 4, dm_home))):

            def rows_at(k, length=length):
                return pl.ds(pl.multiple_of((core + 2 * k) * length, 128), length)

            for k in range(2):
                done[rows_at(k), :] = (full[rows_at(k), :] + got[k].astype(F32)).astype(BF16)
            home_rows(1 + n, lambda k, done=done, rows_at=rows_at: done.at[rows_at(k)], home)

    reached = [0] * count
    sent_home = []

    def advance(s):
        if reached[s] < size - 1:
            reached[s] += 1
            ring(s, reached[s])
            if reached[s] == size - 1:
                finish(s)
                sent_home.append(s)

    def rows_start():
        state["rows"] = row_products()

    def rows_end():
        row_finish(state["rows"])

    def layer_rows():
        for copy in keep:
            copy.wait()
        for copy in give:
            copy.wait_recv()
        home_rows(0, lambda k: lo_buf.at[k], lo_home)

    def vectors():
        if vec_state["level"] < len(vec_peers):
            vec_step()

    state = {}
    actions = {"D": compute_down, "U": compute_up, "Q": compute_qkv, "P": compute_pair, "O": compute_outs,
               "R": rows_start, "E": rows_end, "H": layer_rows, "V": vectors}
    for action in SCHEDULE.split():
        if action in actions:
            actions[action]()
        elif action[0] == "r":
            ring(int(action[1]), 0)
        else:
            for s in action[1:]:
                advance(int(s))
    for s in range(count):
        forward(s)
    for copy in row_waits + tail:
        copy.wait_recv()
    for copy in pending:
        copy.wait_send()
    for copy in stores:
        copy.wait()


def settle_fused(x_full, m_full, w_all, results):
    size = lax.axis_size("dp")
    (layer_rows, mixed, self_low, first_low, cdq, cmixed, cross_low, second_low, up_low, active, down_low, dq,
     part, dkv, dckv, vec_sums) = results
    t_len, d_model = x_full.shape
    s_len, ff, own = m_full.shape[0], up_low.shape[1], dq.shape[0]
    shapes = stream_shapes(d_model, ff, size)
    any_spec = pl.BlockSpec(memory_space=pl.ANY)
    out_shape = [
        jax.ShapeDtypeStruct((2, t_len // 4, d_model), BF16),
        jax.ShapeDtypeStruct((2, t_len // 4, d_model), BF16),
        jax.ShapeDtypeStruct((2, s_len // 4, d_model), BF16),
        jax.ShapeDtypeStruct((24, d_model), F32),
    ]
    out_shape += [jax.ShapeDtypeStruct((2, 2, block, q), BF16) for _, block, q in shapes]
    bf = lambda *shape: pltpu.VMEM(shape, BF16)
    fl = lambda *shape: pltpu.VMEM(shape, F32)
    dma = pltpu.SemaphoreType.DMA
    levels = 2 + size.bit_length() - 1
    count = len(shapes)
    scratch = [bf(t_len, d_model), bf(s_len, d_model), bf(d_model, 2 * d_model), bf(d_model, 2 * d_model)]
    scratch += [bf(own, d_model)] * 8 + [bf(own, ff)] * 2 + [bf(own, d_model)] * 2 + [
        fl(own, d_model), bf(4, t_len, 256), bf(4, s_len, 256),
        fl(t_len, d_model), bf(t_len, d_model), bf(2, t_len // 4, d_model),
        fl(s_len, d_model), bf(s_len, d_model), bf(2, s_len // 4, d_model),
        bf(2, t_len // 4, d_model), fl(levels + 1, 24, d_model), fl(levels, 24, d_model),
    ]
    scratch += [fl(2, rows, q) for rows, _, q in shapes]
    scratch += [bf(2, rows, q) for rows, _, q in shapes] * 2
    scratch += [bf(2, size - 1, block, q) for _, block, q in shapes] * 2
    scratch += [bf(2, block, q) for _, block, q in shapes] * 3
    scratch += [dma((24,)), dma((16,)), dma((count, 2, size)), dma((count, 2, size)), dma((count,)), dma((count,)),
                dma((count, 3)), dma((count, 3)), dma((7,)), dma((7,)), dma((levels,)), dma((levels,)), dma((6,)),
                dma((3,))]
    return pl.pallas_call(
        functools.partial(settle_kernel, size, shapes),
        out_shape=out_shape,
        in_specs=[any_spec] * 19,
        out_specs=[any_spec] * len(out_shape),
        scratch_shapes=scratch,
        compiler_params=pltpu.CompilerParams(
            collective_id=1, has_side_effects=True, vmem_limit_bytes=64 * 1024 * 1024 - 512 * 1024),
        name="settle",
    )(x_full, m_full, w_all, layer_rows, mixed, self_low, first_low, cdq, cmixed, cross_low, second_low, up_low,
      active, down_low, dq, part, dkv, dckv, vec_sums)


def finish_kernel(factor, lo, dt, dm, vec, *refs):
    grads = refs[:4]
    lo_out, dt_out, dm_out, qkv, out, cq, pair, cout, up, down, bias, up_bias, gain, shift = refs[4:]
    lo_out[:, 0] = lo[...]
    dt_out[:, 0] = dt[...]
    dm_out[:, 0] = dm[...]
    firsts = ((qkv, 0), (qkv, 1), (qkv, 2), (pair, 0), (pair, 1))
    others = ((out, 0), (cq, 0), (cout, 0))
    for half in range(2):
        for way in range(2):
            totals = [grad[half, way].astype(F32) * factor for grad in grads]
            block, width = totals[0].shape[0], totals[3].shape[1] // len(others)
            quarter = (2 * half + way) * width
            for n in range(totals[0].shape[1] // width):
                down[n * block:(n + 1) * block, quarter:quarter + width] = totals[0][:, n * width:(n + 1) * width]
            wide = totals[1].shape[1]
            up[:, (2 * half + way) * wide:(2 * half + way + 1) * wide] = totals[1]
            for total, places in ((totals[2], firsts), (totals[3], others)):
                for n, (ref, slot) in enumerate(places):
                    column = slot * 4 * width + quarter
                    ref[:, column:column + width] = total[:, n * width:(n + 1) * width]
    at = lax.axis_index("dp")
    d_model, width = vec.shape[1], bias.shape[1]
    sums = vec[...] * factor
    own = pltpu.roll(sums, lax.rem(d_model - at * width, d_model), 1)[:, :width]
    bias[...] = own[0:7]
    gain[...] = own[11:14]
    shift[...] = own[14:17]
    start = at * 4 * width
    rows = lax.broadcasted_iota(jnp.int32, (4, d_model), 0)
    row = jnp.sum(jnp.where(rows == lax.div(start, d_model), sums[7:11], 0.0), axis=0, keepdims=True)
    row = jnp.broadcast_to(row, (8, d_model))
    up_bias[...] = pltpu.roll(row, lax.rem(d_model - lax.rem(start, d_model), d_model), 1)[0:1, :4 * width]


def finish_fused(settled, factor, d_model, ff):
    lo, dt, dm = settled[:3]
    size = lax.axis_size("dp")
    block = d_model // size
    shapes = [jax.ShapeDtypeStruct((2, 1, *a.shape[1:]), BF16) for a in (lo, dt, dm)]
    shapes += [jax.ShapeDtypeStruct((block, n * d_model), F32) for n in (3, 1, 1, 2, 1)]
    shapes += [jax.ShapeDtypeStruct((block, ff), F32), jax.ShapeDtypeStruct((ff // size, d_model), F32)]
    shapes += [jax.ShapeDtypeStruct(s, F32) for s in ((7, block), (1, ff // size), (3, block), (3, block))]

    def whole(a):
        return pl.BlockSpec(a.shape, lambda i: (0,) * len(a.shape))

    done = pl.pallas_call(
        functools.partial(finish_kernel, factor),
        grid=(1,),
        out_shape=shapes,
        in_specs=[whole(a) for a in settled],
        out_specs=[whole(s) for s in shapes],
        compiler_params=pltpu.CompilerParams(vmem_limit_bytes=63 * 1024 * 1024),
        name="finish",
    )(*settled)
    return (*done[:11], done[11][0], *done[12:])


def pack_vectors(proj_bias, up_bias, norm_gain, norm_bias, d_model):
    size, at = lax.axis_size("dp"), lax.axis_index("dp")
    width = d_model // size
    rows = jnp.concatenate([proj_bias, jnp.zeros((4, width), BF16), norm_gain, norm_bias], axis=0)
    packed = lax.dynamic_update_slice(jnp.zeros((32, d_model), BF16), rows, (0, at * width))
    flat = lax.dynamic_update_slice(jnp.zeros((4 * d_model,), BF16), up_bias, (at * up_bias.shape[0],))
    return lax.dynamic_update_slice(packed, flat.reshape(4, d_model), (7, 0))


def unpack_vectors(sums, d_model):
    size, at = lax.axis_size("dp"), lax.axis_index("dp")
    width = d_model // size
    own = lax.dynamic_slice(sums, (0, at * width), (32, width))
    up = lax.dynamic_slice(sums[7:11].reshape(-1), (at * 4 * width,), (4 * width,))
    return own[:7], up, own[11:14], own[14:17]


def gather_plain(tokens, memory, cotangent, counts, packed, shards):
    micro = lax.axis_index("seq") // MB

    def whole(rows):
        return lax.all_gather(lax.squeeze(rows, (1,)), "seq", axis=1, tiled=True)[micro]

    weights = [lax.all_gather(shard, "dp", axis=0, tiled=True) for shard in shards]
    vec_all = lax.psum(packed, "dp")[None]
    counts = jnp.pad(lax.psum(counts, "seq")[micro][None], ((0, 31), (0, 0)))
    place = jnp.full((8, 128), lax.axis_index("seq") % MB, jnp.int32)
    counts = jnp.concatenate([counts, place], axis=0)
    w_all = jnp.concatenate(weights[:6], axis=1)
    return whole(tokens), whole(memory), whole(cotangent), counts, vec_all, w_all, weights[6]


def own_rows(rows, core):
    blocks = rows.reshape(rows.shape[0] // (2 * RB), 2, RB, rows.shape[1])
    return blocks[:, core].reshape(rows.shape[0] // 2, rows.shape[1])


def spread_rows(rows, core):
    blocks = rows.reshape(rows.shape[0] // RB, 1, RB, rows.shape[1])
    blocks = jnp.concatenate([blocks, jnp.zeros_like(blocks)], axis=1)
    blocks = jnp.where(core == 0, blocks, blocks[:, ::-1])
    return blocks.reshape(rows.shape[0] * 2, rows.shape[1])


def settle_plain(x_full, m_full, w_all, results, factor):
    (layer_rows, mixed, self_low, first_low, cdq, cmixed, cross_low, second_low, up_low, active, down_low, dq,
     part, dkv, dckv, vec_sums) = results
    place = lax.axis_index("seq")
    micro, core = place // MB, place % MB
    d_model = x_full.shape[1]
    dkv = jnp.moveaxis(dkv, 0, 1).reshape(x_full.shape[0], 2 * d_model)
    dckv = jnp.moveaxis(dckv, 0, 1).reshape(m_full.shape[0], 2 * d_model)
    input_rows = spread_rows(part, core) + mm_nt(dkv, w_all[:, d_model:3 * d_model])
    memory_rows = mm_nt(dckv, w_all[:, 5 * d_model:7 * d_model])

    def home(rows):
        both = jnp.stack([rows, jnp.zeros_like(rows)])
        both = jnp.where(micro == 0, both, both[::-1])
        return lax.psum_scatter(both, "seq", scatter_dimension=1, tiled=True).astype(BF16)[:, None]

    grads = [
        jnp.concatenate([mm_tn(own_rows(x_full, core), dq), mm_tn(x_full, dkv)], axis=1),
        mm_tn(mixed, self_low), mm_tn(first_low, cdq), mm_tn(m_full, dckv), mm_tn(cmixed, cross_low),
        mm_tn(second_low, up_low), mm_tn(active, down_low),
    ]
    grads = [
        lax.psum(lax.psum_scatter(grad, "dp", scatter_dimension=0, tiled=True), "seq") * factor for grad in grads
    ]
    vec_sums = lax.psum(vec_sums, ("dp", "seq")) * factor
    return (home(spread_rows(layer_rows.astype(F32), core)), home(input_rows), home(memory_rows), *grads,
            *unpack_vectors(vec_sums, d_model))


def per_device(
    tokens, memory, cotangent, tgt_segments, src_segments,
    self_qkv, self_out, cross_q, cross_kv, cross_out, ffn_up, ffn_down, proj_bias, up_bias, norm_gain, norm_bias,
):
    d_model = tokens.shape[3]
    shards = (self_qkv, self_out, cross_q, cross_kv, cross_out, ffn_up, ffn_down)
    size, rows, ff = lax.axis_size("dp"), self_qkv.shape[0], ffn_up.shape[1]
    fused = rows == 64 and size & (size - 1) == 0 and size > 2
    factor = 1.0 / math.sqrt(MB * size * tokens.shape[2] * lax.axis_size("seq"))
    if fused:
        vectors = (proj_bias, up_bias, norm_gain, norm_bias)
        x_full, m_full, ct_full, counts, vec_all, w_all, w_down = gather_fused(
            tokens, memory, cotangent, tgt_segments, src_segments, vectors, shards)
    else:
        docs = jnp.arange(1, 9)
        tgt_counts = jnp.sum(tgt_segments[:, 0, :, None] < docs, axis=1, dtype=jnp.int32)
        src_counts = jnp.sum(src_segments[:, 0, :, None] < docs, axis=1, dtype=jnp.int32)
        counts = jnp.pad(jnp.concatenate([tgt_counts, src_counts], axis=1), ((0, 0), (1, 111)))
        packed = pack_vectors(proj_bias, up_bias, norm_gain, norm_bias, d_model)
        x_full, m_full, ct_full, counts, vec_all, w_all, w_down = gather_plain(
            tokens, memory, cotangent, counts, packed, shards)
    results = run_layer(counts, x_full, m_full, ct_full, vec_all, w_all, w_down)
    if fused:
        return finish_fused(settle_fused(x_full, m_full, w_all, results), factor, d_model, ff)
    return settle_plain(x_full, m_full, w_all, results, factor)


def solution(mesh):
    rows = P(None, "dp", "seq", None)
    ids = P(None, "dp", "seq")
    sharded = P("dp", None)
    columns = P(None, "dp")
    return jax.shard_map(
        per_device,
        mesh=mesh,
        in_specs=(rows, rows, rows, ids, ids) + (sharded,) * 7 + (columns, P("dp"), columns, columns),
        out_specs=(rows, rows, rows) + (sharded,) * 7 + (columns, P("dp"), columns, columns),
        check_vma=False,
    )
```
